128 devices in a mesh: tm: 32 (over x, z, y_lo), mode: 4 (over y_hi, core).
Axes of the slice: x: 4, y: 4 (y_hi: 2, y_lo: 2; y = y_hi * 2 + y_lo), z: 4, core: 2. Of those that a mesh axis runs over, the one named last changes fastest.
Arguments:
- field_codes: bfloat16 [2, 64, 2, 1024, 1024], P(None, 'tm', None, 'mode'), may hold values from -6 to 6
- scales: float32 [2, 64, 1024], P(None, 'tm', 'mode'), may hold values from 0.01 to 0.1
- mom_index: int32 [4], replicated, may hold values from 0 to 1
- separations: int32 [3], replicated, may hold values from 1 to 6, as said below
- source_slice: int32 [2048], P('tm'), may hold values from 0 to 63
- noise_left: bfloat16 [2048, 2, 1024], P('tm'), may hold values from -0.1875 to 0.1875
- noise_right: bfloat16 [2048, 2, 1024], P('tm', None, 'mode'), may hold values from -6 to 6
Outputs:
- box_trace: float32 [64, 3, 2], P('tm')
- cross_trace: float32 [64, 3, 2], P('tm')
- noise_trace: float32 [64, 3, 2], P('tm')
The draws below stay inside these ranges and needn't reach their ends.
Inputs may be any that keep to these rules, and one draw needn't show every extreme that they name: The three separations lie one in 1 to 2, one in 3 to 4, and one equals 6, in an order drawn from the seed.
All inputs are finite; a program needn't handle non-finite values.
Results may differ from the reference program's by a relative error of at most 0.0072.
Values may be sent and summed in bfloat16 or wider, within the bound.
A program may use at most 256 MiB of HBM per device.

```python
import math
import jax
import jax.numpy as jnp
import numpy as np
from jax import lax

N = 1024
TS = 2
P_MOM = 2
NSEP = 3
T_SIZE = 64
HITS = 2048


def draw_separations(key, part):
    key = jax.random.fold_in(key, 11)
    first_key, second_key, third_key = jax.random.split(key, 3)
    nearest = jax.random.randint(first_key, (), 1, TS + 1, dtype=jnp.int32)
    middle = jax.random.randint(second_key, (), TS + 1, 2 * TS + 1, dtype=jnp.int32)
    farthest = jnp.full((), 3 * TS, jnp.int32)
    values = jnp.stack([nearest, middle, farthest])
    ordering = jax.random.permutation(third_key, 3)
    return values[ordering].astype(jnp.int32)


def with_ends(array, rng, low, high):
    longest = array.shape.index(max(array.shape))
    spots = []
    for shift in (0, 1):
        where = [jax.random.randint(jax.random.fold_in(rng, axis), (), 0, length) for axis, length in enumerate(array.shape)]
        where[longest] = (where[longest] + shift) % array.shape[longest]
        spots.append(tuple(where))
    return array.at[spots[0]].set(low).at[spots[1]].set(high)


def level_of(own_key, dims, cuts, low, largest):
    level, own = 1.0, jax.random.fold_in(own_key, 6)
    for axis_at, shards_of in cuts:
        steps = jnp.exp(jax.random.uniform(jax.random.fold_in(own, axis_at), (shards_of,), jnp.float32, low / len(cuts), largest / len(cuts)))
        level = level * jnp.repeat(steps, dims[axis_at] // shards_of).reshape([-1 if axis == axis_at else 1 for axis in range(len(dims))])
    return level


def rank_table(amount, skew):
    weights = [(1 << 20) // math.isqrt(standing ** skew) + 1 for standing in range(1, amount + 1)]
    width = 1 + sum(weights) // (1 << 30)
    return np.cumsum(np.array([max(1, weight // width) for weight in weights]))


def ranked_ids(key, shape, number_of, skew):
    listing = rank_table(number_of, skew)
    pick = jax.random.randint(jax.random.fold_in(key, 1), shape, 0, int(listing[number_of - 1]))
    rank = jnp.searchsorted(jnp.asarray(listing, jnp.int32), pick, side="right")
    return jax.random.permutation(jax.random.fold_in(key, 2), number_of)[rank].astype(jnp.int32)


def scatter_about(own_key, shape, scale, limit, pieces=(), kind=jnp.bfloat16):
    entries = scale * jax.random.normal(own_key, shape, jnp.float32)
    if pieces:
        entries = entries * level_of(own_key, shape, pieces, -0.22, 0.18)
    return jnp.clip(entries, -limit, limit).astype(kind)


def setup_inputs(seed: int = 0) -> dict:
    key_list = jax.random.split(jax.random.key(seed), 8)
    return {
        "field_codes": scatter_about(key_list[0], (P_MOM, T_SIZE, 2, N, N), 1.0, 6.0, ((1, 32), (3, 4))),
        "scales": jnp.clip(jnp.exp(math.log(0.1) - 2.3025851 * jax.random.uniform(key_list[1], (P_MOM, T_SIZE, N), jnp.float32) ** level_of(key_list[1], (P_MOM, T_SIZE, N), ((1, 32), (2, 4)), -0.2, 0.2)), 0.01, 0.1),
        "mom_index": with_ends(jax.random.randint(key_list[2], (4,), 0, P_MOM), jax.random.fold_in(key_list[2], 1), 0, P_MOM - 1).astype(jnp.int32),
        "separations": draw_separations(jax.random.fold_in(key_list[7], 71), 0),
        "source_slice": with_ends(ranked_ids(key_list[4], (HITS,), T_SIZE, 2), jax.random.fold_in(key_list[4], 3), 0, T_SIZE - 1).astype(jnp.int32),
        "noise_left": scatter_about(key_list[5], (HITS, 2, N), N ** -0.5, 0.1875, ((0, 32),)),
        "noise_right": scatter_about(key_list[6], (HITS, 2, N), 1.0, 6.0, ((0, 32), (2, 4))),
    }


def complex_product(left, right):
    real_real = jnp.dot(left[0], right[0], preferred_element_type=jnp.float32)
    imag_imag = jnp.dot(left[1], right[1], preferred_element_type=jnp.float32)
    real_imag = jnp.dot(left[0], right[1], preferred_element_type=jnp.float32)
    imag_real = jnp.dot(left[1], right[0], preferred_element_type=jnp.float32)
    return jnp.stack([real_real - imag_imag, real_imag + imag_real])


def trace_pair(left, right):
    left_wide = left.astype(jnp.float32)
    right_flip = jnp.swapaxes(right.astype(jnp.float32), 1, 2)
    real_part = jnp.sum(left_wide[0] * right_flip[0]) - jnp.sum(left_wide[1] * right_flip[1])
    imag_part = jnp.sum(left_wide[0] * right_flip[1]) + jnp.sum(left_wide[1] * right_flip[0])
    return jnp.stack([real_part, imag_part])


def entry_pair(left, right):
    left_wide = left.astype(jnp.float32)
    right_wide = right.astype(jnp.float32)
    real_part = jnp.sum(left_wide[0] * right_wide[0]) - jnp.sum(left_wide[1] * right_wide[1])
    imag_part = jnp.sum(left_wide[0] * right_wide[1]) + jnp.sum(left_wide[1] * right_wide[0])
    return jnp.stack([real_part, imag_part])


def times_complex(first, second):
    return jnp.stack([first[..., 0] * second[..., 0] - first[..., 1] * second[..., 1],
                      first[..., 0] * second[..., 1] + first[..., 1] * second[..., 0]], axis=-1)


def reference(field_codes, scales, mom_index, separations, source_slice, noise_left, noise_right):
    def per_slice(moment_slice):
        codes_here = lax.dynamic_index_in_dim(field_codes, moment_slice, 1, keepdims=False)
        scales_here = lax.dynamic_index_in_dim(scales, moment_slice, 1, keepdims=False)
        fields = (codes_here.astype(jnp.float32) * scales_here[:, None, :, None]).astype(jnp.bfloat16)
        picked = [fields[mom_index[insertion]] for insertion in range(4)]
        left_product = complex_product(picked[3], picked[0]).astype(jnp.bfloat16)
        right_product = complex_product(picked[1], picked[2]).astype(jnp.bfloat16)
        return picked[0], picked[1], picked[2], picked[3], left_product, right_product

    slice_ids = jnp.arange(T_SIZE, dtype=jnp.int32)
    first_field, second_field, third_field, fourth_field, left_product, right_product = lax.map(per_slice, slice_ids)

    def add_hit(item, weights_sum):
        start_slice = source_slice[item].astype(jnp.int32)
        left_vec = noise_left[item].astype(jnp.float32)
        right_vec = noise_right[item].astype(jnp.float32)
        outer_real = left_vec[0][:, None] * right_vec[0][None, :] - left_vec[1][:, None] * right_vec[1][None, :]
        outer_imag = left_vec[0][:, None] * right_vec[1][None, :] + left_vec[1][:, None] * right_vec[0][None, :]
        current = lax.dynamic_index_in_dim(weights_sum, start_slice, 0, keepdims=False)
        updated = current + jnp.stack([outer_real, outer_imag])
        return lax.dynamic_update_index_in_dim(weights_sum, updated, start_slice, 0)

    weights_sum = lax.fori_loop(0, HITS, add_hit, jnp.zeros((T_SIZE, 2, N, N), jnp.float32))
    noise_weights = weights_sum.astype(jnp.bfloat16)

    def per_source(source):
        firsts, seconds, crosses, noises = [], [], [], []
        for which in range(NSEP):
            later = (source + separations[which]) % T_SIZE
            firsts.append(trace_pair(first_field[source], second_field[later]))
            seconds.append(trace_pair(third_field[later], fourth_field[source]))
            crosses.append(trace_pair(left_product[source], right_product[later]))
            noises.append(entry_pair(noise_weights[source], right_product[later]))
        return jnp.stack(firsts), jnp.stack(seconds), jnp.stack(crosses), jnp.stack(noises)

    first_trace, second_trace, cross_trace, noise_trace = lax.map(per_source, slice_ids)
    box_trace = times_complex(first_trace, second_trace)
    return box_trace, cross_trace, noise_trace
```

```python
import jax
import jax.numpy as jnp
from jax import lax
from jax.experimental import pallas as pl
from jax.experimental.pallas import tpu as pltpu
from jax.sharding import PartitionSpec as P

MESH = pl.DeviceIdType.MESH
ANY = pl.ANY
PLANE = 8
PLANES = 4
BLK = 128
HALO = 6
SPAN = 16
VMEM_LIMIT = 50 * 1024 * 1024


def home(row, e):
    if e == 0:
        return 0, row % 4, row // 4
    if e == 4:
        return 1, row % 4, row // 4
    if e < 4:
        return 2 * e + row // 4, row % 4, 0
    col = (row + e) % 8
    return 2 * (8 - e) + col // 4, col % 4, 1


def place():
    tm = lax.axis_index("tm")
    mode = lax.axis_index("mode")
    return tm, mode


def greet(tm, mode):
    base = (tm // PLANE) * PLANE
    barrier = pltpu.get_barrier_semaphore()
    for index in range(PLANE):
        for other in range(4):

            @pl.when(jnp.logical_or(base + index != tm, mode != other))
            def _():
                pl.semaphore_signal(
                    barrier, inc=1, device_id=(base + index, other), device_id_type=MESH
                )

    for step in (PLANE, 3 * PLANE):
        pl.semaphore_signal(
            barrier, inc=1, device_id=((tm + step) % 32, mode), device_id_type=MESH
        )
    pl.semaphore_wait(barrier, 33)


def remote(src, dst, send, recv, device):
    return pltpu.make_async_remote_copy(
        src_ref=src, dst_ref=dst, send_sem=send, recv_sem=recv,
        device_id=device, device_id_type=MESH,
    )


def send_or_keep(src, dst, send, recv, device, tm, mode):
    here = jnp.logical_and(device[0] == tm, device[1] == mode)

    @pl.when(jnp.logical_not(here))
    def _():
        remote(src, dst, send, recv, device).start()

    @pl.when(here)
    def _():
        pltpu.make_async_copy(src, dst, recv).start()


def sent(src, dst, send, recv, device, tm, mode):
    here = jnp.logical_and(device[0] == tm, device[1] == mode)

    @pl.when(jnp.logical_not(here))
    def _():
        remote(src, dst, send, recv, device).wait_send()


def landed(ref, sem):
    pltpu.make_async_copy(ref, ref, sem).wait()


def spread_fields(
    fields, noise, whole, homes, hits,
    asm_send, asm_recv, fwd_send, fwd_recv, fld_send, fld_recv, halo_send, halo_recv,
    hit_send, hit_recv, ring_send, ring_recv, relay_send, relay_recv,
):
    tm, mode = place()
    plane, local = tm // PLANE, tm % PLANE
    base = plane * PLANE
    core = mode % 2
    flip = tm + 1 - 2 * (tm % 2)
    sibling = mode + 1 - 2 * core
    greet(tm, mode)

    def rows_of(block):
        return whole.at[:, :, pl.ds(pl.multiple_of(block * 256, 256), 256), :]

    assembly = [
        remote(fields.at[:, s], rows_of(mode), asm_send.at[s], asm_recv.at[mode // 2],
               (flip, 2 * s + core))
        for s in range(2)
    ]
    for copy in assembly:
        copy.start()

    hit_copies = []
    for a in range(2):
        for e in range(8):
            row = 2 * mode + a
            at, other, slot = home(row, e)
            hit_copies.append((
                noise.at[a], hits.at[slot, plane, local], hit_send.at[a, e],
                hit_recv.at[slot, local], (base + at, other),
            ))
    for copy in hit_copies:
        send_or_keep(*copy, tm, mode)

    field_copies = []
    for s in range(2):
        for a in range(2):
            for e in range(8):
                row = 2 * mode + a
                col = (row + e) % 8
                at, other, slot = home(row, e)
                field_copies.append((
                    fields.at[:, s, :, pl.ds(a * BLK, BLK),
                              pl.ds(pl.multiple_of(col * BLK, BLK), BLK)],
                    homes.at[slot, 2 * local + s], fld_send.at[s, a, e],
                    fld_recv.at[slot, 2 * local + s], (base + at, other),
                ))
    for copy in field_copies:
        send_or_keep(*copy, tm, mode)

    forwards = []
    for h in range(2):
        block = rows_of(2 * h + core)
        landed(block, asm_recv.at[h])
        forwards.append(
            remote(block, block, fwd_send.at[h], fwd_recv.at[h], (tm, sibling))
        )
        forwards[-1].start()

    right = ((tm + PLANE) % 32, mode)
    left = ((tm + 3 * PLANE) % 32, mode)
    for slot in range(2):
        for q in range(PLANE):
            landed(hits.at[slot, plane, q], hit_recv.at[slot, q])
    own = hits.at[:, plane]
    ring = [
        remote(own, own, ring_send.at[0], ring_recv.at[0], right),
        remote(own, own, ring_send.at[1], ring_recv.at[1], left),
    ]
    for copy in ring:
        copy.start()

    halos = []
    for slot in range(2):
        for t in range(HALO):
            landed(homes.at[slot, t], fld_recv.at[slot, t])
        halos.append(remote(
            homes.at[slot, pl.ds(0, HALO)], homes.at[slot, pl.ds(SPAN, HALO)],
            halo_send.at[slot], halo_recv.at[slot], left,
        ))
        halos[-1].start()

    before = (plane + 3) % PLANES
    after = (plane + 1) % PLANES
    opposite = (plane + 2) % PLANES
    landed(hits.at[:, before], ring_recv.at[0])
    relays = [remote(hits.at[0, before], hits.at[0, before], relay_send.at[0],
                     relay_recv.at[0], right)]
    relays[0].start()
    landed(hits.at[:, after], ring_recv.at[1])
    relays.append(remote(hits.at[1, after], hits.at[1, after], relay_send.at[1],
                         relay_recv.at[1], left))
    relays[1].start()

    for slot in range(2):
        for t in range(HALO, SPAN):
            landed(homes.at[slot, t], fld_recv.at[slot, t])
    for h in range(2):
        landed(rows_of(2 * h + 1 - core), fwd_recv.at[h])
    for slot in range(2):
        landed(homes.at[slot, pl.ds(SPAN, HALO)], halo_recv.at[slot])
        landed(hits.at[slot, opposite], relay_recv.at[slot])
    for copy in assembly + forwards + ring + halos + relays:
        copy.wait_send()
    for copy in hit_copies + field_copies:
        sent(*copy, tm, mode)


def multiply(mom, whole, out):
    core = lax.axis_index("mode") % 2
    start = pl.multiple_of(core * 512, 512)
    m1, m2, m3, m4 = (mom[i] for i in range(4))
    f32 = jnp.float32

    def cdot(ar, ai, br, bi):
        def dot(a, b):
            return jnp.dot(a, b, preferred_element_type=f32)

        return dot(ar, br) - dot(ai, bi), dot(ar, bi) + dot(ai, br)

    @pl.loop(0, 4)
    def _(step):
        pair, half = step // 2, step % 2
        cols = pl.ds(pl.multiple_of(start + pair * 256, 256), 256)
        rows = pl.ds(pl.multiple_of(half * 512, 512), 512)
        parts = cdot(whole[m4, 0, rows, :], whole[m4, 1, rows, :],
                     whole[m1, 0, :, cols], whole[m1, 1, :, cols])
        for c in range(2):
            for a in range(2):
                for b in range(4):
                    piece = parts[c][b * BLK:(b + 1) * BLK, a * BLK:(a + 1) * BLK]
                    out[2 * pair + a, 4 * half + b, c] = piece.T.astype(jnp.bfloat16)

    @pl.loop(0, 4)
    def _(pair):
        cols = pl.ds(pl.multiple_of(pair * 256, 256), 256)
        rows = pl.ds(start, 512)
        parts = cdot(whole[m2, 0, rows, :], whole[m2, 1, rows, :],
                     whole[m3, 0, :, cols], whole[m3, 1, :, cols])
        for c in range(2):
            for a in range(4):
                for b in range(2):
                    piece = parts[c][a * BLK:(a + 1) * BLK, b * BLK:(b + 1) * BLK]
                    out[a, 2 * pair + b, 2 + c] = piece.astype(jnp.bfloat16)


def spread_products(products, homes, send, recv, halo_send, halo_recv):
    tm, mode = place()
    base = (tm // PLANE) * PLANE
    core = mode % 2
    flip = tm + 1 - 2 * (tm % 2)
    when = 2 * (flip % PLANE) + mode // 2
    left = ((tm + 3 * PLANE) % 32, mode)
    greet(tm, mode)
    copies = []
    for e in range(8):
        for i in range(4):
            row = 4 * core + i
            col = (row + e) % 8
            at, other, slot = home(row, e)
            copies.append((
                products.at[i, col], homes.at[slot, when], send.at[i, e],
                recv.at[slot, when], (base + at, other),
            ))
    for copy in copies:
        send_or_keep(*copy, tm, mode)
    halos = []
    for slot in range(2):
        for t in range(HALO):
            landed(homes.at[slot, t], recv.at[slot, t])
        halos.append(remote(
            homes.at[slot, pl.ds(0, HALO), pl.ds(2, 2)],
            homes.at[slot, pl.ds(SPAN, HALO), pl.ds(2, 2)],
            halo_send.at[slot], halo_recv.at[slot], left,
        ))
        halos[-1].start()
    for slot in range(2):
        for t in range(HALO, SPAN):
            landed(homes.at[slot, t], recv.at[slot, t])
    for slot in range(2):
        landed(homes.at[slot, pl.ds(SPAN, HALO), pl.ds(2, 2)], halo_recv.at[slot])
    for copy in halos:
        copy.wait_send()
    for copy in copies:
        sent(*copy, tm, mode)


def traces(mom, seps, fields, products, hits, out, left_t, source, sums):
    f32 = jnp.float32
    tm = lax.axis_index("tm")
    plane, local = tm // PLANE, tm % PLANE
    diagonal = local == 0
    m1, m2, m3, m4 = (mom[i] for i in range(4))

    for role in range(2):
        for c in range(2):
            @pl.loop(0, 16)
            def _(part):
                block = hits[role, part // 4, pl.ds(2 * (part % 4), 2), c].reshape(BLK, BLK)
                left_t[role, pl.ds(c * BLK, BLK), pl.ds(pl.multiple_of(part * BLK, BLK), BLK)] = block.T

    @pl.loop(0, 16)
    def _(part):
        block = hits[0, part // 4, pl.ds(2 * (part % 4), 2), 4].reshape(BLK, BLK)
        source[:, pl.ds(pl.multiple_of(part * BLK, BLK), BLK)] = block.T[:16]

    def fold(value):
        return jnp.sum(value, axis=0, keepdims=True)

    @pl.loop(0, SPAN)
    def _(t):
        stamp = (plane * SPAN + t).astype(f32)
        chosen = (source[:1, :].astype(f32) == stamp).astype(f32).astype(jnp.bfloat16)
        totals = [[jnp.zeros((1, BLK), f32) for _ in range(8)] for _ in range(3)]
        for slot in range(2):
            mate = jnp.where(diagonal, slot, 1 - slot)
            right = jnp.concatenate(
                [hits[mate, :, :, 2 + c].reshape(2048, BLK) for c in range(2)], axis=1
            )
            pieces = jnp.dot(left_t[slot] * chosen, right, preferred_element_type=f32)
            w_re = pieces[:BLK, :BLK] - pieces[BLK:, BLK:]
            w_im = pieces[:BLK, BLK:] + pieces[BLK:, :BLK]
            p1 = [fields[slot, t, m1, c].astype(f32).T for c in range(2)]
            p4 = [fields[slot, t, m4, c].astype(f32).T for c in range(2)]
            rt = [products[slot, t, c].astype(f32) for c in range(2)]
            for k in range(3):
                u = t + seps[k]
                p2 = [fields[mate, u, m2, c].astype(f32) for c in range(2)]
                p3 = [fields[mate, u, m3, c].astype(f32) for c in range(2)]
                s = [products[slot, u, 2 + c].astype(f32) for c in range(2)]
                for at, (one, two) in enumerate(
                    ((p1, p2), (p4, p3), (rt, s), ((w_re, w_im), s))
                ):
                    totals[k][2 * at] += fold(one[0] * two[0] - one[1] * two[1])
                    totals[k][2 * at + 1] += fold(one[0] * two[1] + one[1] * two[0])
        for k in range(3):
            sums[3 * t + k] = jnp.concatenate(totals[k], axis=0)

    out[...] = jnp.sum(sums[...], axis=-1)


def params(ident=None):
    if ident is None:
        return pltpu.CompilerParams(vmem_limit_bytes=VMEM_LIMIT)
    return pltpu.CompilerParams(collective_id=ident, has_side_effects=True)


def on_device(field_codes, scales, mom_index, separations, source_slice, noise_left, noise_right):
    tm = lax.axis_index("tm")
    mode = lax.axis_index("mode")
    bf16, f32 = jnp.bfloat16, jnp.float32
    dma = pltpu.SemaphoreType.DMA
    fields = (field_codes.astype(f32) * scales[:, :, None, :, None]).astype(bf16)
    mine = lax.dynamic_slice_in_dim(noise_left, mode * 256, 256, axis=2)
    noise = jnp.concatenate(
        [mine, noise_right, jnp.broadcast_to(source_slice.astype(bf16)[:, None, None], (64, 1, 256))],
        axis=1,
    )
    noise = noise.reshape(64, 5, 2, BLK).transpose(2, 1, 0, 3)

    any_spec = pl.BlockSpec(memory_space=ANY)
    smem = pl.BlockSpec(memory_space=pltpu.SMEM)
    vmem = pl.BlockSpec(memory_space=pltpu.VMEM)
    whole, field_homes, hits = pl.pallas_call(
        spread_fields,
        out_shape=(
            jax.ShapeDtypeStruct((2, 2, 1024, 1024), bf16),
            jax.ShapeDtypeStruct((2, SPAN + HALO, 2, 2, BLK, BLK), bf16),
            jax.ShapeDtypeStruct((2, PLANES, PLANE, 5, 64, BLK), bf16),
        ),
        in_specs=[any_spec] * 2,
        out_specs=[any_spec] * 3,
        scratch_shapes=[
            dma((2,)), dma((2,)), dma((2,)), dma((2,)), dma((2, 2, 8)), dma((2, SPAN)),
            dma((2,)), dma((2,)), dma((2, 8)), dma((2, PLANE)), dma((2,)), dma((2,)),
            dma((2,)), dma((2,)),
        ],
        compiler_params=params(0),
        name="spread_fields",
    )(fields, noise)
    products = pl.pallas_call(
        multiply,
        out_shape=jax.ShapeDtypeStruct((4, 8, 4, BLK, BLK), bf16),
        in_specs=[smem, vmem],
        out_specs=vmem,
        compiler_params=params(),
        name="multiply",
    )(mom_index, whole)
    product_homes = pl.pallas_call(
        spread_products,
        out_shape=jax.ShapeDtypeStruct((2, SPAN + HALO, 4, BLK, BLK), bf16),
        in_specs=[any_spec],
        out_specs=any_spec,
        scratch_shapes=[dma((4, 8)), dma((2, SPAN)), dma((2,)), dma((2,))],
        compiler_params=params(1),
        name="spread_products",
    )(products)
    part = pl.pallas_call(
        traces,
        out_shape=jax.ShapeDtypeStruct((3 * SPAN, 8), f32),
        in_specs=[smem, smem, vmem, vmem, vmem],
        out_specs=vmem,
        scratch_shapes=[
            pltpu.VMEM((2, 2 * BLK, 2048), bf16),
            pltpu.VMEM((16, 2048), bf16),
            pltpu.VMEM((3 * SPAN, 8, BLK), f32),
        ],
        compiler_params=params(),
        name="traces",
    )(mom_index, separations, field_homes, product_homes, hits)

    table = jnp.zeros((64, 3, 8), f32)
    table = lax.dynamic_update_slice(
        table, part.reshape(SPAN, 3, 8), ((tm // PLANE) * SPAN, 0, 0)
    )
    total = lax.psum(table, ("tm", "mode"))
    mine = lax.dynamic_slice_in_dim(total, 2 * tm, 2, axis=0)
    box = jnp.stack(
        [
            mine[..., 0] * mine[..., 2] - mine[..., 1] * mine[..., 3],
            mine[..., 0] * mine[..., 3] + mine[..., 1] * mine[..., 2],
        ],
        axis=-1,
    )
    return box, mine[..., 4:6], mine[..., 6:8]


def solution(mesh):
    in_specs = (
        P(None, "tm", None, "mode", None),
        P(None, "tm", "mode"),
        P(),
        P(),
        P("tm"),
        P("tm", None, None),
        P("tm", None, "mode"),
    )
    out_specs = (P("tm", None, None), P("tm", None, None), P("tm", None, None))
    return jax.shard_map(
        on_device, mesh=mesh, in_specs=in_specs, out_specs=out_specs, check_vma=False
    )
```

```python
import jax
import jax.numpy as jnp
from jax import lax
from jax.experimental import pallas as pl
from jax.experimental.pallas import tpu as pltpu
from jax.sharding import PartitionSpec as P

MESH = pl.DeviceIdType.MESH
ANY = pl.ANY
BLK = 128
SPAN = 16
VMEM_LIMIT = 50 * 1024 * 1024


def home(i, half, e, same):
    if same:
        if e == 0:
            unit, slot = i % 2, i // 2
        elif e == 1:
            unit, slot = 4 + i, 0
        elif e == 2:
            unit, slot = 2 + i % 2, i // 2
        else:
            unit, slot = 4 + (i + 3) % 4, 1
        return unit // 2, 0, 2 * half + unit % 2, slot, 4 * half + (i + e) % 4
    return i + half * (e - i), 1, e + half * (i - e), half, 4 * (1 - half) + e


class Place:
    def __init__(self):
        self.tm = lax.axis_index("tm")
        self.mode = lax.axis_index("mode")
        self.x, self.z, self.lo = self.tm // 8, (self.tm // 2) % 4, self.tm % 2
        self.hi, self.core = self.mode // 2, self.mode % 2
        self.right = ((self.tm + 8) % 32, self.mode)
        self.left = ((self.tm + 24) % 32, self.mode)

    def at(self, z, lo, hi, core):
        return (8 * self.x + 2 * z + lo, 2 * hi + core)

    def is_here(self, device):
        return jnp.logical_and(device[0] == self.tm, device[1] == self.mode)


def greet(place, along_x):
    barrier = pltpu.get_barrier_semaphore()

    def signal(device):
        pl.semaphore_signal(barrier, inc=1, device_id=device, device_id_type=MESH)

    for core in range(2):
        for z in range(4):

            @pl.when(jnp.logical_or(place.z != z, place.core != core))
            def _():
                signal(place.at(z, place.lo, place.hi, core))

        for y in range(4):

            @pl.when(jnp.logical_or(place.lo != y // 2, place.hi != y % 2))
            def _():
                signal(place.at(place.z, y // 2, y % 2, core))

    if along_x:
        signal(place.right)
        signal(place.left)
    pl.semaphore_wait(barrier, 15 if along_x else 13)


def remote(src, dst, send, recv, device):
    return pltpu.make_async_remote_copy(
        src_ref=src, dst_ref=dst, send_sem=send, recv_sem=recv,
        device_id=device, device_id_type=MESH,
    )


def send_or_keep(place, src, dst, send, recv, device):
    here = place.is_here(device)

    @pl.when(jnp.logical_not(here))
    def _():
        remote(src, dst, send, recv, device).start()

    @pl.when(here)
    def _():
        pltpu.make_async_copy(src, dst, recv).start()


def sent(place, src, dst, send, recv, device):
    @pl.when(jnp.logical_not(place.is_here(device)))
    def _():
        remote(src, dst, send, recv, device).wait_send()


def landed(ref, sem):
    pltpu.make_async_copy(ref, ref, sem).wait()


def spread_fields(
    fields, noise, whole, homes, hits, mid, mid_hits,
    asm_send, asm_recv, fwd_send, fwd_recv, z_send, z_recv, y_send, y_recv,
    hit_z_send, hit_z_recv, hit_y_send, hit_y_recv,
):
    me = Place()
    flip = me.tm + 1 - 2 * me.lo
    greet(me, False)

    def rows_of(block):
        return whole.at[:, :, pl.ds(pl.multiple_of(block * 256, 256), 256), :]

    assembly = [
        remote(fields.at[s], rows_of(me.mode), asm_send.at[s], asm_recv.at[me.hi],
               (flip, 2 * s + me.core))
        for s in range(2)
    ]
    for copy in assembly:
        copy.start()

    along_z = []
    for a in range(2):
        for same in (False, True):
            for e in range(4):
                z, lo, mode, slot, col = home(2 * me.core + a, me.hi, e, same)
                group = slot if same else 2 + mode // 2
                device = me.at(z, me.lo, me.hi, mode % 2)
                index = (a, int(same), e)
                along_z.append((noise.at[a], mid_hits.at[group, me.z],
                                hit_z_send.at[index], hit_z_recv.at[group, me.z], device))
                along_z.append((
                    fields.at[:, :, :, pl.ds(a * BLK, BLK),
                              pl.ds(pl.multiple_of(col * BLK, BLK), BLK)],
                    mid.at[group, me.z], z_send.at[index], z_recv.at[group, me.z], device,
                ))
    for copy in along_z[0::2] + along_z[1::2]:
        send_or_keep(me, *copy)

    forwards = []
    for h in range(2):
        block = rows_of(2 * h + me.core)
        landed(block, asm_recv.at[h])
        forwards.append(remote(block, block, fwd_send.at[h], fwd_recv.at[h],
                               (me.tm, me.mode + 1 - 2 * me.core)))
        forwards[-1].start()

    along_y = []
    for source in range(4):
        for group in range(4):
            if group < 2:
                slot, device = group, me.at(me.z, 0, me.hi, me.core)
            else:
                slot, device = me.hi, me.at(me.z, 1, group - 2, me.core)
            landed(mid_hits.at[group, source], hit_z_recv.at[group, source])
            along_y.append((
                mid_hits.at[group, source], hits.at[slot, source, me.lo],
                hit_y_send.at[group, source], hit_y_recv.at[slot, source, me.lo], device,
            ))
            send_or_keep(me, *along_y[-1])
            landed(mid.at[group, source], z_recv.at[group, source])
            along_y.append((
                mid.at[group, source], homes.at[slot, source, pl.ds(2 * me.lo, 2)],
                y_send.at[group, source], y_recv.at[slot, source, me.lo], device,
            ))
            send_or_keep(me, *along_y[-1])

    for slot in range(2):
        for z in range(4):
            for lo in range(2):
                landed(hits.at[slot, z, lo], hit_y_recv.at[slot, z, lo])
                landed(homes.at[slot, z, pl.ds(2 * lo, 2)], y_recv.at[slot, z, lo])
    for h in range(2):
        landed(rows_of(2 * h + 1 - me.core), fwd_recv.at[h])
    for copy in assembly + forwards:
        copy.wait_send()
    for copy in along_z + along_y:
        sent(me, *copy)


def multiply(mom, whole, out):
    core = lax.axis_index("mode") % 2
    start = pl.multiple_of(core * 512, 512)
    m1, m2, m3, m4 = (mom[i] for i in range(4))
    f32 = jnp.float32

    def cdot(ar, ai, br, bi):
        def dot(a, b):
            return jnp.dot(a, b, preferred_element_type=f32)

        return dot(ar, br) - dot(ai, bi), dot(ar, bi) + dot(ai, br)

    @pl.loop(0, 4)
    def _(step):
        pair, half = step // 2, step % 2
        cols = pl.ds(pl.multiple_of(start + pair * 256, 256), 256)
        rows = pl.ds(pl.multiple_of(half * 512, 512), 512)
        parts = cdot(whole[m4, 0, rows, :], whole[m4, 1, rows, :],
                     whole[m1, 0, :, cols], whole[m1, 1, :, cols])
        for c in range(2):
            for a in range(2):
                for b in range(4):
                    piece = parts[c][b * BLK:(b + 1) * BLK, a * BLK:(a + 1) * BLK]
                    out[2 * pair + a, 4 * half + b, 2 + c] = piece.T.astype(jnp.bfloat16)

    @pl.loop(0, 4)
    def _(pair):
        cols = pl.ds(pl.multiple_of(pair * 256, 256), 256)
        rows = pl.ds(start, 512)
        parts = cdot(whole[m2, 0, rows, :], whole[m2, 1, rows, :],
                     whole[m3, 0, :, cols], whole[m3, 1, :, cols])
        for c in range(2):
            for a in range(4):
                for b in range(2):
                    piece = parts[c][a * BLK:(a + 1) * BLK, b * BLK:(b + 1) * BLK]
                    out[a, 2 * pair + b, c] = piece.astype(jnp.bfloat16)


def spread_products(
    products, fields, noise, homes, field_homes, hits, mid,
    send1, recv1, send2, recv2, halo_send, halo_recv, field_send, field_recv,
    ring_send, ring_recv, relay_send, relay_recv, keep,
):
    me = Place()
    greet(me, True)
    when = 2 * (1 - me.lo) + me.hi

    ring = []
    for slot in range(2):
        ring.append(remote(noise.at[slot], hits.at[slot, me.x], ring_send.at[0, slot],
                           ring_recv.at[0, slot], me.right))
        ring.append(remote(noise.at[1 - slot], hits.at[1 - slot, me.x], ring_send.at[1, 1 - slot],
                           ring_recv.at[1, 1 - slot], me.left))
    for copy in ring:
        copy.start()
    kept = []
    for slot in range(2):
        kept.append(pltpu.make_async_copy(noise.at[slot], hits.at[slot, me.x], keep.at[0, slot]))
        kept.append(pltpu.make_async_copy(fields.at[slot], field_homes.at[slot, pl.ds(0, 4)],
                                          keep.at[1, slot]))
    for copy in kept:
        copy.start()

    first = []
    for p in range(2):
        for i in range(4):
            for same in (False, True):
                for e in range(4):
                    z, lo, mode, slot, col = home(i, me.core, e, same)
                    hi, core = mode // 2, mode % 2

                    def either(one, two):
                        return one + slot * (two - one)

                    device = me.at(either(me.z, z), either(lo, me.lo), either(hi, me.hi), core)
                    at = (p, slot, either(z, 2 * lo + hi), either(when, me.z))
                    first.append((
                        products.at[i, col, pl.ds(2 * p, 2)], mid.at[at],
                        send1.at[p, i, int(same), e], recv1.at[at], device,
                    ))
    for copy in first:
        send_or_keep(me, *copy)

    halos = []
    for slot in range(2):
        halos.append(remote(fields.at[slot, 0], field_homes.at[slot, 4],
                            field_send.at[slot, 0], field_recv.at[slot, 0], me.left))
        halos.append(remote(fields.at[slot, 1, pl.ds(0, 2)], field_homes.at[slot, 5, pl.ds(0, 2)],
                            field_send.at[slot, 1], field_recv.at[slot, 1], me.left))
    for copy in halos:
        copy.start()

    before, after, opposite = (me.x + 3) % 4, (me.x + 1) % 4, (me.x + 2) % 4
    second = []
    relays = []

    def pass_on(p):
        for j in range(4):
            for k in range(4):
                landed(mid.at[p, 0, k, j], recv1.at[p, 0, k, j])
                second.append((
                    mid.at[p, 0, k, j], homes.at[0, me.z, j, pl.ds(2 * p, 2)],
                    send2.at[p, 0, k, j], recv2.at[p, 0, me.z, j],
                    me.at(k, me.lo, me.hi, me.core),
                ))
                send_or_keep(me, *second[-1])
                landed(mid.at[p, 1, k, j], recv1.at[p, 1, k, j])
                second.append((
                    mid.at[p, 1, k, j], homes.at[1, j, when, pl.ds(2 * p, 2)],
                    send2.at[p, 1, k, j], recv2.at[p, 1, j, when],
                    me.at(me.z, k // 2, k % 2, me.core),
                ))
                send_or_keep(me, *second[-1])

    def arrived(p, slot, z, t):
        landed(homes.at[slot, z, t, pl.ds(2 * p, 2)], recv2.at[p, slot, z, t])

    pass_on(0)
    landed(hits.at[0, before], ring_recv.at[0, 0])
    relays.append(remote(hits.at[0, before], hits.at[0, before], relay_send.at[0],
                         relay_recv.at[0], me.right))
    relays[-1].start()
    landed(hits.at[1, after], ring_recv.at[1, 1])
    relays.append(remote(hits.at[1, after], hits.at[1, after], relay_send.at[1],
                         relay_recv.at[1], me.left))
    relays[-1].start()
    for slot in range(2):
        for t in range(6):
            arrived(0, slot, t // 4, t % 4)
        for part, count in ((0, 4), (1, 2)):
            halos.append(remote(
                homes.at[slot, part, pl.ds(0, count), pl.ds(0, 2)],
                homes.at[slot, 4 + part, pl.ds(0, count), pl.ds(0, 2)],
                halo_send.at[slot, part], halo_recv.at[slot, part], me.left,
            ))
            halos[-1].start()
    pass_on(1)

    for slot in range(2):
        for t in range(6, 16):
            arrived(0, slot, t // 4, t % 4)
        for t in range(16):
            arrived(1, slot, t // 4, t % 4)
        for part, count in ((0, 4), (1, 2)):
            landed(homes.at[slot, 4 + part, pl.ds(0, count), pl.ds(0, 2)], halo_recv.at[slot, part])
            landed(field_homes.at[slot, 4 + part, pl.ds(0, count)], field_recv.at[slot, part])
        landed(hits.at[slot, opposite], relay_recv.at[slot])
    landed(hits.at[1, before], ring_recv.at[0, 1])
    landed(hits.at[0, after], ring_recv.at[1, 0])
    for copy in kept:
        copy.wait()
    for copy in ring + relays + halos:
        copy.wait_send()
    for copy in first + second:
        sent(me, *copy)


def traces(mom, seps, fields, products, hits, out, left_t, source, sums):
    f32 = jnp.float32
    tm = lax.axis_index("tm")
    plane, local = tm // 8, tm % 8
    diagonal = local == 0
    m1, m2, m3, m4 = (mom[i] for i in range(4))

    for role in range(2):
        for c in range(2):
            @pl.loop(0, 16)
            def _(part):
                block = hits[role, part // 4, pl.ds(2 * (part % 4), 2), c].reshape(BLK, BLK)
                left_t[role, pl.ds(c * BLK, BLK), pl.ds(pl.multiple_of(part * BLK, BLK), BLK)] = block.T

    @pl.loop(0, 16)
    def _(part):
        block = hits[0, part // 4, pl.ds(2 * (part % 4), 2), 4].reshape(BLK, BLK)
        source[:, pl.ds(pl.multiple_of(part * BLK, BLK), BLK)] = block.T[:16]

    def fold(value):
        return jnp.sum(value, axis=0, keepdims=True)

    @pl.loop(0, SPAN)
    def _(t):
        stamp = (plane * SPAN + t).astype(f32)
        chosen = (source[:1, :].astype(f32) == stamp).astype(f32).astype(jnp.bfloat16)
        totals = [[jnp.zeros((1, BLK), f32) for _ in range(8)] for _ in range(3)]
        for slot in range(2):
            mate = jnp.where(diagonal, slot, 1 - slot)
            right = jnp.concatenate(
                [hits[mate, :, :, 2 + c].reshape(2048, BLK) for c in range(2)], axis=1
            )
            pieces = jnp.dot(left_t[slot] * chosen, right, preferred_element_type=f32)
            w_re = (pieces[:BLK, :BLK] - pieces[BLK:, BLK:]).astype(jnp.bfloat16).astype(f32)
            w_im = (pieces[:BLK, BLK:] + pieces[BLK:, :BLK]).astype(jnp.bfloat16).astype(f32)
            p1 = [fields[slot, t, m1, c].astype(f32).T for c in range(2)]
            p4 = [fields[slot, t, m4, c].astype(f32).T for c in range(2)]
            rt = [products[slot, t, 2 + c].astype(f32) for c in range(2)]
            for k in range(3):
                u = t + seps[k]
                p2 = [fields[mate, u, m2, c].astype(f32) for c in range(2)]
                p3 = [fields[mate, u, m3, c].astype(f32) for c in range(2)]
                s = [products[slot, u, c].astype(f32) for c in range(2)]
                for at, (one, two) in enumerate(
                    ((p1, p2), (p4, p3), (rt, s), ((w_re, w_im), s))
                ):
                    totals[k][2 * at] += fold(one[0] * two[0] - one[1] * two[1])
                    totals[k][2 * at + 1] += fold(one[0] * two[1] + one[1] * two[0])
        for k in range(3):
            sums[3 * t + k] = jnp.concatenate(totals[k], axis=0)

    out[...] = jnp.sum(sums[...], axis=-1)


def reduce(part, out, gather, send, recv):
    me = Place()
    barrier = pltpu.get_barrier_semaphore()
    base = 8 * me.x
    mine = 4 * (me.tm % 8) + me.mode
    others = [(base + n // 4, n % 4) for n in range(32)]
    for n in range(32):
        @pl.when(mine != n)
        def _():
            pl.semaphore_signal(barrier, inc=1, device_id=others[n], device_id_type=MESH)
    pl.semaphore_wait(barrier, 31)
    copies = [(part.at[n // 4], gather.at[mine], send.at[n], recv.at[mine], others[n])
              for n in range(32)]
    for copy in copies:
        send_or_keep(me, *copy)
    for n in range(32):
        landed(gather.at[n], recv.at[n])
    total = jnp.sum(gather[...], axis=0)
    out[...] = total
    out[0:1] = total[0:1] * total[2:3] - total[1:2] * total[3:4]
    out[1:2] = total[0:1] * total[3:4] + total[1:2] * total[2:3]
    for copy in copies:
        sent(me, *copy)


def params(ident=None):
    if ident is None:
        return pltpu.CompilerParams(vmem_limit_bytes=VMEM_LIMIT)
    return pltpu.CompilerParams(
        vmem_limit_bytes=VMEM_LIMIT, collective_id=ident, has_side_effects=True
    )


def on_device(field_codes, scales, mom_index, separations, source_slice, noise_left, noise_right):
    mode = lax.axis_index("mode")
    bf16, f32 = jnp.bfloat16, jnp.float32
    dma = pltpu.SemaphoreType.DMA
    fields = (field_codes.astype(f32) * scales[:, :, None, :, None]).astype(bf16)
    fields = fields.transpose(1, 0, 2, 3, 4)
    mine = lax.dynamic_slice_in_dim(noise_left, mode * 256, 256, axis=2)
    noise = jnp.concatenate(
        [mine, noise_right, jnp.broadcast_to(source_slice.astype(bf16)[:, None, None], (64, 1, 256))],
        axis=1,
    )
    noise = noise.reshape(64, 5, 2, BLK).transpose(2, 1, 0, 3)

    any_spec = pl.BlockSpec(memory_space=ANY)
    smem = pl.BlockSpec(memory_space=pltpu.SMEM)
    vmem = pl.BlockSpec(memory_space=pltpu.VMEM)
    whole, field_homes, hits = pl.pallas_call(
        spread_fields,
        out_shape=(
            jax.ShapeDtypeStruct((2, 2, 1024, 1024), bf16),
            jax.ShapeDtypeStruct((2, 4, 4, 2, 2, BLK, BLK), bf16),
            jax.ShapeDtypeStruct((2, 4, 2, 5, 64, BLK), bf16),
        ),
        in_specs=[any_spec] * 2,
        out_specs=[any_spec] * 3,
        scratch_shapes=[
            pltpu.VMEM((4, 4, 2, 2, 2, BLK, BLK), bf16),
            pltpu.VMEM((4, 4, 5, 64, BLK), bf16),
            dma((2,)), dma((2,)), dma((2,)), dma((2,)),
            dma((2, 2, 4)), dma((4, 4)), dma((4, 4)), dma((2, 4, 2)),
            dma((2, 2, 4)), dma((4, 4)), dma((4, 4)), dma((2, 4, 2)),
        ],
        compiler_params=params(0),
        name="spread_fields",
    )(fields, noise)
    products = pl.pallas_call(
        multiply,
        out_shape=jax.ShapeDtypeStruct((4, 8, 4, BLK, BLK), bf16),
        in_specs=[smem, vmem],
        out_specs=vmem,
        compiler_params=params(),
        name="multiply",
    )(mom_index, whole)
    product_homes, field_homes, hits = pl.pallas_call(
        spread_products,
        out_shape=(
            jax.ShapeDtypeStruct((2, 6, 4, 4, BLK, BLK), bf16),
            jax.ShapeDtypeStruct((2, 6, 4, 2, 2, BLK, BLK), bf16),
            jax.ShapeDtypeStruct((2, 4, 4, 2, 5, 64, BLK), bf16),
        ),
        in_specs=[any_spec] * 3,
        out_specs=[any_spec] * 3,
        scratch_shapes=[
            pltpu.VMEM((2, 2, 4, 4, 2, BLK, BLK), bf16),
            dma((2, 4, 2, 4)), dma((2, 2, 4, 4)), dma((2, 2, 4, 4)), dma((2, 2, 4, 4)),
            dma((2, 2)), dma((2, 2)), dma((2, 2)), dma((2, 2)),
            dma((2, 2)), dma((2, 2)), dma((2,)), dma((2,)), dma((2, 2)),
        ],
        compiler_params=params(1),
        name="spread_products",
    )(products, field_homes, hits)
    part = pl.pallas_call(
        traces,
        out_shape=jax.ShapeDtypeStruct((3 * SPAN, 8), f32),
        in_specs=[smem, smem, vmem, vmem, vmem],
        out_specs=vmem,
        scratch_shapes=[
            pltpu.VMEM((2, 2 * BLK, 2048), bf16),
            pltpu.VMEM((16, 2048), bf16),
            pltpu.VMEM((3 * SPAN, 8, BLK), f32),
        ],
        compiler_params=params(),
        name="traces",
    )(
        mom_index, separations,
        field_homes.reshape(2, 24, 2, 2, BLK, BLK),
        product_homes.reshape(2, 24, 4, BLK, BLK),
        hits.reshape(2, 4, 8, 5, 64, BLK),
    )
    part = jnp.pad(part.reshape(8, 6, 8).transpose(0, 2, 1), ((0, 0), (0, 0), (0, BLK - 6)))
    total = pl.pallas_call(
        reduce,
        out_shape=jax.ShapeDtypeStruct((8, BLK), f32),
        in_specs=[vmem],
        out_specs=vmem,
        scratch_shapes=[pltpu.VMEM((32, 8, BLK), f32), dma((32,)), dma((32,))],
        compiler_params=params(2),
        name="reduce",
    )(part)
    table = total[:, :6].T.reshape(2, 3, 8)
    return table[..., 0:2], table[..., 4:6], table[..., 6:8]


def solution(mesh):
    in_specs = (
        P(None, "tm", None, "mode", None),
        P(None, "tm", "mode"),
        P(),
        P(),
        P("tm"),
        P("tm", None, None),
        P("tm", None, "mode"),
    )
    out_specs = (P("tm", None, None), P("tm", None, None), P("tm", None, None))
    return jax.shard_map(
        on_device, mesh=mesh, in_specs=in_specs, out_specs=out_specs, check_vma=False
    )
```

```python
import jax
import jax.numpy as jnp
from jax import lax
from jax.experimental import pallas as pl
from jax.experimental.pallas import tpu as pltpu
from jax.sharding import PartitionSpec as P

MESH = pl.DeviceIdType.MESH
ANY = pl.ANY
BLK = 128
SPAN = 16
VMEM_LIMIT = 56 * 1024 * 1024


def home(i, half, e, same):
    if same:
        if e == 0:
            unit, slot = i % 2, i // 2
        elif e == 1:
            unit, slot = 4 + i, 0
        elif e == 2:
            unit, slot = 2 + i % 2, i // 2
        else:
            unit, slot = 4 + (i + 3) % 4, 1
        return unit // 2, 0, half, unit % 2, slot, 4 * half + (i + e) % 4
    upper, lower = i + half * (e - i), e + half * (i - e)
    return upper, 1, (i + e) % 2, lower // 2, half, 4 * (1 - half) + e


def blocks_of(z, lo, hi, core):
    if z < 2:
        near = (core, core + 2)
    elif z == 2:
        near = (core, core + 1)
    else:
        near = (2 + core, (3 + core) % 4)
    far = (z, 4 + 2 * core + (hi + z) % 2)
    return tuple(4 * hi * (1 - lo) + n + lo * (f - n) for n, f in zip(near, far))


class Place:
    def __init__(self):
        self.tm = lax.axis_index("tm")
        self.mode = lax.axis_index("mode")
        self.x, self.z, self.lo = self.tm // 8, (self.tm // 2) % 4, self.tm % 2
        self.hi, self.core = self.mode // 2, self.mode % 2
        self.right = ((self.tm + 8) % 32, self.mode)
        self.left = ((self.tm + 24) % 32, self.mode)

    def at(self, z, lo, hi, core):
        return (8 * self.x + 2 * z + lo, 2 * hi + core)

    def is_here(self, device):
        return jnp.logical_and(device[0] == self.tm, device[1] == self.mode)


def greet(place):
    barrier = pltpu.get_barrier_semaphore()

    def signal(device):
        pl.semaphore_signal(barrier, inc=1, device_id=device, device_id_type=MESH)

    for core in range(2):
        for z in range(4):

            @pl.when(jnp.logical_or(place.z != z, place.core != core))
            def _():
                signal(place.at(z, place.lo, place.hi, core))

        for y in range(4):

            @pl.when(jnp.logical_or(place.lo != y // 2, place.hi != y % 2))
            def _():
                signal(place.at(place.z, y // 2, y % 2, core))

    signal(place.right)
    signal(place.left)
    pl.semaphore_wait(barrier, 15)


def remote(src, dst, send, recv, device):
    return pltpu.make_async_remote_copy(
        src_ref=src, dst_ref=dst, send_sem=send, recv_sem=recv,
        device_id=device, device_id_type=MESH,
    )


def send_or_keep(place, src, dst, send, recv, device):
    here = place.is_here(device)

    @pl.when(jnp.logical_not(here))
    def _():
        remote(src, dst, send, recv, device).start()

    @pl.when(here)
    def _():
        pltpu.make_async_copy(src, dst, recv).start()


def sent(place, src, dst, send, recv, device):
    @pl.when(jnp.logical_not(place.is_here(device)))
    def _():
        remote(src, dst, send, recv, device).wait_send()


def landed(ref, sem):
    pltpu.make_async_copy(ref, ref, sem).wait()


def pair_sums(one, two):
    real = one[0] * two[0] - one[1] * two[1]
    imag = one[0] * two[1] + one[1] * two[0]
    return [jnp.sum(value, axis=0, keepdims=True) for value in (real, imag)]


def contract(
    mom, seps, fields, noise, out,
    whole, homes, mid_y, mid_z, products, mid, product_homes, mid_hits, hits,
    left_t, source, weights, box_sums, product_sums,
    asm_send, asm_recv, fwd_send, fwd_recv,
    hit_z_send, hit_z_recv, hit_y_send, hit_y_recv,
    ring_send, ring_recv, relay_send, relay_recv,
    near_send, cross_z_send, cross_z_recv, cross_y_send,
    whole_z_send, whole_y_send, whole_y_recv, whole_pass_send, home_recv,
    send1, recv1, send2, recv2,
    field_send, field_recv, halo_send, halo_recv,
):
    f32, bf16 = jnp.float32, jnp.bfloat16
    me = Place()
    greet(me)
    flip = me.tm + 1 - 2 * me.lo
    when = 2 * (1 - me.lo) + me.hi
    sends = []

    def start(*copy, only=None):
        sends.append((copy, only))
        if only is None:
            send_or_keep(me, *copy)
        else:

            @pl.when(me.lo == only)
            def _():
                send_or_keep(me, *copy)

    def tile(n):
        return pl.ds(n * BLK if isinstance(n, int) else pl.multiple_of(n * BLK, BLK), BLK)

    def rows_of(block):
        return whole.at[:, :, pl.ds(pl.multiple_of(block * 256, 256), 256), :]

    assembly = [
        remote(fields.at[s], rows_of(me.mode), asm_send.at[s], asm_recv.at[me.hi],
               (flip, 2 * s + me.core))
        for s in range(2)
    ]
    for copy in assembly:
        copy.start()

    for a in range(2):
        for same in (False, True):
            for e in range(4):
                z, lo, hi, core, slot, col = home(2 * me.core + a, me.hi, e, same)
                group = slot if same else 2 + hi
                start(noise.at[a], mid_hits.at[group, me.z], hit_z_send.at[a, int(same), e],
                      hit_z_recv.at[group, me.z], me.at(z, me.lo, me.hi, core))

    def half_way(s, a, z, core, col, e, group):
        start(fields.at[s, :, :, tile(a), tile(col)], mid_y.at[group, me.z],
              cross_z_send.at[a, e], cross_z_recv.at[group, me.z], me.at(z, me.lo, me.hi, core))

    for a in range(2):
        row = 2 * me.core + a
        for e in range(4):
            z, _, hi, core, slot, col = home(row, me.hi, e, True)
            far = home(row, me.hi, e, False)

            def pick(one, two):
                return one + me.lo * (two - one)

            half_way(pick(1 - far[2], 1 - me.hi), a, pick(far[0], z), pick(far[3], core),
                     pick(far[5], col), e, pick(far[2], slot))
        for e in range(4):
            z, _, hi, core, slot, col = home(row, me.hi, e, True)
            for s in range(2):

                start(fields.at[s, :, :, tile(a), tile(col)], homes.at[slot, me.z, s],
                      near_send.at[s, a, e], home_recv.at[slot, me.z, s],
                      me.at(z, 0, me.hi, core), only=0)

        for b in range(2):
            other = 2 * b + (me.hi + a) % 2
            z, _, hi, core, slot, col = home(row, me.hi, other, False)
            for s in range(2):

                start(fields.at[s, :, :, tile(a), tile(col)], homes.at[slot, me.z, 2 + s],
                      near_send.at[s, a, 4 + b], home_recv.at[slot, me.z, 2 + s],
                      me.at(z, 1, me.hi, core), only=1)

    for z in range(4):
        for group in range(4):
            if group < 2:
                slot, device = group, me.at(me.z, 0, me.hi, me.core)
            else:
                slot, device = me.hi, me.at(me.z, 1, group - 2, me.core)
            landed(mid_hits.at[group, z], hit_z_recv.at[group, z])
            start(mid_hits.at[group, z], hits.at[slot, me.x, z, me.lo],
                  hit_y_send.at[group, z], hit_y_recv.at[slot, z, me.lo], device)

    for slot in range(2):
        for z in range(4):
            for lo in range(2):
                landed(hits.at[slot, me.x, z, lo], hit_y_recv.at[slot, z, lo])
    ring = []
    for slot in range(2):
        own = hits.at[slot, me.x]
        ring.append(remote(own, own, ring_send.at[0, slot], ring_recv.at[0, slot], me.right))
        ring.append(remote(own, own, ring_send.at[1, slot], ring_recv.at[1, slot], me.left))
    for copy in ring:
        copy.start()

    forwards = []
    for h in range(2):
        block = rows_of(2 * h + me.core)
        landed(block, asm_recv.at[h])
        forwards.append(remote(block, block, fwd_send.at[h], fwd_recv.at[h],
                               (me.tm, me.mode + 1 - 2 * me.core)))
        forwards[-1].start()

    for z in range(4):
        for group in range(2):
            landed(mid_y.at[group, z], cross_z_recv.at[group, z])
            lo, hi = 1 - me.lo, group + me.lo * (me.hi - group)
            slot = me.hi + me.lo * (group - me.hi)
            t = 2 * me.lo + (1 - group) + me.lo * (group - me.hi)
            start(mid_y.at[group, z], homes.at[slot, z, t], cross_y_send.at[group, z],
                  home_recv.at[slot, z, t], me.at(me.z, lo, hi, me.core))

    before, after, opposite = (me.x + 3) % 4, (me.x + 1) % 4, (me.x + 2) % 4
    relays = []
    for slot in range(2):
        landed(hits.at[slot, before], ring_recv.at[0, slot])
        relays.append(remote(hits.at[slot, before], hits.at[slot, before], relay_send.at[slot],
                             relay_recv.at[slot], me.right))
        relays[-1].start()

    for h in range(2):
        landed(rows_of(2 * h + 1 - me.core), fwd_recv.at[h])
    for hi in range(2):
        for z in range(4):
            pair = blocks_of(z, 1, hi, me.core)
            row, col = pair[1 - hi], pair[hi]

            start(whole.at[:, :, tile(row), tile(col)], mid_z.at[me.hi, z],
                  whole_y_send.at[hi, z], whole_y_recv.at[me.hi, z],
                  me.at(me.z, 1, hi, me.core), only=0)
    for z in range(4):
        pair = blocks_of(z, me.lo, me.hi, me.core)
        for slot in range(2):
            row, col = pair[slot], pair[1 - slot]
            if z == 0:
                col = col + (1 - me.lo) * (row - col)
            start(whole.at[:, :, tile(row), tile(col)], homes.at[slot, me.z, when],
                  whole_z_send.at[z, slot], home_recv.at[slot, me.z, when],
                  me.at(z, me.lo, me.hi, me.core))

    base = pl.multiple_of(me.core * 512, 512)
    m1, m2, m3, m4 = (mom[i] for i in range(4))

    def cdot(ar, ai, br, bi):
        def dot(a, b):
            return jnp.dot(a, b, preferred_element_type=f32)

        return dot(ar, br) - dot(ai, bi), dot(ar, bi) + dot(ai, br)

    @pl.loop(0, 4)
    def _(pair):
        cols = pl.ds(pl.multiple_of(pair * 256, 256), 256)
        rows = pl.ds(base, 512)
        parts = cdot(whole[m2, 0, rows, :], whole[m2, 1, rows, :],
                     whole[m3, 0, :, cols], whole[m3, 1, :, cols])
        for c in range(2):
            for a in range(4):
                for b in range(2):
                    piece = parts[c][a * BLK:(a + 1) * BLK, b * BLK:(b + 1) * BLK]
                    products[0, a, 2 * pair + b, c] = piece.astype(bf16)

    def right_product():
        @pl.loop(0, 4)
        def _(step):
            pair, half = step // 2, step % 2
            cols = pl.ds(pl.multiple_of(base + pair * 256, 256), 256)
            rows = pl.ds(pl.multiple_of(half * 512, 512), 512)
            parts = cdot(whole[m4, 0, rows, :], whole[m4, 1, rows, :],
                         whole[m1, 0, :, cols], whole[m1, 1, :, cols])
            for c in range(2):
                for a in range(2):
                    for b in range(4):
                        piece = parts[c][b * BLK:(b + 1) * BLK, a * BLK:(a + 1) * BLK]
                        products[1, 2 * pair + a, 4 * half + b, c] = piece.T.astype(bf16)

    def send_products(p):
        for i in range(4):
            for same in (False, True):
                for e in range(4):
                    z, lo, hi, core, slot, col = home(i, me.core, e, same)

                    def either(one, two):
                        return one + slot * (two - one)

                    device = me.at(either(me.z, z), either(lo, me.lo), either(hi, me.hi), core)
                    at = (p, slot, either(z, 2 * lo + hi), either(when, me.z))
                    start(products.at[p, i, col], mid.at[at], send1.at[p, i, int(same), e],
                          recv1.at[at], device)

    def pass_on(p):
        for j in range(4):
            for k in range(4):
                landed(mid.at[p, 0, k, j], recv1.at[p, 0, k, j])
                start(mid.at[p, 0, k, j], product_homes.at[p, 0, me.z, j],
                      send2.at[p, 0, k, j], recv2.at[p, 0, me.z, j],
                      me.at(k, me.lo, me.hi, me.core))
                landed(mid.at[p, 1, k, j], recv1.at[p, 1, k, j])
                start(mid.at[p, 1, k, j], product_homes.at[p, 1, j, when],
                      send2.at[p, 1, k, j], recv2.at[p, 1, j, when],
                      me.at(me.z, k // 2, k % 2, me.core))

    send_products(0)

    for hi in range(2):
        for z in range(4):

            @pl.when(me.lo == 1)
            def _():
                landed(mid_z.at[hi, z], whole_y_recv.at[hi, z])

            start(mid_z.at[hi, z], homes.at[1 - me.hi, me.z, 2 + hi],
                  whole_pass_send.at[hi, z], home_recv.at[1 - me.hi, me.z, 2 + hi],
                  me.at(z, 1, me.hi, me.core), only=1)

    right_product()
    send_products(1)

    halos = []
    parts = ((0, 4), (1, 2))
    for slot in range(2):
        for t in range(6):
            landed(homes.at[slot, t // 4, t % 4], home_recv.at[slot, t // 4, t % 4])
        for part, count in parts:
            halos.append(remote(
                homes.at[slot, part, pl.ds(0, count)], homes.at[slot, 4 + part, pl.ds(0, count)],
                field_send.at[slot, part], field_recv.at[slot, part], me.left,
            ))
            halos[-1].start()

    pass_on(0)

    for slot in range(2):
        landed(hits.at[slot, after], ring_recv.at[1, slot])
        landed(hits.at[slot, opposite], relay_recv.at[slot])
    for role in range(2):
        for c in range(2):

            @pl.loop(0, 16)
            def _(part):
                block = hits[role, part // 4, part % 4, :, c].reshape(BLK, BLK)
                left_t[role, pl.ds(c * BLK, BLK), tile(part)] = block.T

    @pl.loop(0, 16)
    def _(part):
        block = hits[0, part // 4, part % 4, :, 4].reshape(BLK, BLK)
        source[:, tile(part)] = block.T[:16]

    diagonal = jnp.logical_and(me.lo == 0, me.z == 0)

    @pl.loop(0, SPAN)
    def _(t):
        stamp = (me.x * SPAN + t).astype(f32)
        chosen = (source[:1, :].astype(f32) == stamp).astype(f32).astype(bf16)
        for slot in range(2):
            mate = jnp.where(diagonal, slot, 1 - slot)
            right = jnp.concatenate(
                [hits[mate, :, :, :, 2 + c].reshape(2048, BLK) for c in range(2)], axis=1
            )
            pieces = jnp.dot(left_t[slot] * chosen, right, preferred_element_type=f32)
            weights[slot, t, 0] = (pieces[:BLK, :BLK] - pieces[BLK:, BLK:]).astype(bf16)
            weights[slot, t, 1] = (pieces[:BLK, BLK:] + pieces[BLK:, :BLK]).astype(bf16)

    for slot in range(2):
        for t in range(6):
            landed(product_homes.at[0, slot, t // 4, t % 4], recv2.at[0, slot, t // 4, t % 4])
        for part, count in parts:
            halos.append(remote(
                product_homes.at[0, slot, part, pl.ds(0, count)],
                product_homes.at[0, slot, 4 + part, pl.ds(0, count)],
                halo_send.at[slot, part], halo_recv.at[slot, part], me.left,
            ))
            halos[-1].start()
    pass_on(1)

    for slot in range(2):
        for t in range(6, 16):
            landed(homes.at[slot, t // 4, t % 4], home_recv.at[slot, t // 4, t % 4])
        for part, count in parts:
            landed(homes.at[slot, 4 + part, pl.ds(0, count)], field_recv.at[slot, part])

    @pl.loop(0, SPAN)
    def _(t):
        totals = [[jnp.zeros((1, BLK), f32) for _ in range(4)] for _ in range(3)]
        for slot in range(2):
            mate = jnp.where(diagonal, slot, 1 - slot)
            p1 = [homes[slot, t // 4, t % 4, m1, c].astype(f32).T for c in range(2)]
            p4 = [homes[slot, t // 4, t % 4, m4, c].astype(f32).T for c in range(2)]
            for k in range(3):
                u = t + seps[k]
                p2 = [homes[mate, u // 4, u % 4, m2, c].astype(f32) for c in range(2)]
                p3 = [homes[mate, u // 4, u % 4, m3, c].astype(f32) for c in range(2)]
                new = pair_sums(p1, p2) + pair_sums(p4, p3)
                totals[k] = [a + b for a, b in zip(totals[k], new)]
        for k in range(3):
            box_sums[3 * t + k] = jnp.concatenate(totals[k], axis=0)

    for slot in range(2):
        for t in range(6, 16):
            landed(product_homes.at[0, slot, t // 4, t % 4], recv2.at[0, slot, t // 4, t % 4])
        for t in range(16):
            landed(product_homes.at[1, slot, t // 4, t % 4], recv2.at[1, slot, t // 4, t % 4])
        for part, count in parts:
            landed(product_homes.at[0, slot, 4 + part, pl.ds(0, count)], halo_recv.at[slot, part])

    @pl.loop(0, SPAN)
    def _(t):
        totals = [[jnp.zeros((1, BLK), f32) for _ in range(4)] for _ in range(3)]
        for slot in range(2):
            rt = [product_homes[1, slot, t // 4, t % 4, c].astype(f32) for c in range(2)]
            w = [weights[slot, t, c].astype(f32) for c in range(2)]
            for k in range(3):
                u = t + seps[k]
                s = [product_homes[0, slot, u // 4, u % 4, c].astype(f32) for c in range(2)]
                new = pair_sums(rt, s) + pair_sums(w, s)
                totals[k] = [a + b for a, b in zip(totals[k], new)]
        for k in range(3):
            product_sums[3 * t + k] = jnp.concatenate(totals[k], axis=0)

    out[:, 0:4] = jnp.sum(box_sums[...], axis=-1)
    out[:, 4:8] = jnp.sum(product_sums[...], axis=-1)

    for copy in assembly + forwards + ring + relays + halos:
        copy.wait_send()
    for copy, only in sends:
        if only is None:
            sent(me, *copy)
        else:

            @pl.when(me.lo == only)
            def _():
                sent(me, *copy)


def reduce(part, out, gather, send, recv):
    me = Place()
    barrier = pltpu.get_barrier_semaphore()
    base = 8 * me.x
    mine = 4 * (me.tm % 8) + me.mode
    others = [(base + n // 4, n % 4) for n in range(32)]
    for n in range(32):
        @pl.when(mine != n)
        def _():
            pl.semaphore_signal(barrier, inc=1, device_id=others[n], device_id_type=MESH)
    pl.semaphore_wait(barrier, 31)
    copies = [(part.at[n // 4], gather.at[mine], send.at[n], recv.at[mine], others[n])
              for n in range(32)]
    for copy in copies:
        send_or_keep(me, *copy)
    for n in range(32):
        landed(gather.at[n], recv.at[n])
    total = jnp.sum(gather[...], axis=0)
    out[...] = total
    out[0:1] = total[0:1] * total[2:3] - total[1:2] * total[3:4]
    out[1:2] = total[0:1] * total[3:4] + total[1:2] * total[2:3]
    for copy in copies:
        sent(me, *copy)


def params(ident):
    return pltpu.CompilerParams(
        vmem_limit_bytes=VMEM_LIMIT, collective_id=ident, has_side_effects=True
    )


def on_device(field_codes, scales, mom_index, separations, source_slice, noise_left, noise_right):
    mode = lax.axis_index("mode")
    bf16, f32 = jnp.bfloat16, jnp.float32
    dma = pltpu.SemaphoreType.DMA
    fields = (field_codes.astype(f32) * scales[:, :, None, :, None]).astype(bf16)
    fields = fields.transpose(1, 0, 2, 3, 4)
    mine = lax.dynamic_slice_in_dim(noise_left, mode * 256, 256, axis=2)
    noise = jnp.concatenate(
        [mine, noise_right, jnp.broadcast_to(source_slice.astype(bf16)[:, None, None], (64, 1, 256))],
        axis=1,
    )
    noise = noise.reshape(64, 5, 2, BLK).transpose(2, 1, 0, 3)

    any_spec = pl.BlockSpec(memory_space=ANY)
    smem = pl.BlockSpec(memory_space=pltpu.SMEM)
    vmem = pl.BlockSpec(memory_space=pltpu.VMEM)
    dims = lambda *shape: pltpu.VMEM(shape, bf16)
    part = pl.pallas_call(
        contract,
        out_shape=jax.ShapeDtypeStruct((3 * SPAN, 8), f32),
        in_specs=[smem, smem, any_spec, any_spec],
        out_specs=vmem,
        scratch_shapes=[
            dims(2, 2, 1024, 1024),
            dims(2, 6, 4, 2, 2, BLK, BLK),
            dims(2, 4, 2, 2, BLK, BLK),
            dims(2, 4, 2, 2, BLK, BLK),
            dims(2, 4, 8, 2, BLK, BLK),
            dims(2, 2, 4, 4, 2, BLK, BLK),
            dims(2, 2, 6, 4, 2, BLK, BLK),
            dims(4, 4, 5, 64, BLK),
            dims(2, 4, 4, 2, 5, 64, BLK),
            dims(2, 2 * BLK, 2048),
            dims(16, 2048),
            dims(2, SPAN, 2, BLK, BLK),
            pltpu.VMEM((3 * SPAN, 4, BLK), f32),
            pltpu.VMEM((3 * SPAN, 4, BLK), f32),
            dma((2,)), dma((2,)), dma((2,)), dma((2,)),
            dma((2, 2, 4)), dma((4, 4)), dma((4, 4)), dma((2, 4, 2)),
            dma((2, 2)), dma((2, 2)), dma((2,)), dma((2,)),
            dma((2, 2, 6)), dma((2, 4)), dma((2, 4)), dma((2, 4)),
            dma((4, 2)), dma((2, 4)), dma((2, 4)), dma((2, 4)), dma((2, 4, 4)),
            dma((2, 4, 2, 4)), dma((2, 2, 4, 4)), dma((2, 2, 4, 4)), dma((2, 2, 4, 4)),
            dma((2, 2)), dma((2, 2)), dma((2, 2)), dma((2, 2)),
        ],
        compiler_params=params(0),
        name="contract",
    )(mom_index, separations, fields, noise)
    part = jnp.pad(part.reshape(8, 6, 8).transpose(0, 2, 1), ((0, 0), (0, 0), (0, BLK - 6)))
    total = pl.pallas_call(
        reduce,
        out_shape=jax.ShapeDtypeStruct((8, BLK), f32),
        in_specs=[vmem],
        out_specs=vmem,
        scratch_shapes=[pltpu.VMEM((32, 8, BLK), f32), dma((32,)), dma((32,))],
        compiler_params=params(2),
        name="reduce",
    )(part)
    table = total[:, :6].T.reshape(2, 3, 8)
    return table[..., 0:2], table[..., 4:6], table[..., 6:8]


def solution(mesh):
    in_specs = (
        P(None, "tm", None, "mode", None),
        P(None, "tm", "mode"),
        P(),
        P(),
        P("tm"),
        P("tm", None, None),
        P("tm", None, "mode"),
    )
    out_specs = (P("tm", None, None), P("tm", None, None), P("tm", None, None))
    return jax.shard_map(
        on_device, mesh=mesh, in_specs=in_specs, out_specs=out_specs, check_vma=False
    )
```

```python
import jax
import jax.numpy as jnp
from jax import lax
from jax.experimental import pallas as pl
from jax.experimental.pallas import tpu as pltpu
from jax.sharding import PartitionSpec as P

MESH = pl.DeviceIdType.MESH
ANY = pl.ANY
BLK = 128
SPAN = 16
VMEM_LIMIT = 56 * 1024 * 1024


def home(i, half, e, same):
    if same:
        if e == 0:
            unit, slot = i % 2, i // 2
        elif e == 1:
            unit, slot = 4 + i, 0
        elif e == 2:
            unit, slot = 2 + i % 2, i // 2
        else:
            unit, slot = 4 + (i + 3) % 4, 1
        return unit // 2, 0, half, unit % 2, slot, 4 * half + (i + e) % 4
    upper, lower = i + half * (e - i), e + half * (i - e)
    return upper, 1, (i + e) % 2, lower // 2, half, 4 * (1 - half) + e


def blocks_of(z, lo, hi, core):
    if z < 2:
        near = (core, core + 2)
    elif z == 2:
        near = (core, core + 1)
    else:
        near = (2 + core, (3 + core) % 4)
    far = (z, 4 + 2 * core + (hi + z) % 2)
    return tuple(4 * hi * (1 - lo) + n + lo * (f - n) for n, f in zip(near, far))


class Place:
    def __init__(self):
        self.tm = lax.axis_index("tm")
        self.mode = lax.axis_index("mode")
        self.x, self.z, self.lo = self.tm // 8, (self.tm // 2) % 4, self.tm % 2
        self.hi, self.core = self.mode // 2, self.mode % 2
        self.right = ((self.tm + 8) % 32, self.mode)
        self.left = ((self.tm + 24) % 32, self.mode)

    def at(self, z, lo, hi, core):
        return (8 * self.x + 2 * z + lo, 2 * hi + core)

    def is_here(self, device):
        return jnp.logical_and(device[0] == self.tm, device[1] == self.mode)


def greet(place):
    barrier = pltpu.get_barrier_semaphore()

    def signal(device):
        pl.semaphore_signal(barrier, inc=1, device_id=device, device_id_type=MESH)

    for n in range(32):
        device = (8 * place.x + n // 4, n % 4)

        @pl.when(jnp.logical_not(place.is_here(device)))
        def _():
            signal(device)

    signal(place.right)
    signal(place.left)
    pl.semaphore_wait(barrier, 33)


def remote(src, dst, send, recv, device):
    return pltpu.make_async_remote_copy(
        src_ref=src, dst_ref=dst, send_sem=send, recv_sem=recv,
        device_id=device, device_id_type=MESH,
    )


def send_or_keep(place, src, dst, send, recv, device):
    here = place.is_here(device)

    @pl.when(jnp.logical_not(here))
    def _():
        remote(src, dst, send, recv, device).start()

    @pl.when(here)
    def _():
        pltpu.make_async_copy(src, dst, recv).start()


def sent(place, src, dst, send, recv, device):
    @pl.when(jnp.logical_not(place.is_here(device)))
    def _():
        remote(src, dst, send, recv, device).wait_send()


def landed(ref, sem):
    pltpu.make_async_copy(ref, ref, sem).wait()


def pair_sums(one, two):
    real = one[0] * two[0] - one[1] * two[1]
    imag = one[0] * two[1] + one[1] * two[0]
    return [jnp.sum(value, axis=0, keepdims=True) for value in (real, imag)]


def contract(
    mom, seps, fields, noise, out,
    whole, homes, mid_y, mid_z, products, mid, s_homes, r_homes, mid_hits, hits,
    left_t, source, weights, box_sums, cross_sums, noise_sums, tiles, gather,
    asm_send, asm_recv, fwd_send, fwd_recv,
    hit_z_send, hit_z_recv, hit_y_send, hit_y_recv,
    ring_send, ring_recv, relay_send, relay_recv,
    near_send, cross_z_send, cross_z_recv, cross_y_send,
    whole_z_send, whole_y_send, whole_y_recv, whole_pass_send, home_recv,
    send1, recv1, send2, recv2,
    field_send, field_recv, halo_send, halo_recv, sum_send, sum_recv,
):
    f32, bf16 = jnp.float32, jnp.bfloat16
    me = Place()
    greet(me)
    flip = me.tm + 1 - 2 * me.lo
    tiles[...] = jnp.zeros_like(tiles)
    when = 2 * (1 - me.lo) + me.hi
    sends = []

    def start(*copy, only=None):
        sends.append((copy, only))
        if only is None:
            send_or_keep(me, *copy)
        else:

            @pl.when(me.lo == only)
            def _():
                send_or_keep(me, *copy)

    def tile(n):
        return pl.ds(n * BLK if isinstance(n, int) else pl.multiple_of(n * BLK, BLK), BLK)

    def rows_of(block):
        return whole.at[:, :, pl.ds(pl.multiple_of(block * 256, 256), 256), :]

    assembly = [
        remote(fields.at[s], rows_of(me.mode), asm_send.at[s], asm_recv.at[me.hi],
               (flip, 2 * s + me.core))
        for s in range(2)
    ]
    for copy in assembly:
        copy.start()

    for a in range(2):
        for same in (False, True):
            for e in range(4):
                z, lo, hi, core, slot, col = home(2 * me.core + a, me.hi, e, same)
                group = slot if same else 2 + hi
                start(noise.at[a], mid_hits.at[group, me.z], hit_z_send.at[a, int(same), e],
                      hit_z_recv.at[group, me.z], me.at(z, me.lo, me.hi, core))

    def half_way(s, a, z, core, col, e, group):
        start(fields.at[s, :, :, tile(a), tile(col)], mid_y.at[group, me.z],
              cross_z_send.at[a, e], cross_z_recv.at[group, me.z], me.at(z, me.lo, me.hi, core))

    for a in range(2):
        row = 2 * me.core + a
        for e in range(4):
            z, _, hi, core, slot, col = home(row, me.hi, e, True)
            far = home(row, me.hi, e, False)

            def pick(one, two):
                return one + me.lo * (two - one)

            half_way(pick(1 - far[2], 1 - me.hi), a, pick(far[0], z), pick(far[3], core),
                     pick(far[5], col), e, pick(far[2], slot))
        for e in range(4):
            z, _, hi, core, slot, col = home(row, me.hi, e, True)
            for s in range(2):

                start(fields.at[s, :, :, tile(a), tile(col)], homes.at[slot, me.z, s],
                      near_send.at[s, a, e], home_recv.at[slot, me.z, s],
                      me.at(z, 0, me.hi, core), only=0)

        for b in range(2):
            other = 2 * b + (me.hi + a) % 2
            z, _, hi, core, slot, col = home(row, me.hi, other, False)
            for s in range(2):

                start(fields.at[s, :, :, tile(a), tile(col)], homes.at[slot, me.z, 2 + s],
                      near_send.at[s, a, 4 + b], home_recv.at[slot, me.z, 2 + s],
                      me.at(z, 1, me.hi, core), only=1)

    for z in range(4):
        for group in range(4):
            if group < 2:
                slot, device = group, me.at(me.z, 0, me.hi, me.core)
            else:
                slot, device = me.hi, me.at(me.z, 1, group - 2, me.core)
            landed(mid_hits.at[group, z], hit_z_recv.at[group, z])
            start(mid_hits.at[group, z], hits.at[slot, me.x, z, me.lo],
                  hit_y_send.at[group, z], hit_y_recv.at[slot, z, me.lo], device)

    forwards = []
    for h in range(2):
        block = rows_of(2 * h + me.core)
        landed(block, asm_recv.at[h])
        forwards.append(remote(block, block, fwd_send.at[h], fwd_recv.at[h],
                               (me.tm, me.mode + 1 - 2 * me.core)))
        forwards[-1].start()

    for slot in range(2):
        for z in range(4):
            for lo in range(2):
                landed(hits.at[slot, me.x, z, lo], hit_y_recv.at[slot, z, lo])
    ring = []
    for slot in range(2):
        own = hits.at[slot, me.x]
        ring.append(remote(own, own, ring_send.at[0, slot], ring_recv.at[0, slot], me.right))
        ring.append(remote(own, own, ring_send.at[1, slot], ring_recv.at[1, slot], me.left))
    for copy in ring:
        copy.start()

    for z in range(4):
        for group in range(2):
            landed(mid_y.at[group, z], cross_z_recv.at[group, z])
            lo, hi = 1 - me.lo, group + me.lo * (me.hi - group)
            slot = me.hi + me.lo * (group - me.hi)
            t = 2 * me.lo + (1 - group) + me.lo * (group - me.hi)
            start(mid_y.at[group, z], homes.at[slot, z, t], cross_y_send.at[group, z],
                  home_recv.at[slot, z, t], me.at(me.z, lo, hi, me.core))

    for h in range(2):
        landed(rows_of(2 * h + 1 - me.core), fwd_recv.at[h])
    for hi in range(2):
        for z in range(4):
            pair = blocks_of(z, 1, hi, me.core)
            row, col = pair[1 - hi], pair[hi]

            start(whole.at[:, :, tile(row), tile(col)], mid_z.at[me.hi, z],
                  whole_y_send.at[hi, z], whole_y_recv.at[me.hi, z],
                  me.at(me.z, 1, hi, me.core), only=0)
    for z in range(4):
        pair = blocks_of(z, me.lo, me.hi, me.core)
        for slot in range(2):
            row, col = pair[slot], pair[1 - slot]
            if z == 0:
                col = col + (1 - me.lo) * (row - col)
            start(whole.at[:, :, tile(row), tile(col)], homes.at[slot, me.z, when],
                  whole_z_send.at[z, slot], home_recv.at[slot, me.z, when],
                  me.at(z, me.lo, me.hi, me.core))

    base = pl.multiple_of(me.core * 512, 512)
    m1, m2, m3, m4 = (mom[i] for i in range(4))

    def cdot(ar, ai, br, bi):
        def dot(a, b):
            return jnp.dot(a, b, preferred_element_type=f32)

        return dot(ar, br) - dot(ai, bi), dot(ar, bi) + dot(ai, br)

    @pl.loop(0, 4)
    def _(pair):
        cols = pl.ds(pl.multiple_of(pair * 256, 256), 256)
        rows = pl.ds(base, 512)
        parts = cdot(whole[m2, 0, rows, :], whole[m2, 1, rows, :],
                     whole[m3, 0, :, cols], whole[m3, 1, :, cols])
        for c in range(2):
            for a in range(4):
                for b in range(2):
                    piece = parts[c][a * BLK:(a + 1) * BLK, b * BLK:(b + 1) * BLK]
                    products[0, a, 2 * pair + b, c] = piece.astype(bf16)

    def right_product():
        @pl.loop(0, 4)
        def _(step):
            pair, half = step // 2, step % 2
            cols = pl.ds(pl.multiple_of(base + pair * 256, 256), 256)
            rows = pl.ds(pl.multiple_of(half * 512, 512), 512)
            parts = cdot(whole[m4, 0, rows, :], whole[m4, 1, rows, :],
                         whole[m1, 0, :, cols], whole[m1, 1, :, cols])
            for c in range(2):
                for a in range(2):
                    for b in range(4):
                        piece = parts[c][b * BLK:(b + 1) * BLK, a * BLK:(a + 1) * BLK]
                        products[1, 2 * pair + a, 4 * half + b, c] = piece.T.astype(bf16)

    def send_products(p):
        for i in range(4):
            for same in (False, True):
                for e in range(4):
                    z, lo, hi, core, slot, col = home(i, me.core, e, same)

                    def either(one, two):
                        return one + slot * (two - one)

                    device = me.at(either(me.z, z), either(lo, me.lo), either(hi, me.hi), core)
                    at = (p, slot, either(z, 2 * lo + hi), either(when, me.z))
                    start(products.at[p, i, col], mid.at[at], send1.at[p, i, int(same), e],
                          recv1.at[at], device)

    def pass_on(p):
        for j in range(4):
            for k in range(4):
                landed(mid.at[p, 0, k, j], recv1.at[p, 0, k, j])
                start(mid.at[p, 0, k, j], (s_homes, r_homes)[p].at[0, me.z, j],
                      send2.at[p, 0, k, j], recv2.at[p, 0, me.z, j],
                      me.at(k, me.lo, me.hi, me.core))
                landed(mid.at[p, 1, k, j], recv1.at[p, 1, k, j])
                start(mid.at[p, 1, k, j], (s_homes, r_homes)[p].at[1, j, when],
                      send2.at[p, 1, k, j], recv2.at[p, 1, j, when],
                      me.at(me.z, k // 2, k % 2, me.core))

    send_products(0)

    for hi in range(2):
        for z in range(4):

            @pl.when(me.lo == 1)
            def _():
                landed(mid_z.at[hi, z], whole_y_recv.at[hi, z])

            start(mid_z.at[hi, z], homes.at[1 - me.hi, me.z, 2 + hi],
                  whole_pass_send.at[hi, z], home_recv.at[1 - me.hi, me.z, 2 + hi],
                  me.at(z, 1, me.hi, me.core), only=1)

    right_product()
    send_products(1)

    before, after, opposite = (me.x + 3) % 4, (me.x + 1) % 4, (me.x + 2) % 4
    relays = []
    for slot in range(2):
        landed(hits.at[slot, before], ring_recv.at[0, slot])
        relays.append(remote(hits.at[slot, before], hits.at[slot, before], relay_send.at[slot],
                             relay_recv.at[slot], me.right))
        relays[-1].start()

    halos = []
    parts = ((0, 4), (1, 2))
    for slot in range(2):
        for t in range(6):
            landed(homes.at[slot, t // 4, t % 4], home_recv.at[slot, t // 4, t % 4])
        for part, count in parts:
            halos.append(remote(
                homes.at[slot, part, pl.ds(0, count)], homes.at[slot, 4 + part, pl.ds(0, count)],
                field_send.at[slot, part], field_recv.at[slot, part], me.left,
            ))
            halos[-1].start()

    pass_on(0)

    for slot in range(2):
        landed(hits.at[slot, after], ring_recv.at[1, slot])
        landed(hits.at[slot, opposite], relay_recv.at[slot])
    for role in range(2):
        for c in range(2):

            @pl.loop(0, 16)
            def _(part):
                block = hits[role, part // 4, part % 4, :, c].reshape(BLK, BLK)
                left_t[role, pl.ds(c * BLK, BLK), tile(part)] = block.T

    @pl.loop(0, 16)
    def _(part):
        block = hits[0, part // 4, part % 4, :, 4].reshape(BLK, BLK)
        source[:, tile(part)] = block.T[:16]

    diagonal = jnp.logical_and(me.lo == 0, me.z == 0)

    @pl.loop(0, SPAN)
    def _(t):
        stamp = (me.x * SPAN + t).astype(f32)
        chosen = (source[:1, :].astype(f32) == stamp).astype(f32).astype(bf16)
        for slot in range(2):
            mate = jnp.where(diagonal, slot, 1 - slot)
            right = jnp.concatenate(
                [hits[mate, :, :, :, 2 + c].reshape(2048, BLK) for c in range(2)], axis=1
            )
            pieces = jnp.dot(left_t[slot] * chosen, right, preferred_element_type=f32)
            weights[slot, t, 0] = (pieces[:BLK, :BLK] - pieces[BLK:, BLK:]).astype(bf16)
            weights[slot, t, 1] = (pieces[:BLK, BLK:] + pieces[BLK:, :BLK]).astype(bf16)

    for slot in range(2):
        for t in range(6):
            landed(s_homes.at[slot, t // 4, t % 4], recv2.at[0, slot, t // 4, t % 4])
        for part, count in parts:
            halos.append(remote(
                s_homes.at[slot, part, pl.ds(0, count)],
                s_homes.at[slot, 4 + part, pl.ds(0, count)],
                halo_send.at[slot, part], halo_recv.at[slot, part], me.left,
            ))
            halos[-1].start()
    pass_on(1)

    for slot in range(2):
        for t in range(6, 16):
            landed(homes.at[slot, t // 4, t % 4], home_recv.at[slot, t // 4, t % 4])
        for part, count in parts:
            landed(homes.at[slot, 4 + part, pl.ds(0, count)], field_recv.at[slot, part])

    @pl.loop(0, SPAN)
    def _(t):
        totals = [[jnp.zeros((1, BLK), f32) for _ in range(4)] for _ in range(3)]
        for slot in range(2):
            mate = jnp.where(diagonal, slot, 1 - slot)
            p1 = [homes[slot, t // 4, t % 4, m1, c].astype(f32).T for c in range(2)]
            p4 = [homes[slot, t // 4, t % 4, m4, c].astype(f32).T for c in range(2)]
            for k in range(3):
                u = t + seps[k]
                p2 = [homes[mate, u // 4, u % 4, m2, c].astype(f32) for c in range(2)]
                p3 = [homes[mate, u // 4, u % 4, m3, c].astype(f32) for c in range(2)]
                new = pair_sums(p1, p2) + pair_sums(p4, p3)
                totals[k] = [a + b for a, b in zip(totals[k], new)]
        for k in range(3):
            box_sums[3 * t + k] = jnp.concatenate(totals[k], axis=0)

    for slot in range(2):
        for t in range(6, 16):
            landed(s_homes.at[slot, t // 4, t % 4], recv2.at[0, slot, t // 4, t % 4])
        for part, count in parts:
            landed(s_homes.at[slot, 4 + part, pl.ds(0, count)], halo_recv.at[slot, part])

    def product_sums_of(first, sums):
        @pl.loop(0, SPAN)
        def _(t):
            totals = [[jnp.zeros((1, BLK), f32) for _ in range(2)] for _ in range(3)]
            for slot in range(2):
                one = first(slot, t)
                for k in range(3):
                    u = t + seps[k]
                    two = [s_homes[slot, u // 4, u % 4, c].astype(f32) for c in range(2)]
                    totals[k] = [a + b for a, b in zip(totals[k], pair_sums(one, two))]
            for k in range(3):
                sums[3 * t + k] = jnp.concatenate(totals[k], axis=0)

    product_sums_of(lambda slot, t: [weights[slot, t, c].astype(f32) for c in range(2)], noise_sums)

    for slot in range(2):
        for t in range(16):
            landed(r_homes.at[slot, t // 4, t % 4], recv2.at[1, slot, t // 4, t % 4])
    product_sums_of(
        lambda slot, t: [r_homes[slot, t // 4, t % 4, c].astype(f32) for c in range(2)], cross_sums
    )

    sums = [(0, 4, box_sums), (4, 6, cross_sums), (6, 8, noise_sums)]
    for start_at, stop_at, values in sums:
        reduced = jnp.sum(values[...], axis=-1)
        for q in range(8):
            tiles[q, 0:6, start_at:stop_at] = reduced[6 * q:6 * q + 6]
    mine = 4 * (me.tm % 8) + me.mode
    for n in range(32):
        start(tiles.at[n // 4], gather.at[mine], sum_send.at[n], sum_recv.at[mine],
              (8 * me.x + n // 4, n % 4))
    for n in range(32):
        landed(gather.at[n], sum_recv.at[n])
    out[...] = jnp.sum(gather[...], axis=0)

    for copy in assembly + forwards + ring + relays + halos:
        copy.wait_send()
    for copy, only in sends:
        if only is None:
            sent(me, *copy)
        else:

            @pl.when(me.lo == only)
            def _():
                sent(me, *copy)


def params(ident):
    return pltpu.CompilerParams(
        vmem_limit_bytes=VMEM_LIMIT, collective_id=ident, has_side_effects=True
    )


def on_device(field_codes, scales, mom_index, separations, source_slice, noise_left, noise_right):
    mode = lax.axis_index("mode")
    bf16, f32 = jnp.bfloat16, jnp.float32
    dma = pltpu.SemaphoreType.DMA
    fields = (field_codes.astype(f32) * scales[:, :, None, :, None]).astype(bf16)
    fields = fields.transpose(1, 0, 2, 3, 4)
    mine = lax.dynamic_slice_in_dim(noise_left, mode * 256, 256, axis=2)
    noise = jnp.concatenate(
        [mine, noise_right, jnp.broadcast_to(source_slice.astype(bf16)[:, None, None], (64, 1, 256))],
        axis=1,
    )
    noise = noise.reshape(64, 5, 2, BLK).transpose(2, 1, 0, 3)

    any_spec = pl.BlockSpec(memory_space=ANY)
    smem = pl.BlockSpec(memory_space=pltpu.SMEM)
    vmem = pl.BlockSpec(memory_space=pltpu.VMEM)
    dims = lambda *shape: pltpu.VMEM(shape, bf16)
    total = pl.pallas_call(
        contract,
        out_shape=jax.ShapeDtypeStruct((8, BLK), f32),
        in_specs=[smem, smem, any_spec, any_spec],
        out_specs=vmem,
        scratch_shapes=[
            dims(2, 2, 1024, 1024),
            dims(2, 6, 4, 2, 2, BLK, BLK),
            dims(2, 4, 2, 2, BLK, BLK),
            dims(2, 4, 2, 2, BLK, BLK),
            dims(2, 4, 8, 2, BLK, BLK),
            dims(2, 2, 4, 4, 2, BLK, BLK),
            dims(2, 6, 4, 2, BLK, BLK),
            dims(2, 4, 4, 2, BLK, BLK),
            dims(4, 4, 5, 64, BLK),
            dims(2, 4, 4, 2, 5, 64, BLK),
            dims(2, 2 * BLK, 2048),
            dims(16, 2048),
            dims(2, SPAN, 2, BLK, BLK),
            pltpu.VMEM((3 * SPAN, 4, BLK), f32),
            pltpu.VMEM((3 * SPAN, 2, BLK), f32),
            pltpu.VMEM((3 * SPAN, 2, BLK), f32),
            pltpu.VMEM((8, 8, BLK), f32),
            pltpu.VMEM((32, 8, BLK), f32),
            dma((2,)), dma((2,)), dma((2,)), dma((2,)),
            dma((2, 2, 4)), dma((4, 4)), dma((4, 4)), dma((2, 4, 2)),
            dma((2, 2)), dma((2, 2)), dma((2,)), dma((2,)),
            dma((2, 2, 6)), dma((2, 4)), dma((2, 4)), dma((2, 4)),
            dma((4, 2)), dma((2, 4)), dma((2, 4)), dma((2, 4)), dma((2, 4, 4)),
            dma((2, 4, 2, 4)), dma((2, 2, 4, 4)), dma((2, 2, 4, 4)), dma((2, 2, 4, 4)),
            dma((2, 2)), dma((2, 2)), dma((2, 2)), dma((2, 2)),
            dma((32,)), dma((32,)),
        ],
        compiler_params=params(0),
        name="contract",
    )(mom_index, separations, fields, noise)
    mine = total[:6, :8].reshape(2, 3, 8)
    box = jnp.stack(
        [
            mine[..., 0] * mine[..., 2] - mine[..., 1] * mine[..., 3],
            mine[..., 0] * mine[..., 3] + mine[..., 1] * mine[..., 2],
        ],
        axis=-1,
    )
    return box, mine[..., 4:6], mine[..., 6:8]


def solution(mesh):
    in_specs = (
        P(None, "tm", None, "mode", None),
        P(None, "tm", "mode"),
        P(),
        P(),
        P("tm"),
        P("tm", None, None),
        P("tm", None, "mode"),
    )
    out_specs = (P("tm", None, None), P("tm", None, None), P("tm", None, None))
    return jax.shard_map(
        on_device, mesh=mesh, in_specs=in_specs, out_specs=out_specs, check_vma=False
    )
```

```python
import jax
import jax.numpy as jnp
from jax import lax
from jax.experimental import pallas as pl
from jax.experimental.pallas import tpu as pltpu
from jax.sharding import PartitionSpec as P

MESH = pl.DeviceIdType.MESH
ANY = pl.ANY
BLK = 128
SPAN = 16
VMEM_LIMIT = 56 * 1024 * 1024


def home(i, half, e, same):
    if same:
        if e == 0:
            unit, slot = i % 2, i // 2
        elif e == 1:
            unit, slot = 4 + i, 0
        elif e == 2:
            unit, slot = 2 + i % 2, i // 2
        else:
            unit, slot = 4 + (i + 3) % 4, 1
        return unit // 2, 0, half, unit % 2, slot, 4 * half + (i + e) % 4
    upper, lower = i + half * (e - i), e + half * (i - e)
    return upper, 1, (i + e) % 2, lower // 2, half, 4 * (1 - half) + e


def blocks_of(z, lo, hi, core):
    if z < 2:
        near = (core, core + 2)
    elif z == 2:
        near = (core, core + 1)
    else:
        near = (2 + core, (3 + core) % 4)
    far = (z, 4 + 2 * core + (hi + z) % 2)
    return tuple(4 * hi * (1 - lo) + n + lo * (f - n) for n, f in zip(near, far))


class Place:
    def __init__(self):
        self.tm = lax.axis_index("tm")
        self.mode = lax.axis_index("mode")
        self.x, self.z, self.lo = self.tm // 8, (self.tm // 2) % 4, self.tm % 2
        self.hi, self.core = self.mode // 2, self.mode % 2
        self.right = ((self.tm + 8) % 32, self.mode)
        self.left = ((self.tm + 24) % 32, self.mode)

    def at(self, z, lo, hi, core):
        return (8 * self.x + 2 * z + lo, 2 * hi + core)

    def is_here(self, device):
        return jnp.logical_and(device[0] == self.tm, device[1] == self.mode)


def greet(place):
    barrier = pltpu.get_barrier_semaphore()

    def signal(device):
        pl.semaphore_signal(barrier, inc=1, device_id=device, device_id_type=MESH)

    for n in range(32):
        device = (8 * place.x + n // 4, n % 4)

        @pl.when(jnp.logical_not(place.is_here(device)))
        def _():
            signal(device)

    signal(place.right)
    signal(place.left)
    pl.semaphore_wait(barrier, 33)


def remote(src, dst, send, recv, device):
    return pltpu.make_async_remote_copy(
        src_ref=src, dst_ref=dst, send_sem=send, recv_sem=recv,
        device_id=device, device_id_type=MESH,
    )


def send_or_keep(place, src, dst, send, recv, device):
    here = place.is_here(device)

    @pl.when(jnp.logical_not(here))
    def _():
        remote(src, dst, send, recv, device).start()

    @pl.when(here)
    def _():
        pltpu.make_async_copy(src, dst, recv).start()


def sent(place, src, dst, send, recv, device):
    @pl.when(jnp.logical_not(place.is_here(device)))
    def _():
        remote(src, dst, send, recv, device).wait_send()


def landed(ref, sem):
    pltpu.make_async_copy(ref, ref, sem).wait()


def pair_sums(one, two):
    real = one[0] * two[0] - one[1] * two[1]
    imag = one[0] * two[1] + one[1] * two[0]
    return [jnp.sum(value, axis=0, keepdims=True) for value in (real, imag)]


def contract(
    mom, seps, codes, scales, left, right, ids, out,
    fields, whole, homes, field_tail, mid_y, mid_z, products, mid, s_homes, s_tail, r_homes,
    mid_left, mid_right, mid_ids, hits_left, hits_right, hits_ids,
    left_t, source, weights, box_sums, cross_sums, noise_sums, tiles, gather,
    code_sem, asm_send, asm_recv, fwd_send, fwd_recv,
    left_send, left_z_send, left_z_recv, left_y_send, left_recv,
    id_send, id_z_send, id_z_recv, id_y_send, id_recv,
    right_z_send, right_z_recv, right_y_send, right_recv,
    ring_send, ring_recv, relay_send, relay_recv,
    near_send, cross_z_send, cross_z_recv, cross_y_send,
    whole_z_send, whole_y_send, whole_y_recv, whole_pass_send, home_recv,
    send1, recv1, send2, recv2,
    field_send, field_recv, halo_send, halo_recv, keep, sum_send, sum_recv,
):
    f32, bf16 = jnp.float32, jnp.bfloat16
    me = Place()
    loads = [pltpu.make_async_copy(codes.at[:, s], fields.at[:, s], code_sem.at[s])
             for s in range(2)]
    for copy in loads:
        copy.start()
    tiles[...] = jnp.zeros_like(tiles)
    greet(me)
    flip = me.tm + 1 - 2 * me.lo
    when = 2 * (1 - me.lo) + me.hi
    sends = []

    def start(*copy, only=None):
        sends.append((copy, only))
        if only is None:
            send_or_keep(me, *copy)
        else:

            @pl.when(me.lo == only)
            def _():
                send_or_keep(me, *copy)

    def landed_if(only, ref, sem):
        @pl.when(me.lo == only)
        def _():
            landed(ref, sem)

    def tile(n):
        return pl.ds(n * BLK if isinstance(n, int) else pl.multiple_of(n * BLK, BLK), BLK)

    def rows_of(block):
        return whole.at[:, :, pl.ds(pl.multiple_of(block * 256, 256), 256), :]

    for z in range(4):
        for slot in range(2):
            hi = me.hi + slot * (1 - 2 * me.hi)
            far = blocks_of(z, 1 - me.lo, hi, me.core)[slot]
            start(left.at[far], mid_left.at[slot, me.z], left_z_send.at[z, slot],
                  left_z_recv.at[slot, me.z], me.at(z, me.lo, me.hi, me.core))
        start(ids, mid_ids.at[me.z], id_z_send.at[z], id_z_recv.at[me.z],
              me.at(z, me.lo, me.hi, me.core))
    for a in range(2):
        for same in (False, True):
            for e in range(4):
                z, lo, hi, core, slot, col = home(2 * me.core + a, me.hi, e, same)
                group = slot if same else 2 + hi
                start(right.at[a], mid_right.at[group, me.z], right_z_send.at[a, int(same), e],
                      right_z_recv.at[group, me.z], me.at(z, me.lo, me.hi, core))

    assembly = []
    for s in range(2):
        loads[s].wait()
        for m in range(2):
            column = jnp.broadcast_to(scales[m, s:s + 1, :], (BLK, 256)).T

            @pl.loop(0, 8)
            def _(n):
                for c in range(2):
                    value = fields[m, s, c, :, tile(n)].astype(f32) * column
                    fields[m, s, c, :, tile(n)] = value.astype(bf16)

        assembly.append(remote(fields.at[:, s], rows_of(me.mode), asm_send.at[s],
                               asm_recv.at[me.hi], (flip, 2 * s + me.core)))
        assembly[-1].start()

    for a in range(2):
        row = 2 * me.core + a
        for e in range(4):
            z, _, hi, core, slot, col = home(row, me.hi, e, True)
            far = home(row, me.hi, e, False)

            def pick(one, two):
                return one + me.lo * (two - one)

            s, group = pick(1 - far[2], 1 - me.hi), pick(far[2], slot)
            start(fields.at[:, s, :, tile(a), tile(pick(far[5], col))], mid_y.at[group, me.z],
                  cross_z_send.at[a, e], cross_z_recv.at[group, me.z],
                  me.at(pick(far[0], z), me.lo, me.hi, pick(far[3], core)))
        for s in range(2):
            for e in range(4):
                z, _, hi, core, slot, col = home(row, me.hi, e, True)
                start(fields.at[:, s, :, tile(a), tile(col)], homes.at[slot, 4 * me.z + s],
                      near_send.at[s, a, e], home_recv.at[slot, 4 * me.z + s],
                      me.at(z, 0, me.hi, core), only=0)
            for b in range(2):
                other = 2 * b + (me.hi + a) % 2
                z, _, hi, core, slot, col = home(row, me.hi, other, False)
                start(fields.at[:, s, :, tile(a), tile(col)], homes.at[slot, 4 * me.z + 2 + s],
                      near_send.at[s, a, 4 + b], home_recv.at[slot, 4 * me.z + 2 + s],
                      me.at(z, 1, me.hi, core), only=1)

    for z in range(4):
        for slot in range(2):
            hi = me.hi + slot * (1 - 2 * me.hi)
            landed(mid_left.at[slot, z], left_z_recv.at[slot, z])
            start(mid_left.at[slot, z], hits_left.at[slot, me.x, z, me.lo],
                  left_y_send.at[slot, z], left_recv.at[slot, z, me.lo],
                  me.at(me.z, 1 - me.lo, hi, me.core))
        landed(mid_ids.at[z], id_z_recv.at[z])
        start(mid_ids.at[z], hits_ids.at[me.x, z, me.lo], id_y_send.at[z],
              id_recv.at[z, me.lo], me.at(me.z, 1 - me.lo, me.hi, me.core))
        for group in range(4):
            if group < 2:
                slot, device = group, me.at(me.z, 0, me.hi, me.core)
            else:
                slot, device = me.hi, me.at(me.z, 1, group - 2, me.core)
            landed(mid_right.at[group, z], right_z_recv.at[group, z])
            start(mid_right.at[group, z], hits_right.at[slot, me.x, z, me.lo],
                  right_y_send.at[group, z], right_recv.at[slot, z, me.lo], device)
        for slot in range(2):
            near = blocks_of(z, me.lo, me.hi, me.core)[slot]
            start(left.at[near], hits_left.at[slot, me.x, me.z, me.lo], left_send.at[z, slot],
                  left_recv.at[slot, me.z, me.lo], me.at(z, me.lo, me.hi, me.core))
        start(ids, hits_ids.at[me.x, me.z, me.lo], id_send.at[z], id_recv.at[me.z, me.lo],
              me.at(z, me.lo, me.hi, me.core))

    ring = []

    def start_ring():
        for z in range(4):
            for lo in range(2):
                for slot in range(2):
                    landed(hits_left.at[slot, me.x, z, lo], left_recv.at[slot, z, lo])
                    landed(hits_right.at[slot, me.x, z, lo], right_recv.at[slot, z, lo])
                landed(hits_ids.at[me.x, z, lo], id_recv.at[z, lo])
        own = [hits_left.at[:, me.x], hits_right.at[:, me.x], hits_ids.at[me.x]]
        for n, ref in enumerate(own):
            ring.append(remote(ref, ref, ring_send.at[0, n], ring_recv.at[0, n], me.right))
        for n, ref in enumerate(own):
            ring.append(remote(ref, ref, ring_send.at[1, n], ring_recv.at[1, n], me.left))
        for copy in ring:
            copy.start()

    before, after, opposite = (me.x + 3) % 4, (me.x + 1) % 4, (me.x + 2) % 4
    relays = []

    def relay():
        held = [hits_left.at[:, before], hits_right.at[:, before], hits_ids.at[before]]
        for n, ref in enumerate(held):
            landed(ref, ring_recv.at[0, n])
            relays.append(remote(ref, ref, relay_send.at[n], relay_recv.at[n], me.right))
            relays[-1].start()

    start_ring()

    forwards = []
    for h in range(2):
        block = rows_of(2 * h + me.core)
        landed(block, asm_recv.at[h])
        forwards.append(remote(block, block, fwd_send.at[h], fwd_recv.at[h],
                               (me.tm, me.mode + 1 - 2 * me.core)))
        forwards[-1].start()

    for z in range(4):
        for group in range(2):
            landed(mid_y.at[group, z], cross_z_recv.at[group, z])
            lo, hi = 1 - me.lo, group + me.lo * (me.hi - group)
            slot = me.hi + me.lo * (group - me.hi)
            t = 4 * z + 2 * me.lo + (1 - group) + me.lo * (group - me.hi)
            start(mid_y.at[group, z], homes.at[slot, t], cross_y_send.at[group, z],
                  home_recv.at[slot, t], me.at(me.z, lo, hi, me.core))

    def serve(only, slot, t):
        landed_if(only, homes.at[slot, t], home_recv.at[slot, t])
        start(homes.at[slot, t], field_tail.at[slot, 6 + t], field_send.at[slot, t],
              field_recv.at[slot, t], me.left, only=only)

    for t in (0, 1, 4, 5):
        for slot in range(2):
            serve(0, slot, t)
    for t in (2, 3):
        serve(1, me.hi, t)

    for h in range(2):
        landed(rows_of(2 * h + 1 - me.core), fwd_recv.at[h])
    for hi in range(2):
        for z in range(4):
            pair = blocks_of(z, 1, hi, me.core)
            row, col = pair[1 - hi], pair[hi]
            start(whole.at[:, :, tile(row), tile(col)], mid_z.at[me.hi, z],
                  whole_y_send.at[hi, z], whole_y_recv.at[me.hi, z],
                  me.at(me.z, 1, hi, me.core), only=0)
    for z in range(4):
        pair = blocks_of(z, me.lo, me.hi, me.core)
        for slot in range(2):
            row, col = pair[slot], pair[1 - slot]
            if z == 0:
                col = col + (1 - me.lo) * (row - col)
            start(whole.at[:, :, tile(row), tile(col)], homes.at[slot, 4 * me.z + when],
                  whole_z_send.at[z, slot], home_recv.at[slot, 4 * me.z + when],
                  me.at(z, me.lo, me.hi, me.core))

    base = pl.multiple_of(me.core * 512, 512)
    m1, m2, m3, m4 = (mom[i] for i in range(4))

    def cdot(ar, ai, br, bi):
        def dot(a, b):
            return jnp.dot(a, b, preferred_element_type=f32)

        return dot(ar, br) - dot(ai, bi), dot(ar, bi) + dot(ai, br)

    def product_s():
        @pl.loop(0, 4)
        def _(pair):
            cols = pl.ds(pl.multiple_of(pair * 256, 256), 256)
            rows = pl.ds(base, 512)
            parts = cdot(whole[m2, 0, rows, :], whole[m2, 1, rows, :],
                         whole[m3, 0, :, cols], whole[m3, 1, :, cols])
            for c in range(2):
                for a in range(4):
                    for b in range(2):
                        piece = parts[c][a * BLK:(a + 1) * BLK, b * BLK:(b + 1) * BLK]
                        products[0, a, 2 * pair + b, c] = piece.astype(bf16)

    def product_r():
        @pl.loop(0, 4)
        def _(step):
            pair, half = step // 2, step % 2
            cols = pl.ds(pl.multiple_of(base + pair * 256, 256), 256)
            rows = pl.ds(pl.multiple_of(half * 512, 512), 512)
            parts = cdot(whole[m4, 0, rows, :], whole[m4, 1, rows, :],
                         whole[m1, 0, :, cols], whole[m1, 1, :, cols])
            for c in range(2):
                for a in range(2):
                    for b in range(4):
                        piece = parts[c][b * BLK:(b + 1) * BLK, a * BLK:(a + 1) * BLK]
                        products[1, 2 * pair + a, 4 * half + b, c] = piece.T.astype(bf16)

    def send_products(p):
        for i in range(4):
            for same in (False, True):
                for e in range(4):
                    z, lo, hi, core, slot, col = home(i, me.core, e, same)

                    def either(one, two):
                        return one + slot * (two - one)

                    device = me.at(either(me.z, z), either(lo, me.lo), either(hi, me.hi), core)
                    at = (p, slot, either(z, 2 * lo + hi), either(when, me.z))
                    start(products.at[p, i, col], mid.at[at], send1.at[p, i, int(same), e],
                          recv1.at[at], device)

    def pass_on(p):
        ref = (s_homes, r_homes)[p]
        for j in range(4):
            for k in range(4):
                landed(mid.at[p, 0, k, j], recv1.at[p, 0, k, j])
                start(mid.at[p, 0, k, j], ref.at[0, 4 * me.z + j],
                      send2.at[p, 0, k, j], recv2.at[p, 0, 4 * me.z + j],
                      me.at(k, me.lo, me.hi, me.core))
                landed(mid.at[p, 1, k, j], recv1.at[p, 1, k, j])
                start(mid.at[p, 1, k, j], ref.at[1, 4 * j + when],
                      send2.at[p, 1, k, j], recv2.at[p, 1, 4 * j + when],
                      me.at(me.z, k // 2, k % 2, me.core))

    def pass_fields():
        for hi in range(2):
            for z in range(4):
                landed_if(1, mid_z.at[hi, z], whole_y_recv.at[hi, z])
                start(mid_z.at[hi, z], homes.at[1 - me.hi, 4 * me.z + 2 + hi],
                      whole_pass_send.at[hi, z], home_recv.at[1 - me.hi, 4 * me.z + 2 + hi],
                      me.at(z, 1, me.hi, me.core), only=1)

    def serve_rest():
        for t in (2, 3):
            for slot in range(2):
                serve(0, slot, t)
        for t in (0, 1, 4, 5):
            serve(1, me.hi, t)
        for t in range(6):
            serve(1, 1 - me.hi, t)

    kept = []

    def fields_here():
        for slot in range(2):
            for t in range(6, 16):
                landed(homes.at[slot, t], home_recv.at[slot, t])
            kept.append(pltpu.make_async_copy(
                homes.at[slot, pl.ds(10, 6)], field_tail.at[slot, pl.ds(0, 6)], keep.at[0, slot]))
            kept[-1].start()

    def serve_products():
        for slot in range(2):
            for t in range(6):
                landed(s_homes.at[slot, t], recv2.at[0, slot, t])
                start(s_homes.at[slot, t], s_tail.at[slot, 6 + t], halo_send.at[slot, t],
                      halo_recv.at[slot, t], me.left)

    def products_here():
        for slot in range(2):
            for t in range(6, 16):
                landed(s_homes.at[slot, t], recv2.at[0, slot, t])
            kept.append(pltpu.make_async_copy(
                s_homes.at[slot, pl.ds(10, 6)], s_tail.at[slot, pl.ds(0, 6)], keep.at[1, slot]))
            kept[-1].start()

    def left_vectors():
        for role in range(2):
            for c in range(2):

                @pl.loop(0, 16)
                def _(part):
                    block = hits_left[role, part // 4, part % 4, :, c].reshape(BLK, BLK)
                    left_t[role, pl.ds(c * BLK, BLK), tile(part)] = block.T

        lanes = lax.broadcasted_iota(jnp.int32, (16, BLK), 1)

        @pl.loop(0, 16)
        def _(part):
            one, two = (hits_ids[part // 4, part % 4, lo].astype(f32) for lo in range(2))
            source[:, tile(part)] = jnp.where(lanes < 64, one, two)

    diagonal = jnp.logical_and(me.lo == 0, me.z == 0)

    def all_weights():
        @pl.loop(0, SPAN)
        def _(t):
            stamp = (me.x * SPAN + t).astype(f32)
            chosen = (source[:1, :] == stamp).astype(f32).astype(bf16)
            for slot in range(2):
                mate = jnp.where(diagonal, slot, 1 - slot)
                vectors = jnp.concatenate(
                    [hits_right[mate, :, :, :, c].reshape(2048, BLK) for c in range(2)], axis=1
                )
                pieces = jnp.dot(left_t[slot] * chosen, vectors, preferred_element_type=f32)
                weights[slot, t, 0] = (pieces[:BLK, :BLK] - pieces[BLK:, BLK:]).astype(bf16)
                weights[slot, t, 1] = (pieces[:BLK, BLK:] + pieces[BLK:, :BLK]).astype(bf16)

    def box(begin, end, later, shift):
        @pl.loop(begin, end)
        def _(t):
            totals = [[jnp.zeros((1, BLK), f32) for _ in range(4)] for _ in range(3)]
            for slot in range(2):
                mate = jnp.where(diagonal, slot, 1 - slot)
                p1 = [homes[slot, t, m1, c].astype(f32).T for c in range(2)]
                p4 = [homes[slot, t, m4, c].astype(f32).T for c in range(2)]
                for k in range(3):
                    u = t + seps[k] - shift
                    p2 = [later[mate, u, m2, c].astype(f32) for c in range(2)]
                    p3 = [later[mate, u, m3, c].astype(f32) for c in range(2)]
                    new = pair_sums(p1, p2) + pair_sums(p4, p3)
                    totals[k] = [a + b for a, b in zip(totals[k], new)]
            for k in range(3):
                box_sums[3 * t + k] = jnp.concatenate(totals[k], axis=0)

    def product_sums(begin, end, later, shift, first, sums):
        @pl.loop(begin, end)
        def _(t):
            totals = [[jnp.zeros((1, BLK), f32) for _ in range(2)] for _ in range(3)]
            for slot in range(2):
                one = [first[slot, t, c].astype(f32) for c in range(2)]
                for k in range(3):
                    u = t + seps[k] - shift
                    two = [later[slot, u, c].astype(f32) for c in range(2)]
                    totals[k] = [a + b for a, b in zip(totals[k], pair_sums(one, two))]
            for k in range(3):
                sums[3 * t + k] = jnp.concatenate(totals[k], axis=0)

    def to_tiles(begin, end, sums):
        reduced = jnp.sum(sums[...], axis=-1)
        for q in range(8):
            tiles[q, 0:6, begin:end] = reduced[6 * q:6 * q + 6]

    product_s()
    send_products(0)
    product_r()
    pass_fields()
    relay()
    serve_rest()
    pass_on(0)
    send_products(1)
    fields_here()
    box(0, 10, homes, 0)
    ring_refs = [hits_left.at[:, after], hits_right.at[:, after], hits_ids.at[after]]
    relay_refs = [hits_left.at[:, opposite], hits_right.at[:, opposite], hits_ids.at[opposite]]
    for n in range(3):
        landed(ring_refs[n], ring_recv.at[1, n])
        landed(relay_refs[n], relay_recv.at[n])
    left_vectors()
    serve_products()
    pass_on(1)
    all_weights()
    for copy in kept:
        copy.wait()
    for slot in range(2):
        for t in range(6):
            landed(field_tail.at[slot, 6 + t], field_recv.at[slot, t])
    box(10, 16, field_tail, 10)
    to_tiles(0, 4, box_sums)
    products_here()
    product_sums(0, 10, s_homes, 0, weights, noise_sums)
    for copy in kept[2:]:
        copy.wait()
    for slot in range(2):
        for t in range(6):
            landed(s_tail.at[slot, 6 + t], halo_recv.at[slot, t])
    product_sums(10, 16, s_tail, 10, weights, noise_sums)
    to_tiles(6, 8, noise_sums)
    for slot in range(2):
        for t in range(16):
            landed(r_homes.at[slot, t], recv2.at[1, slot, t])
    product_sums(0, 10, s_homes, 0, r_homes, cross_sums)
    product_sums(10, 16, s_tail, 10, r_homes, cross_sums)
    to_tiles(4, 6, cross_sums)

    mine = 4 * (me.tm % 8) + me.mode
    for n in range(32):
        start(tiles.at[n // 4], gather.at[mine], sum_send.at[n], sum_recv.at[mine],
              (8 * me.x + n // 4, n % 4))
    for n in range(32):
        landed(gather.at[n], sum_recv.at[n])
    out[...] = jnp.sum(gather[...], axis=0)

    for copy in assembly + forwards + ring + relays:
        copy.wait_send()
    for copy, only in sends:
        if only is None:
            sent(me, *copy)
        else:

            @pl.when(me.lo == only)
            def _():
                sent(me, *copy)


def params(ident):
    return pltpu.CompilerParams(
        vmem_limit_bytes=VMEM_LIMIT, collective_id=ident, has_side_effects=True
    )


def on_device(field_codes, scales, mom_index, separations, source_slice, noise_left, noise_right):
    bf16, f32 = jnp.bfloat16, jnp.float32
    dma = pltpu.SemaphoreType.DMA
    blocks = noise_left.reshape(64, 2, 8, BLK).transpose(2, 1, 0, 3)
    own_blocks = noise_right.reshape(64, 2, 2, BLK).transpose(2, 1, 0, 3)
    ids = jnp.broadcast_to(jnp.tile(source_slice.astype(bf16), 2), (16, BLK))

    any_spec = pl.BlockSpec(memory_space=ANY)
    smem = pl.BlockSpec(memory_space=pltpu.SMEM)
    vmem = pl.BlockSpec(memory_space=pltpu.VMEM)
    dims = lambda *shape: pltpu.VMEM(shape, bf16)
    total = pl.pallas_call(
        contract,
        out_shape=jax.ShapeDtypeStruct((8, BLK), f32),
        in_specs=[smem, smem, any_spec, vmem, any_spec, any_spec, any_spec],
        out_specs=vmem,
        scratch_shapes=[
            dims(2, 2, 2, 256, 1024),
            dims(2, 2, 1024, 1024),
            dims(2, 16, 2, 2, BLK, BLK),
            dims(2, 12, 2, 2, BLK, BLK),
            dims(2, 4, 2, 2, BLK, BLK),
            dims(2, 4, 2, 2, BLK, BLK),
            dims(2, 4, 8, 2, BLK, BLK),
            dims(2, 2, 4, 4, 2, BLK, BLK),
            dims(2, 16, 2, BLK, BLK),
            dims(2, 12, 2, BLK, BLK),
            dims(2, 16, 2, BLK, BLK),
            dims(2, 4, 2, 64, BLK),
            dims(4, 4, 2, 64, BLK),
            dims(4, 16, BLK),
            dims(2, 4, 4, 2, 2, 64, BLK),
            dims(2, 4, 4, 2, 2, 64, BLK),
            dims(4, 4, 2, 16, BLK),
            dims(2, 2 * BLK, 2048),
            pltpu.VMEM((16, 2048), f32),
            dims(2, SPAN, 2, BLK, BLK),
            pltpu.VMEM((3 * SPAN, 4, BLK), f32),
            pltpu.VMEM((3 * SPAN, 2, BLK), f32),
            pltpu.VMEM((3 * SPAN, 2, BLK), f32),
            pltpu.VMEM((8, 8, BLK), f32),
            pltpu.VMEM((32, 8, BLK), f32),
            dma((2,)), dma((2,)), dma((2,)), dma((2,)), dma((2,)),
            dma((4, 2)), dma((4, 2)), dma((2, 4)), dma((2, 4)), dma((2, 4, 2)),
            dma((4,)), dma((4,)), dma((4,)), dma((4,)), dma((4, 2)),
            dma((2, 2, 4)), dma((4, 4)), dma((4, 4)), dma((2, 4, 2)),
            dma((2, 3)), dma((2, 3)), dma((3,)), dma((3,)),
            dma((2, 2, 6)), dma((2, 4)), dma((2, 4)), dma((2, 4)),
            dma((4, 2)), dma((2, 4)), dma((2, 4)), dma((2, 4)), dma((2, 16)),
            dma((2, 4, 2, 4)), dma((2, 2, 4, 4)), dma((2, 2, 4, 4)), dma((2, 2, 16)),
            dma((2, 6)), dma((2, 6)), dma((2, 6)), dma((2, 6)), dma((2, 2)),
            dma((32,)), dma((32,)),
        ],
        compiler_params=params(0),
        name="contract",
    )(mom_index, separations, field_codes, scales, blocks, own_blocks, ids)
    mine = total[:6, :8].reshape(2, 3, 8)
    box = jnp.stack(
        [
            mine[..., 0] * mine[..., 2] - mine[..., 1] * mine[..., 3],
            mine[..., 0] * mine[..., 3] + mine[..., 1] * mine[..., 2],
        ],
        axis=-1,
    )
    return box, mine[..., 4:6], mine[..., 6:8]


def solution(mesh):
    in_specs = (
        P(None, "tm", None, "mode", None),
        P(None, "tm", "mode"),
        P(),
        P(),
        P("tm"),
        P("tm", None, None),
        P("tm", None, "mode"),
    )
    out_specs = (P("tm", None, None), P("tm", None, None), P("tm", None, None))
    return jax.shard_map(
        on_device, mesh=mesh, in_specs=in_specs, out_specs=out_specs, check_vma=False
    )
```

```python
import jax
import jax.numpy as jnp
from jax import lax
from jax.experimental import pallas as pl
from jax.experimental.pallas import tpu as pltpu
from jax.sharding import PartitionSpec as P

MESH = pl.DeviceIdType.MESH
ANY = pl.ANY
BLK = 128
SPAN = 16
VMEM_LIMIT = 56 * 1024 * 1024


def home(i, half, e, same):
    if same:
        if e == 0:
            unit, slot = i % 2, i // 2
        elif e == 1:
            unit, slot = 4 + i, 0
        elif e == 2:
            unit, slot = 2 + i % 2, i // 2
        else:
            unit, slot = 4 + (i + 3) % 4, 1
        return unit // 2, 0, half, unit % 2, slot, 4 * half + (i + e) % 4
    upper, lower = i + half * (e - i), e + half * (i - e)
    return upper, 1, (i + e) % 2, lower // 2, half, 4 * (1 - half) + e


def blocks_of(z, lo, hi, core):
    if z < 2:
        near = (core, core + 2)
    elif z == 2:
        near = (core, core + 1)
    else:
        near = (2 + core, (3 + core) % 4)
    far = (z, 4 + 2 * core + (hi + z) % 2)
    return tuple(4 * hi * (1 - lo) + n + lo * (f - n) for n, f in zip(near, far))


class Place:
    def __init__(self):
        self.tm = lax.axis_index("tm")
        self.mode = lax.axis_index("mode")
        self.x, self.z, self.lo = self.tm // 8, (self.tm // 2) % 4, self.tm % 2
        self.hi, self.core = self.mode // 2, self.mode % 2
        self.right = ((self.tm + 8) % 32, self.mode)
        self.left = ((self.tm + 24) % 32, self.mode)

    def at(self, z, lo, hi, core):
        return (8 * self.x + 2 * z + lo, 2 * hi + core)

    def is_here(self, device):
        return jnp.logical_and(device[0] == self.tm, device[1] == self.mode)


def greet(place):
    barrier = pltpu.get_barrier_semaphore()

    def signal(device):
        pl.semaphore_signal(barrier, inc=1, device_id=device, device_id_type=MESH)

    for n in range(32):
        device = (8 * place.x + n // 4, n % 4)

        @pl.when(jnp.logical_not(place.is_here(device)))
        def _():
            signal(device)

    signal(place.right)
    signal(place.left)
    pl.semaphore_wait(barrier, 33)


def remote(src, dst, send, recv, device):
    return pltpu.make_async_remote_copy(
        src_ref=src, dst_ref=dst, send_sem=send, recv_sem=recv,
        device_id=device, device_id_type=MESH,
    )


def send_or_keep(place, src, dst, send, recv, device):
    here = place.is_here(device)

    @pl.when(jnp.logical_not(here))
    def _():
        remote(src, dst, send, recv, device).start()

    @pl.when(here)
    def _():
        pltpu.make_async_copy(src, dst, recv).start()


def sent(place, src, dst, send, recv, device):
    @pl.when(jnp.logical_not(place.is_here(device)))
    def _():
        remote(src, dst, send, recv, device).wait_send()


def landed(ref, sem):
    pltpu.make_async_copy(ref, ref, sem).wait()


def pair_sums(one, two):
    real = one[0] * two[0] - one[1] * two[1]
    imag = one[0] * two[1] + one[1] * two[0]
    return [jnp.sum(value, axis=0, keepdims=True) for value in (real, imag)]


def contract(
    mom, seps, codes, scales, left, right, ids, out,
    fields, whole, homes, field_tail, mid_y, mid_z, products, mid, s_homes, s_tail, r_homes,
    mid_left, mid_right, mid_ids, hits_left, hits_right, hits_ids,
    left_t, source, weights, box_sums, cross_sums, noise_sums, tiles, gather,
    code_sem, asm_send, asm_recv, fwd_send, fwd_recv,
    left_send, left_z_send, left_z_recv, left_y_send, left_recv,
    id_send, id_z_send, id_z_recv, id_y_send, id_recv,
    right_z_send, right_z_recv, right_y_send, right_recv,
    ring_send, ring_recv, relay_send, relay_recv,
    near_send, cross_z_send, cross_z_recv, cross_y_send,
    whole_z_send, whole_y_send, whole_y_recv, whole_pass_send, home_recv,
    send1, recv1, send2, recv2,
    field_send, field_recv, halo_send, halo_recv, keep, sum_send, sum_recv,
):
    f32, bf16 = jnp.float32, jnp.bfloat16
    me = Place()
    loads = [pltpu.make_async_copy(codes.at[:, s], fields.at[:, s], code_sem.at[s])
             for s in range(2)]
    for copy in loads:
        copy.start()
    tiles[...] = jnp.zeros_like(tiles)
    greet(me)
    flip = me.tm + 1 - 2 * me.lo
    when = 2 * (1 - me.lo) + me.hi
    sends = []

    def start(*copy, only=None):
        sends.append((copy, only))
        if only is None:
            send_or_keep(me, *copy)
        else:

            @pl.when(me.lo == only)
            def _():
                send_or_keep(me, *copy)

    def all_sent():
        for copy, only in sends:
            if only is None:
                sent(me, *copy)
            else:

                @pl.when(me.lo == only)
                def _():
                    sent(me, *copy)

        sends.clear()

    def landed_if(only, ref, sem):
        @pl.when(me.lo == only)
        def _():
            landed(ref, sem)

    def tile(n):
        return pl.ds(n * BLK if isinstance(n, int) else pl.multiple_of(n * BLK, BLK), BLK)

    def rows_of(block):
        return whole.at[:, :, pl.ds(pl.multiple_of(block * 256, 256), 256), :]

    for z in range(4):
        for slot in range(2):
            hi = me.hi + slot * (1 - 2 * me.hi)
            far = blocks_of(z, 1 - me.lo, hi, me.core)[slot]
            start(left.at[far], mid_left.at[slot, me.z], left_z_send.at[z, slot],
                  left_z_recv.at[slot, me.z], me.at(z, me.lo, me.hi, me.core))
        start(ids, mid_ids.at[me.z], id_z_send.at[z], id_z_recv.at[me.z],
              me.at(z, me.lo, me.hi, me.core))
    for a in range(2):
        for same in (False, True):
            for e in range(4):
                z, lo, hi, core, slot, col = home(2 * me.core + a, me.hi, e, same)
                group = slot if same else 2 + hi
                start(right.at[a], mid_right.at[group, me.z], right_z_send.at[a, int(same), e],
                      right_z_recv.at[group, me.z], me.at(z, me.lo, me.hi, core))

    assembly = []
    for s in range(2):
        loads[s].wait()
        for m in range(2):
            column = jnp.broadcast_to(scales[m, s:s + 1, :], (BLK, 256)).T

            @pl.loop(0, 8)
            def _(n):
                for c in range(2):
                    value = fields[m, s, c, :, tile(n)].astype(f32) * column
                    fields[m, s, c, :, tile(n)] = value.astype(bf16)

        assembly.append(remote(fields.at[:, s], rows_of(me.mode), asm_send.at[s],
                               asm_recv.at[me.hi], (flip, 2 * s + me.core)))
        assembly[-1].start()

    for a in range(2):
        row = 2 * me.core + a
        for e in range(4):
            z, _, hi, core, slot, col = home(row, me.hi, e, True)
            far = home(row, me.hi, e, False)

            def pick(one, two):
                return one + me.lo * (two - one)

            s, group = pick(1 - far[2], 1 - me.hi), pick(far[2], slot)
            start(fields.at[:, s, :, tile(a), tile(pick(far[5], col))], mid_y.at[group, me.z],
                  cross_z_send.at[a, e], cross_z_recv.at[group, me.z],
                  me.at(pick(far[0], z), me.lo, me.hi, pick(far[3], core)))
        for s in range(2):
            for e in range(4):
                z, _, hi, core, slot, col = home(row, me.hi, e, True)
                start(fields.at[:, s, :, tile(a), tile(col)], homes.at[slot, 4 * me.z + s],
                      near_send.at[s, a, e], home_recv.at[slot, 4 * me.z + s],
                      me.at(z, 0, me.hi, core), only=0)
            for b in range(2):
                other = 2 * b + (me.hi + a) % 2
                z, _, hi, core, slot, col = home(row, me.hi, other, False)
                start(fields.at[:, s, :, tile(a), tile(col)], homes.at[slot, 4 * me.z + 2 + s],
                      near_send.at[s, a, 4 + b], home_recv.at[slot, 4 * me.z + 2 + s],
                      me.at(z, 1, me.hi, core), only=1)

    for z in range(4):
        for slot in range(2):
            hi = me.hi + slot * (1 - 2 * me.hi)
            landed(mid_left.at[slot, z], left_z_recv.at[slot, z])
            start(mid_left.at[slot, z], hits_left.at[slot, me.x, z, me.lo],
                  left_y_send.at[slot, z], left_recv.at[slot, z, me.lo],
                  me.at(me.z, 1 - me.lo, hi, me.core))
        landed(mid_ids.at[z], id_z_recv.at[z])
        start(mid_ids.at[z], hits_ids.at[me.x, z, me.lo], id_y_send.at[z],
              id_recv.at[z, me.lo], me.at(me.z, 1 - me.lo, me.hi, me.core))
        for group in range(4):
            if group < 2:
                slot, device = group, me.at(me.z, 0, me.hi, me.core)
            else:
                slot, device = me.hi, me.at(me.z, 1, group - 2, me.core)
            landed(mid_right.at[group, z], right_z_recv.at[group, z])
            start(mid_right.at[group, z], hits_right.at[slot, me.x, z, me.lo],
                  right_y_send.at[group, z], right_recv.at[slot, z, me.lo], device)
        for slot in range(2):
            near = blocks_of(z, me.lo, me.hi, me.core)[slot]
            start(left.at[near], hits_left.at[slot, me.x, me.z, me.lo], left_send.at[z, slot],
                  left_recv.at[slot, me.z, me.lo], me.at(z, me.lo, me.hi, me.core))
        start(ids, hits_ids.at[me.x, me.z, me.lo], id_send.at[z], id_recv.at[me.z, me.lo],
              me.at(z, me.lo, me.hi, me.core))

    ring = []

    def start_ring():
        for z in range(4):
            for lo in range(2):
                for slot in range(2):
                    landed(hits_left.at[slot, me.x, z, lo], left_recv.at[slot, z, lo])
                    landed(hits_right.at[slot, me.x, z, lo], right_recv.at[slot, z, lo])
                landed(hits_ids.at[me.x, z, lo], id_recv.at[z, lo])
        own = [hits_left.at[:, me.x], hits_right.at[:, me.x], hits_ids.at[me.x]]
        for n, ref in enumerate(own):
            ring.append(remote(ref, ref, ring_send.at[0, n], ring_recv.at[0, n], me.right))
        for n, ref in enumerate(own):
            ring.append(remote(ref, ref, ring_send.at[1, n], ring_recv.at[1, n], me.left))
        for copy in ring:
            copy.start()

    before, after, opposite = (me.x + 3) % 4, (me.x + 1) % 4, (me.x + 2) % 4
    relays = []

    def relay():
        held = [hits_left.at[:, before], hits_right.at[:, before], hits_ids.at[before]]
        for n, ref in enumerate(held):
            landed(ref, ring_recv.at[0, n])
            relays.append(remote(ref, ref, relay_send.at[n], relay_recv.at[n], me.right))
            relays[-1].start()

    forwards = []
    for h in range(2):
        block = rows_of(2 * h + me.core)
        landed(block, asm_recv.at[h])
        forwards.append(remote(block, block, fwd_send.at[h], fwd_recv.at[h],
                               (me.tm, me.mode + 1 - 2 * me.core)))
        forwards[-1].start()

    for z in range(4):
        for group in range(2):
            landed(mid_y.at[group, z], cross_z_recv.at[group, z])
            lo, hi = 1 - me.lo, group + me.lo * (me.hi - group)
            slot = me.hi + me.lo * (group - me.hi)
            t = 4 * z + 2 * me.lo + (1 - group) + me.lo * (group - me.hi)
            start(mid_y.at[group, z], homes.at[slot, t], cross_y_send.at[group, z],
                  home_recv.at[slot, t], me.at(me.z, lo, hi, me.core))

    start_ring()

    def serve(only, slot, t):
        landed_if(only, homes.at[slot, t], home_recv.at[slot, t])
        start(homes.at[slot, t], field_tail.at[slot, 6 + t], field_send.at[slot, t],
              field_recv.at[slot, t], me.left, only=only)

    for t in (0, 1, 4, 5):
        for slot in range(2):
            serve(0, slot, t)
    for t in (2, 3):
        serve(1, me.hi, t)

    for h in range(2):
        landed(rows_of(2 * h + 1 - me.core), fwd_recv.at[h])
    for hi in range(2):
        for z in range(4):
            pair = blocks_of(z, 1, hi, me.core)
            row, col = pair[1 - hi], pair[hi]
            start(whole.at[:, :, tile(row), tile(col)], mid_z.at[me.hi, z],
                  whole_y_send.at[hi, z], whole_y_recv.at[me.hi, z],
                  me.at(me.z, 1, hi, me.core), only=0)
    for z in range(4):
        pair = blocks_of(z, me.lo, me.hi, me.core)
        for slot in range(2):
            row, col = pair[slot], pair[1 - slot]
            if z == 0:
                col = col + (1 - me.lo) * (row - col)
            start(whole.at[:, :, tile(row), tile(col)], homes.at[slot, 4 * me.z + when],
                  whole_z_send.at[z, slot], home_recv.at[slot, 4 * me.z + when],
                  me.at(z, me.lo, me.hi, me.core))

    base = pl.multiple_of(me.core * 512, 512)
    m1, m2, m3, m4 = (mom[i] for i in range(4))

    def cdot(ar, ai, br, bi):
        def dot(a, b):
            return jnp.dot(a, b, preferred_element_type=f32)

        return dot(ar, br) - dot(ai, bi), dot(ar, bi) + dot(ai, br)

    def product_s():
        @pl.loop(0, 4)
        def _(pair):
            cols = pl.ds(pl.multiple_of(pair * 256, 256), 256)
            rows = pl.ds(base, 512)
            parts = cdot(whole[m2, 0, rows, :], whole[m2, 1, rows, :],
                         whole[m3, 0, :, cols], whole[m3, 1, :, cols])
            for c in range(2):
                for a in range(4):
                    for b in range(2):
                        piece = parts[c][a * BLK:(a + 1) * BLK, b * BLK:(b + 1) * BLK]
                        products[0, a, 2 * pair + b, c] = piece.astype(bf16)

    def product_r():
        @pl.loop(0, 4)
        def _(step):
            pair, half = step // 2, step % 2
            cols = pl.ds(pl.multiple_of(base + pair * 256, 256), 256)
            rows = pl.ds(pl.multiple_of(half * 512, 512), 512)
            parts = cdot(whole[m4, 0, rows, :], whole[m4, 1, rows, :],
                         whole[m1, 0, :, cols], whole[m1, 1, :, cols])
            for c in range(2):
                for a in range(2):
                    for b in range(4):
                        piece = parts[c][b * BLK:(b + 1) * BLK, a * BLK:(a + 1) * BLK]
                        products[1, 2 * pair + a, 4 * half + b, c] = piece.T.astype(bf16)

    def send_products(p):
        for i in range(4):
            for same in (False, True):
                for e in range(4):
                    z, lo, hi, core, slot, col = home(i, me.core, e, same)

                    def either(one, two):
                        return one + slot * (two - one)

                    device = me.at(either(me.z, z), either(lo, me.lo), either(hi, me.hi), core)
                    at = (p, slot, either(z, 2 * lo + hi), either(when, me.z))
                    start(products.at[p, i, col], mid.at[at], send1.at[p, i, int(same), e],
                          recv1.at[at], device)

    def pass_on(p):
        ref = (s_homes, r_homes)[p]
        for j in range(4):
            for k in range(4):
                landed(mid.at[p, 0, k, j], recv1.at[p, 0, k, j])
                start(mid.at[p, 0, k, j], ref.at[0, 4 * me.z + j],
                      send2.at[p, 0, k, j], recv2.at[p, 0, 4 * me.z + j],
                      me.at(k, me.lo, me.hi, me.core))
                landed(mid.at[p, 1, k, j], recv1.at[p, 1, k, j])
                start(mid.at[p, 1, k, j], ref.at[1, 4 * j + when],
                      send2.at[p, 1, k, j], recv2.at[p, 1, 4 * j + when],
                      me.at(me.z, k // 2, k % 2, me.core))

    def pass_fields():
        for hi in range(2):
            for z in range(4):
                landed_if(1, mid_z.at[hi, z], whole_y_recv.at[hi, z])
                start(mid_z.at[hi, z], homes.at[1 - me.hi, 4 * me.z + 2 + hi],
                      whole_pass_send.at[hi, z], home_recv.at[1 - me.hi, 4 * me.z + 2 + hi],
                      me.at(z, 1, me.hi, me.core), only=1)

    def serve_rest():
        for t in (2, 3):
            for slot in range(2):
                serve(0, slot, t)
        for t in (0, 1, 4, 5):
            serve(1, me.hi, t)
        for t in range(6):
            serve(1, 1 - me.hi, t)

    kept = []

    def fields_here():
        for slot in range(2):
            for t in range(6, 16):
                landed(homes.at[slot, t], home_recv.at[slot, t])
            kept.append(pltpu.make_async_copy(
                homes.at[slot, pl.ds(10, 6)], field_tail.at[slot, pl.ds(0, 6)], keep.at[0, slot]))
            kept[-1].start()

    def serve_products():
        for slot in range(2):
            for t in range(6):
                landed(s_homes.at[slot, t], recv2.at[0, slot, t])
                start(s_homes.at[slot, t], s_tail.at[slot, 6 + t], halo_send.at[slot, t],
                      halo_recv.at[slot, t], me.left)

    def products_here():
        for slot in range(2):
            for t in range(6, 16):
                landed(s_homes.at[slot, t], recv2.at[0, slot, t])
            kept.append(pltpu.make_async_copy(
                s_homes.at[slot, pl.ds(10, 6)], s_tail.at[slot, pl.ds(0, 6)], keep.at[1, slot]))
            kept[-1].start()

    def left_vectors():
        for role in range(2):
            for c in range(2):

                @pl.loop(0, 16)
                def _(part):
                    block = hits_left[role, part // 4, part % 4, :, c].reshape(BLK, BLK)
                    left_t[role, pl.ds(c * BLK, BLK), tile(part)] = block.T

        lanes = lax.broadcasted_iota(jnp.int32, (16, BLK), 1)

        @pl.loop(0, 16)
        def _(part):
            one, two = (hits_ids[part // 4, part % 4, lo].astype(f32) for lo in range(2))
            source[:, tile(part)] = jnp.where(lanes < 64, one, two)

    diagonal = jnp.logical_and(me.lo == 0, me.z == 0)

    def all_weights():
        @pl.loop(0, SPAN)
        def _(t):
            stamp = (me.x * SPAN + t).astype(f32)
            chosen = (source[:1, :] == stamp).astype(f32).astype(bf16)
            for slot in range(2):
                mate = jnp.where(diagonal, slot, 1 - slot)
                vectors = jnp.concatenate(
                    [hits_right[mate, :, :, :, c].reshape(2048, BLK) for c in range(2)], axis=1
                )
                pieces = jnp.dot(left_t[slot] * chosen, vectors, preferred_element_type=f32)
                weights[slot, t, 0] = (pieces[:BLK, :BLK] - pieces[BLK:, BLK:]).astype(bf16)
                weights[slot, t, 1] = (pieces[:BLK, BLK:] + pieces[BLK:, :BLK]).astype(bf16)

    def box(begin, end, later, shift):
        @pl.loop(begin, end)
        def _(t):
            totals = [[jnp.zeros((1, BLK), f32) for _ in range(4)] for _ in range(3)]
            for slot in range(2):
                mate = jnp.where(diagonal, slot, 1 - slot)
                p1 = [homes[slot, t, m1, c].astype(f32).T for c in range(2)]
                p4 = [homes[slot, t, m4, c].astype(f32).T for c in range(2)]
                for k in range(3):
                    u = t + seps[k] - shift
                    p2 = [later[mate, u, m2, c].astype(f32) for c in range(2)]
                    p3 = [later[mate, u, m3, c].astype(f32) for c in range(2)]
                    new = pair_sums(p1, p2) + pair_sums(p4, p3)
                    totals[k] = [a + b for a, b in zip(totals[k], new)]
            for k in range(3):
                box_sums[3 * t + k] = jnp.concatenate(totals[k], axis=0)

    def product_sums(begin, end, later, shift, first, sums):
        @pl.loop(begin, end)
        def _(t):
            totals = [[jnp.zeros((1, BLK), f32) for _ in range(2)] for _ in range(3)]
            for slot in range(2):
                one = [first[slot, t, c].astype(f32) for c in range(2)]
                for k in range(3):
                    u = t + seps[k] - shift
                    two = [later[slot, u, c].astype(f32) for c in range(2)]
                    totals[k] = [a + b for a, b in zip(totals[k], pair_sums(one, two))]
            for k in range(3):
                sums[3 * t + k] = jnp.concatenate(totals[k], axis=0)

    def to_tiles(begin, end, sums):
        reduced = jnp.sum(sums[...], axis=-1)
        for q in range(8):
            tiles[q, 0:6, begin:end] = reduced[6 * q:6 * q + 6]

    product_s()
    send_products(0)
    product_r()
    pass_fields()
    relay()
    serve_rest()
    pass_on(0)
    send_products(1)
    fields_here()
    box(0, 10, homes, 0)
    ring_refs = [hits_left.at[:, after], hits_right.at[:, after], hits_ids.at[after]]
    relay_refs = [hits_left.at[:, opposite], hits_right.at[:, opposite], hits_ids.at[opposite]]
    for n in range(3):
        landed(ring_refs[n], ring_recv.at[1, n])
        landed(relay_refs[n], relay_recv.at[n])
    left_vectors()
    serve_products()
    pass_on(1)
    all_weights()
    for copy in kept:
        copy.wait()
    for slot in range(2):
        for t in range(6):
            landed(field_tail.at[slot, 6 + t], field_recv.at[slot, t])
    box(10, 16, field_tail, 10)
    to_tiles(0, 4, box_sums)
    products_here()
    product_sums(0, 10, s_homes, 0, weights, noise_sums)
    for copy in kept[2:]:
        copy.wait()
    for slot in range(2):
        for t in range(6):
            landed(s_tail.at[slot, 6 + t], halo_recv.at[slot, t])
    product_sums(10, 16, s_tail, 10, weights, noise_sums)
    to_tiles(6, 8, noise_sums)
    for copy in assembly + forwards + ring + relays:
        copy.wait_send()
    all_sent()
    for slot in range(2):
        for t in range(16):
            landed(r_homes.at[slot, t], recv2.at[1, slot, t])
    product_sums(0, 10, s_homes, 0, r_homes, cross_sums)
    product_sums(10, 16, s_tail, 10, r_homes, cross_sums)
    to_tiles(4, 6, cross_sums)

    mine = 4 * (me.tm % 8) + me.mode
    for n in range(32):
        start(tiles.at[n // 4], gather.at[mine], sum_send.at[n], sum_recv.at[mine],
              (8 * me.x + n // 4, n % 4))
    for n in range(32):
        landed(gather.at[n], sum_recv.at[n])
    out[...] = jnp.sum(gather[...], axis=0)

    all_sent()


def params(ident):
    return pltpu.CompilerParams(
        vmem_limit_bytes=VMEM_LIMIT, collective_id=ident, has_side_effects=True
    )


def on_device(field_codes, scales, mom_index, separations, source_slice, noise_left, noise_right):
    bf16, f32 = jnp.bfloat16, jnp.float32
    dma = pltpu.SemaphoreType.DMA
    blocks = noise_left.reshape(64, 2, 8, BLK).transpose(2, 1, 0, 3)
    own_blocks = noise_right.reshape(64, 2, 2, BLK).transpose(2, 1, 0, 3)
    ids = jnp.broadcast_to(jnp.tile(source_slice.astype(bf16), 2), (16, BLK))

    any_spec = pl.BlockSpec(memory_space=ANY)
    smem = pl.BlockSpec(memory_space=pltpu.SMEM)
    vmem = pl.BlockSpec(memory_space=pltpu.VMEM)
    dims = lambda *shape: pltpu.VMEM(shape, bf16)
    total = pl.pallas_call(
        contract,
        out_shape=jax.ShapeDtypeStruct((8, BLK), f32),
        in_specs=[smem, smem, any_spec, vmem, any_spec, any_spec, any_spec],
        out_specs=vmem,
        scratch_shapes=[
            dims(2, 2, 2, 256, 1024),
            dims(2, 2, 1024, 1024),
            dims(2, 16, 2, 2, BLK, BLK),
            dims(2, 12, 2, 2, BLK, BLK),
            dims(2, 4, 2, 2, BLK, BLK),
            dims(2, 4, 2, 2, BLK, BLK),
            dims(2, 4, 8, 2, BLK, BLK),
            dims(2, 2, 4, 4, 2, BLK, BLK),
            dims(2, 16, 2, BLK, BLK),
            dims(2, 12, 2, BLK, BLK),
            dims(2, 16, 2, BLK, BLK),
            dims(2, 4, 2, 64, BLK),
            dims(4, 4, 2, 64, BLK),
            dims(4, 16, BLK),
            dims(2, 4, 4, 2, 2, 64, BLK),
            dims(2, 4, 4, 2, 2, 64, BLK),
            dims(4, 4, 2, 16, BLK),
            dims(2, 2 * BLK, 2048),
            pltpu.VMEM((16, 2048), f32),
            dims(2, SPAN, 2, BLK, BLK),
            pltpu.VMEM((3 * SPAN, 4, BLK), f32),
            pltpu.VMEM((3 * SPAN, 2, BLK), f32),
            pltpu.VMEM((3 * SPAN, 2, BLK), f32),
            pltpu.VMEM((8, 8, BLK), f32),
            pltpu.VMEM((32, 8, BLK), f32),
            dma((2,)), dma((2,)), dma((2,)), dma((2,)), dma((2,)),
            dma((4, 2)), dma((4, 2)), dma((2, 4)), dma((2, 4)), dma((2, 4, 2)),
            dma((4,)), dma((4,)), dma((4,)), dma((4,)), dma((4, 2)),
            dma((2, 2, 4)), dma((4, 4)), dma((4, 4)), dma((2, 4, 2)),
            dma((2, 3)), dma((2, 3)), dma((3,)), dma((3,)),
            dma((2, 2, 6)), dma((2, 4)), dma((2, 4)), dma((2, 4)),
            dma((4, 2)), dma((2, 4)), dma((2, 4)), dma((2, 4)), dma((2, 16)),
            dma((2, 4, 2, 4)), dma((2, 2, 4, 4)), dma((2, 2, 4, 4)), dma((2, 2, 16)),
            dma((2, 6)), dma((2, 6)), dma((2, 6)), dma((2, 6)), dma((2, 2)),
            dma((32,)), dma((32,)),
        ],
        compiler_params=params(0),
        name="contract",
    )(mom_index, separations, field_codes, scales, blocks, own_blocks, ids)
    mine = total[:6, :8].reshape(2, 3, 8)
    box = jnp.stack(
        [
            mine[..., 0] * mine[..., 2] - mine[..., 1] * mine[..., 3],
            mine[..., 0] * mine[..., 3] + mine[..., 1] * mine[..., 2],
        ],
        axis=-1,
    )
    return box, mine[..., 4:6], mine[..., 6:8]


def solution(mesh):
    in_specs = (
        P(None, "tm", None, "mode", None),
        P(None, "tm", "mode"),
        P(),
        P(),
        P("tm"),
        P("tm", None, None),
        P("tm", None, "mode"),
    )
    out_specs = (P("tm", None, None), P("tm", None, None), P("tm", None, None))
    return jax.shard_map(
        on_device, mesh=mesh, in_specs=in_specs, out_specs=out_specs, check_vma=False
    )
```

```python
import jax
import jax.numpy as jnp
from jax import lax
from jax.experimental import pallas as pl
from jax.experimental.pallas import tpu as pltpu
from jax.sharding import PartitionSpec as P

MESH = pl.DeviceIdType.MESH
ANY = pl.ANY
BLK = 128
SPAN = 16
VMEM_LIMIT = 56 * 1024 * 1024


def home(i, half, e, same):
    if same:
        if e == 0:
            unit, slot = i % 2, i // 2
        elif e == 1:
            unit, slot = 4 + i, 0
        elif e == 2:
            unit, slot = 2 + i % 2, i // 2
        else:
            unit, slot = 4 + (i + 3) % 4, 1
        return unit // 2, 0, half, unit % 2, slot, 4 * half + (i + e) % 4
    upper, lower = i + half * (e - i), e + half * (i - e)
    return upper, 1, (i + e) % 2, lower // 2, half, 4 * (1 - half) + e


def blocks_of(z, lo, hi, core):
    if z < 2:
        near = (core, core + 2)
    elif z == 2:
        near = (core, core + 1)
    else:
        near = (2 + core, (3 + core) % 4)
    far = (z, 4 + 2 * core + (hi + z) % 2)
    return tuple(4 * hi * (1 - lo) + n + lo * (f - n) for n, f in zip(near, far))


class Place:
    def __init__(self):
        self.tm = lax.axis_index("tm")
        self.mode = lax.axis_index("mode")
        self.x, self.z, self.lo = self.tm // 8, (self.tm // 2) % 4, self.tm % 2
        self.hi, self.core = self.mode // 2, self.mode % 2
        self.right = ((self.tm + 8) % 32, self.mode)
        self.left = ((self.tm + 24) % 32, self.mode)

    def at(self, z, lo, hi, core):
        return (8 * self.x + 2 * z + lo, 2 * hi + core)

    def is_here(self, device):
        return jnp.logical_and(device[0] == self.tm, device[1] == self.mode)


def greet(place):
    barrier = pltpu.get_barrier_semaphore()

    def signal(device):
        pl.semaphore_signal(barrier, inc=1, device_id=device, device_id_type=MESH)

    for n in range(32):
        device = (8 * place.x + n // 4, n % 4)

        @pl.when(jnp.logical_not(place.is_here(device)))
        def _():
            signal(device)

    signal(place.right)
    signal(place.left)
    pl.semaphore_wait(barrier, 33)


def remote(src, dst, send, recv, device):
    return pltpu.make_async_remote_copy(
        src_ref=src, dst_ref=dst, send_sem=send, recv_sem=recv,
        device_id=device, device_id_type=MESH,
    )


def send_or_keep(place, src, dst, send, recv, device):
    here = place.is_here(device)

    @pl.when(jnp.logical_not(here))
    def _():
        remote(src, dst, send, recv, device).start()

    @pl.when(here)
    def _():
        pltpu.make_async_copy(src, dst, recv).start()


def sent(place, src, dst, send, recv, device):
    @pl.when(jnp.logical_not(place.is_here(device)))
    def _():
        remote(src, dst, send, recv, device).wait_send()


def landed(ref, sem):
    pltpu.make_async_copy(ref, ref, sem).wait()


def pair_sums(one, two):
    real = one[0] * two[0] - one[1] * two[1]
    imag = one[0] * two[1] + one[1] * two[0]
    return [jnp.sum(value, axis=0, keepdims=True) for value in (real, imag)]


def contract(
    mom, seps, codes, scales, all_left, all_right, all_ids, out,
    left, right, ids,
    fields, whole, homes, field_tail, mid_y, mid_z, products, mid, s_homes, s_tail, r_homes,
    mid_left, mid_right, mid_ids, hits_left, hits_right, hits_ids,
    left_t, source, partial, weights, box_sums, cross_sums, noise_sums, tiles, gather,
    code_sem, asm_send, asm_recv, fwd_send, fwd_recv,
    left_send, left_z_send, left_z_recv, left_y_send, left_recv,
    id_send, id_z_send, id_z_recv, id_y_send, id_recv,
    right_z_send, right_z_recv, right_y_send, right_recv,
    ring_send, ring_recv, relay_send, relay_recv,
    near_send, cross_z_send, cross_z_recv, cross_y_send,
    whole_z_send, whole_y_send, whole_y_recv, whole_pass_send, home_recv,
    send1, recv1, send2, recv2,
    field_send, field_recv, halo_send, halo_recv, keep, sum_send, sum_recv,
):
    f32, bf16 = jnp.float32, jnp.bfloat16
    me = Place()
    loads = [pltpu.make_async_copy(codes.at[:, s], fields.at[:, s], code_sem.at[s])
             for s in range(2)]
    for copy in loads:
        copy.start()
    tiles[...] = jnp.zeros_like(tiles)
    greet(me)
    flip = me.tm + 1 - 2 * me.lo
    when = 2 * (1 - me.lo) + me.hi
    sends = []

    def start(*copy, only=None):
        sends.append((copy, only))
        if only is None:
            send_or_keep(me, *copy)
        else:

            @pl.when(me.lo == only)
            def _():
                send_or_keep(me, *copy)

    def all_sent():
        for copy, only in sends:
            if only is None:
                sent(me, *copy)
            else:

                @pl.when(me.lo == only)
                def _():
                    sent(me, *copy)

        sends.clear()

    def landed_if(only, ref, sem):
        @pl.when(me.lo == only)
        def _():
            landed(ref, sem)

    def tile(n):
        return pl.ds(n * BLK if isinstance(n, int) else pl.multiple_of(n * BLK, BLK), BLK)

    def rows_of(block):
        return whole.at[:, :, pl.ds(pl.multiple_of(block * 256, 256), 256), :]

    assembly = []
    for s in range(2):
        loads[s].wait()
        for m in range(2):
            column = jnp.broadcast_to(scales[m, s:s + 1, :], (BLK, 256)).T

            @pl.loop(0, 8)
            def _(n):
                for c in range(2):
                    value = fields[m, s, c, :, tile(n)].astype(f32) * column
                    fields[m, s, c, :, tile(n)] = value.astype(bf16)

        assembly.append(remote(fields.at[:, s], rows_of(me.mode), asm_send.at[s],
                               asm_recv.at[me.hi], (flip, 2 * s + me.core)))
        assembly[-1].start()

    for ref, into, count in ((all_left, left, 8), (all_right, right, 2)):
        for c in range(2):
            value = ref[:, c, :]
            for n in range(count):
                into[n, c] = value[:, n * BLK:(n + 1) * BLK]
    row = all_ids[...].astype(f32)
    ids[...] = jnp.broadcast_to(jnp.concatenate([row, row], axis=1), (16, BLK)).astype(bf16)

    for z in range(4):
        for slot in range(2):
            hi = me.hi + slot * (1 - 2 * me.hi)
            far = blocks_of(z, 1 - me.lo, hi, me.core)[slot]
            start(left.at[far], mid_left.at[slot, me.z], left_z_send.at[z, slot],
                  left_z_recv.at[slot, me.z], me.at(z, me.lo, me.hi, me.core))
        start(ids, mid_ids.at[me.z], id_z_send.at[z], id_z_recv.at[me.z],
              me.at(z, me.lo, me.hi, me.core))
    for a in range(2):
        for same in (False, True):
            for e in range(4):
                z, lo, hi, core, slot, col = home(2 * me.core + a, me.hi, e, same)
                group = slot if same else 2 + hi
                start(right.at[a], mid_right.at[group, me.z], right_z_send.at[a, int(same), e],
                      right_z_recv.at[group, me.z], me.at(z, me.lo, me.hi, core))

    for a in range(2):
        row = 2 * me.core + a
        for e in range(4):
            z, _, hi, core, slot, col = home(row, me.hi, e, True)
            far = home(row, me.hi, e, False)

            def pick(one, two):
                return one + me.lo * (two - one)

            s, group = pick(1 - far[2], 1 - me.hi), pick(far[2], slot)
            start(fields.at[:, s, :, tile(a), tile(pick(far[5], col))], mid_y.at[group, me.z],
                  cross_z_send.at[a, e], cross_z_recv.at[group, me.z],
                  me.at(pick(far[0], z), me.lo, me.hi, pick(far[3], core)))
        for s in range(2):
            for e in range(4):
                z, _, hi, core, slot, col = home(row, me.hi, e, True)
                start(fields.at[:, s, :, tile(a), tile(col)], homes.at[slot, 4 * me.z + s],
                      near_send.at[s, a, e], home_recv.at[slot, 4 * me.z + s],
                      me.at(z, 0, me.hi, core), only=0)
            for b in range(2):
                other = 2 * b + (me.hi + a) % 2
                z, _, hi, core, slot, col = home(row, me.hi, other, False)
                start(fields.at[:, s, :, tile(a), tile(col)], homes.at[slot, 4 * me.z + 2 + s],
                      near_send.at[s, a, 4 + b], home_recv.at[slot, 4 * me.z + 2 + s],
                      me.at(z, 1, me.hi, core), only=1)

    for z in range(4):
        for slot in range(2):
            hi = me.hi + slot * (1 - 2 * me.hi)
            landed(mid_left.at[slot, z], left_z_recv.at[slot, z])
            start(mid_left.at[slot, z], hits_left.at[slot, me.x, z, me.lo],
                  left_y_send.at[slot, z], left_recv.at[slot, z, me.lo],
                  me.at(me.z, 1 - me.lo, hi, me.core))
        landed(mid_ids.at[z], id_z_recv.at[z])
        start(mid_ids.at[z], hits_ids.at[me.x, z, me.lo], id_y_send.at[z],
              id_recv.at[z, me.lo], me.at(me.z, 1 - me.lo, me.hi, me.core))
        for group in range(4):
            if group < 2:
                slot, device = group, me.at(me.z, 0, me.hi, me.core)
            else:
                slot, device = me.hi, me.at(me.z, 1, group - 2, me.core)
            landed(mid_right.at[group, z], right_z_recv.at[group, z])
            start(mid_right.at[group, z], hits_right.at[slot, me.x, z, me.lo],
                  right_y_send.at[group, z], right_recv.at[slot, z, me.lo], device)
        for slot in range(2):
            near = blocks_of(z, me.lo, me.hi, me.core)[slot]
            start(left.at[near], hits_left.at[slot, me.x, me.z, me.lo], left_send.at[z, slot],
                  left_recv.at[slot, me.z, me.lo], me.at(z, me.lo, me.hi, me.core))
        start(ids, hits_ids.at[me.x, me.z, me.lo], id_send.at[z], id_recv.at[me.z, me.lo],
              me.at(z, me.lo, me.hi, me.core))

    ring = []

    def start_ring():
        for z in range(4):
            for lo in range(2):
                for slot in range(2):
                    landed(hits_left.at[slot, me.x, z, lo], left_recv.at[slot, z, lo])
                    landed(hits_right.at[slot, me.x, z, lo], right_recv.at[slot, z, lo])
                landed(hits_ids.at[me.x, z, lo], id_recv.at[z, lo])
        own = [hits_left.at[:, me.x], hits_right.at[:, me.x], hits_ids.at[me.x]]
        for n, ref in enumerate(own):
            ring.append(remote(ref, ref, ring_send.at[0, n], ring_recv.at[0, n], me.right))
        for n, ref in enumerate(own):
            ring.append(remote(ref, ref, ring_send.at[1, n], ring_recv.at[1, n], me.left))
        for copy in ring:
            copy.start()

    before, after, opposite = (me.x + 3) % 4, (me.x + 1) % 4, (me.x + 2) % 4
    relays = []

    def relay():
        held = [hits_left.at[:, before], hits_right.at[:, before], hits_ids.at[before]]
        for n, ref in enumerate(held):
            landed(ref, ring_recv.at[0, n])
            relays.append(remote(ref, ref, relay_send.at[n], relay_recv.at[n], me.right))
            relays[-1].start()

    def serve(only, slot, t):
        landed_if(only, homes.at[slot, t], home_recv.at[slot, t])
        start(homes.at[slot, t], field_tail.at[slot, 6 + t], field_send.at[slot, t],
              field_recv.at[slot, t], me.left, only=only)

    for t in (0, 1, 4, 5):
        for slot in range(2):
            serve(0, slot, t)
    for t in (2, 3):
        serve(1, me.hi, t)

    forwards = []
    for h in range(2):
        block = rows_of(2 * h + me.core)
        landed(block, asm_recv.at[h])
        forwards.append(remote(block, block, fwd_send.at[h], fwd_recv.at[h],
                               (me.tm, me.mode + 1 - 2 * me.core)))
        forwards[-1].start()

    for z in range(4):
        for group in range(2):
            landed(mid_y.at[group, z], cross_z_recv.at[group, z])
            lo, hi = 1 - me.lo, group + me.lo * (me.hi - group)
            slot = me.hi + me.lo * (group - me.hi)
            t = 4 * z + 2 * me.lo + (1 - group) + me.lo * (group - me.hi)
            start(mid_y.at[group, z], homes.at[slot, t], cross_y_send.at[group, z],
                  home_recv.at[slot, t], me.at(me.z, lo, hi, me.core))

    start_ring()

    for h in range(2):
        landed(rows_of(2 * h + 1 - me.core), fwd_recv.at[h])
    for hi in range(2):
        for z in range(4):
            pair = blocks_of(z, 1, hi, me.core)
            row, col = pair[1 - hi], pair[hi]
            start(whole.at[:, :, tile(row), tile(col)], mid_z.at[me.hi, z],
                  whole_y_send.at[hi, z], whole_y_recv.at[me.hi, z],
                  me.at(me.z, 1, hi, me.core), only=0)
    for z in range(4):
        pair = blocks_of(z, me.lo, me.hi, me.core)
        for slot in range(2):
            row, col = pair[slot], pair[1 - slot]
            if z == 0:
                col = col + (1 - me.lo) * (row - col)
            start(whole.at[:, :, tile(row), tile(col)], homes.at[slot, 4 * me.z + when],
                  whole_z_send.at[z, slot], home_recv.at[slot, 4 * me.z + when],
                  me.at(z, me.lo, me.hi, me.core))

    base = pl.multiple_of(me.core * 512, 512)
    m1, m2, m3, m4 = (mom[i] for i in range(4))

    def cdot(ar, ai, br, bi):
        def dot(a, b):
            return jnp.dot(a, b, preferred_element_type=f32)

        return dot(ar, br) - dot(ai, bi), dot(ar, bi) + dot(ai, br)

    def product_s():
        @pl.loop(0, 4)
        def _(pair):
            cols = pl.ds(pl.multiple_of(pair * 256, 256), 256)
            rows = pl.ds(base, 512)
            parts = cdot(whole[m2, 0, rows, :], whole[m2, 1, rows, :],
                         whole[m3, 0, :, cols], whole[m3, 1, :, cols])
            for c in range(2):
                for a in range(4):
                    for b in range(2):
                        piece = parts[c][a * BLK:(a + 1) * BLK, b * BLK:(b + 1) * BLK]
                        products[0, a, 2 * pair + b, c] = piece.astype(bf16)

    def product_r():
        @pl.loop(0, 4)
        def _(step):
            pair, half = step // 2, step % 2
            cols = pl.ds(pl.multiple_of(base + pair * 256, 256), 256)
            rows = pl.ds(pl.multiple_of(half * 512, 512), 512)
            parts = cdot(whole[m4, 0, rows, :], whole[m4, 1, rows, :],
                         whole[m1, 0, :, cols], whole[m1, 1, :, cols])
            for c in range(2):
                for a in range(2):
                    for b in range(4):
                        piece = parts[c][b * BLK:(b + 1) * BLK, a * BLK:(a + 1) * BLK]
                        products[1, 2 * pair + a, 4 * half + b, c] = piece.T.astype(bf16)

    def send_products(p):
        for i in range(4):
            for same in (False, True):
                for e in range(4):
                    z, lo, hi, core, slot, col = home(i, me.core, e, same)

                    def either(one, two):
                        return one + slot * (two - one)

                    device = me.at(either(me.z, z), either(lo, me.lo), either(hi, me.hi), core)
                    at = (p, slot, either(z, 2 * lo + hi), either(when, me.z))
                    start(products.at[p, i, col], mid.at[at], send1.at[p, i, int(same), e],
                          recv1.at[at], device)

    def pass_on(p):
        ref = (s_homes, r_homes)[p]
        for j in range(4):
            for k in range(4):
                landed(mid.at[p, 0, k, j], recv1.at[p, 0, k, j])
                start(mid.at[p, 0, k, j], ref.at[0, 4 * me.z + j],
                      send2.at[p, 0, k, j], recv2.at[p, 0, 4 * me.z + j],
                      me.at(k, me.lo, me.hi, me.core))
                landed(mid.at[p, 1, k, j], recv1.at[p, 1, k, j])
                start(mid.at[p, 1, k, j], ref.at[1, 4 * j + when],
                      send2.at[p, 1, k, j], recv2.at[p, 1, 4 * j + when],
                      me.at(me.z, k // 2, k % 2, me.core))

    def pass_fields():
        for hi in range(2):
            for z in range(4):
                landed_if(1, mid_z.at[hi, z], whole_y_recv.at[hi, z])
                start(mid_z.at[hi, z], homes.at[1 - me.hi, 4 * me.z + 2 + hi],
                      whole_pass_send.at[hi, z], home_recv.at[1 - me.hi, 4 * me.z + 2 + hi],
                      me.at(z, 1, me.hi, me.core), only=1)

    def serve_rest():
        for t in (2, 3):
            for slot in range(2):
                serve(0, slot, t)
        for t in (0, 1, 4, 5):
            serve(1, me.hi, t)
        for t in range(6):
            serve(1, 1 - me.hi, t)

    kept = []

    def fields_here():
        for slot in range(2):
            for t in range(6, 16):
                landed(homes.at[slot, t], home_recv.at[slot, t])
            kept.append(pltpu.make_async_copy(
                homes.at[slot, pl.ds(10, 6)], field_tail.at[slot, pl.ds(0, 6)], keep.at[0, slot]))
            kept[-1].start()

    def serve_products():
        for slot in range(2):
            for t in range(6):
                landed(s_homes.at[slot, t], recv2.at[0, slot, t])
                start(s_homes.at[slot, t], s_tail.at[slot, 6 + t], halo_send.at[slot, t],
                      halo_recv.at[slot, t], me.left)

    def products_here():
        for slot in range(2):
            for t in range(6, 16):
                landed(s_homes.at[slot, t], recv2.at[0, slot, t])
            kept.append(pltpu.make_async_copy(
                s_homes.at[slot, pl.ds(10, 6)], s_tail.at[slot, pl.ds(0, 6)], keep.at[1, slot]))
            kept[-1].start()

    lanes = lax.broadcasted_iota(jnp.int32, (16, BLK), 1)
    order = (me.x, before, after, opposite)

    def left_vectors(planes):
        for n in planes:
            for role in range(2):
                for c in range(2):

                    @pl.loop(0, 4)
                    def _(part):
                        block = hits_left[role, order[n], part, :, c].reshape(BLK, BLK)
                        left_t[role, pl.ds(c * BLK, BLK), tile(4 * n + part)] = block.T

            @pl.loop(0, 4)
            def _(part):
                one, two = (hits_ids[order[n], part, lo].astype(f32) for lo in range(2))
                source[:, tile(4 * n + part)] = jnp.where(lanes < 64, one, two)

    diagonal = jnp.logical_and(me.lo == 0, me.z == 0)

    def add_weights(planes, first):
        span = slice(512 * planes[0], 512 * (planes[-1] + 1))

        @pl.loop(0, SPAN)
        def _(t):
            stamp = (me.x * SPAN + t).astype(f32)
            chosen = (source[:1, span] == stamp).astype(f32).astype(bf16)
            for slot in range(2):
                mate = jnp.where(diagonal, slot, 1 - slot)
                vectors = jnp.concatenate([
                    jnp.concatenate([hits_right[mate, order[n], :, :, c].reshape(512, BLK)
                                     for n in planes], axis=0)
                    for c in range(2)
                ], axis=1)
                pieces = jnp.dot(left_t[slot, :, span] * chosen, vectors,
                                 preferred_element_type=f32)
                values = (pieces[:BLK, :BLK] - pieces[BLK:, BLK:],
                          pieces[:BLK, BLK:] + pieces[BLK:, :BLK])
                for c in range(2):
                    if first:
                        partial[slot, t, c] = values[c]
                    else:
                        weights[slot, t, c] = (partial[slot, t, c] + values[c]).astype(bf16)

    def box(begin, end, later, shift):
        @pl.loop(begin, end)
        def _(t):
            totals = [[jnp.zeros((1, BLK), f32) for _ in range(4)] for _ in range(3)]
            for slot in range(2):
                mate = jnp.where(diagonal, slot, 1 - slot)
                p1 = [homes[slot, t, m1, c].astype(f32).T for c in range(2)]
                p4 = [homes[slot, t, m4, c].astype(f32).T for c in range(2)]
                for k in range(3):
                    u = t + seps[k] - shift
                    p2 = [later[mate, u, m2, c].astype(f32) for c in range(2)]
                    p3 = [later[mate, u, m3, c].astype(f32) for c in range(2)]
                    new = pair_sums(p1, p2) + pair_sums(p4, p3)
                    totals[k] = [a + b for a, b in zip(totals[k], new)]
            for k in range(3):
                box_sums[3 * t + k] = jnp.concatenate(totals[k], axis=0)

    def product_sums(begin, end, later, shift, first, sums):
        @pl.loop(begin, end)
        def _(t):
            totals = [[jnp.zeros((1, BLK), f32) for _ in range(2)] for _ in range(3)]
            for slot in range(2):
                one = [first[slot, t, c].astype(f32) for c in range(2)]
                for k in range(3):
                    u = t + seps[k] - shift
                    two = [later[slot, u, c].astype(f32) for c in range(2)]
                    totals[k] = [a + b for a, b in zip(totals[k], pair_sums(one, two))]
            for k in range(3):
                sums[3 * t + k] = jnp.concatenate(totals[k], axis=0)

    def to_tiles(begin, end, sums):
        reduced = jnp.sum(sums[...], axis=-1)
        for q in range(8):
            tiles[q, 0:6, begin:end] = reduced[6 * q:6 * q + 6]

    product_s()
    send_products(0)
    product_r()
    pass_fields()
    relay()
    serve_rest()
    pass_on(0)
    send_products(1)
    fields_here()
    box(0, 10, homes, 0)
    ring_refs = [hits_left.at[:, after], hits_right.at[:, after], hits_ids.at[after]]
    relay_refs = [hits_left.at[:, opposite], hits_right.at[:, opposite], hits_ids.at[opposite]]
    for n in range(3):
        landed(ring_refs[n], ring_recv.at[1, n])
    left_vectors((0, 1, 2))
    add_weights((0, 1, 2), True)
    serve_products()
    pass_on(1)
    for n in range(3):
        landed(relay_refs[n], relay_recv.at[n])
    left_vectors((3,))
    add_weights((3,), False)
    for copy in kept:
        copy.wait()
    for slot in range(2):
        for t in range(6):
            landed(field_tail.at[slot, 6 + t], field_recv.at[slot, t])
    box(10, 16, field_tail, 10)
    to_tiles(0, 4, box_sums)
    products_here()
    product_sums(0, 10, s_homes, 0, weights, noise_sums)
    for copy in kept[2:]:
        copy.wait()
    for slot in range(2):
        for t in range(6):
            landed(s_tail.at[slot, 6 + t], halo_recv.at[slot, t])
    product_sums(10, 16, s_tail, 10, weights, noise_sums)
    to_tiles(6, 8, noise_sums)
    for copy in assembly + forwards + ring + relays:
        copy.wait_send()
    all_sent()
    for slot in range(2):
        for t in range(16):
            landed(r_homes.at[slot, t], recv2.at[1, slot, t])
    product_sums(0, 10, s_homes, 0, r_homes, cross_sums)
    product_sums(10, 16, s_tail, 10, r_homes, cross_sums)
    to_tiles(4, 6, cross_sums)

    mine = 4 * (me.tm % 8) + me.mode
    for n in range(32):
        start(tiles.at[n // 4], gather.at[mine], sum_send.at[n], sum_recv.at[mine],
              (8 * me.x + n // 4, n % 4))
    for n in range(32):
        landed(gather.at[n], sum_recv.at[n])
    out[...] = jnp.sum(gather[...], axis=0)

    all_sent()


def params(ident):
    return pltpu.CompilerParams(
        vmem_limit_bytes=VMEM_LIMIT, collective_id=ident, has_side_effects=True
    )


def on_device(field_codes, scales, mom_index, separations, source_slice, noise_left, noise_right):
    bf16, f32 = jnp.bfloat16, jnp.float32
    dma = pltpu.SemaphoreType.DMA
    any_spec = pl.BlockSpec(memory_space=ANY)
    smem = pl.BlockSpec(memory_space=pltpu.SMEM)
    vmem = pl.BlockSpec(memory_space=pltpu.VMEM)
    dims = lambda *shape: pltpu.VMEM(shape, bf16)
    total = pl.pallas_call(
        contract,
        out_shape=jax.ShapeDtypeStruct((8, BLK), f32),
        in_specs=[smem, smem, any_spec, vmem, vmem, vmem, vmem],
        out_specs=vmem,
        scratch_shapes=[
            dims(8, 2, 64, BLK),
            dims(2, 2, 64, BLK),
            dims(16, BLK),
            dims(2, 2, 2, 256, 1024),
            dims(2, 2, 1024, 1024),
            dims(2, 16, 2, 2, BLK, BLK),
            dims(2, 12, 2, 2, BLK, BLK),
            dims(2, 4, 2, 2, BLK, BLK),
            dims(2, 4, 2, 2, BLK, BLK),
            dims(2, 4, 8, 2, BLK, BLK),
            dims(2, 2, 4, 4, 2, BLK, BLK),
            dims(2, 16, 2, BLK, BLK),
            dims(2, 12, 2, BLK, BLK),
            dims(2, 16, 2, BLK, BLK),
            dims(2, 4, 2, 64, BLK),
            dims(4, 4, 2, 64, BLK),
            dims(4, 16, BLK),
            dims(2, 4, 4, 2, 2, 64, BLK),
            dims(2, 4, 4, 2, 2, 64, BLK),
            dims(4, 4, 2, 16, BLK),
            dims(2, 2 * BLK, 2048),
            pltpu.VMEM((16, 2048), f32),
            pltpu.VMEM((2, SPAN, 2, BLK, BLK), f32),
            dims(2, SPAN, 2, BLK, BLK),
            pltpu.VMEM((3 * SPAN, 4, BLK), f32),
            pltpu.VMEM((3 * SPAN, 2, BLK), f32),
            pltpu.VMEM((3 * SPAN, 2, BLK), f32),
            pltpu.VMEM((8, 8, BLK), f32),
            pltpu.VMEM((32, 8, BLK), f32),
            dma((2,)), dma((2,)), dma((2,)), dma((2,)), dma((2,)),
            dma((4, 2)), dma((4, 2)), dma((2, 4)), dma((2, 4)), dma((2, 4, 2)),
            dma((4,)), dma((4,)), dma((4,)), dma((4,)), dma((4, 2)),
            dma((2, 2, 4)), dma((4, 4)), dma((4, 4)), dma((2, 4, 2)),
            dma((2, 3)), dma((2, 3)), dma((3,)), dma((3,)),
            dma((2, 2, 6)), dma((2, 4)), dma((2, 4)), dma((2, 4)),
            dma((4, 2)), dma((2, 4)), dma((2, 4)), dma((2, 4)), dma((2, 16)),
            dma((2, 4, 2, 4)), dma((2, 2, 4, 4)), dma((2, 2, 4, 4)), dma((2, 2, 16)),
            dma((2, 6)), dma((2, 6)), dma((2, 6)), dma((2, 6)), dma((2, 2)),
            dma((32,)), dma((32,)),
        ],
        compiler_params=params(0),
        name="contract",
    )(
        mom_index, separations, field_codes, scales, noise_left, noise_right,
        source_slice.reshape(1, 64),
    )
    mine = total[:6, :8].reshape(2, 3, 8)
    box = jnp.stack(
        [
            mine[..., 0] * mine[..., 2] - mine[..., 1] * mine[..., 3],
            mine[..., 0] * mine[..., 3] + mine[..., 1] * mine[..., 2],
        ],
        axis=-1,
    )
    return box, mine[..., 4:6], mine[..., 6:8]


def solution(mesh):
    in_specs = (
        P(None, "tm", None, "mode", None),
        P(None, "tm", "mode"),
        P(),
        P(),
        P("tm"),
        P("tm", None, None),
        P("tm", None, "mode"),
    )
    out_specs = (P("tm", None, None), P("tm", None, None), P("tm", None, None))
    return jax.shard_map(
        on_device, mesh=mesh, in_specs=in_specs, out_specs=out_specs, check_vma=False
    )
```

```python
import jax
import jax.numpy as jnp
from jax import lax
from jax.experimental import pallas as pl
from jax.experimental.pallas import tpu as pltpu
from jax.sharding import PartitionSpec as P

MESH = pl.DeviceIdType.MESH
ANY = pl.ANY
BLK = 128
SPAN = 16
VMEM_LIMIT = 56 * 1024 * 1024


def home(i, half, e, same):
    if same:
        if e == 0:
            unit, slot = i % 2, i // 2
        elif e == 1:
            unit, slot = 4 + i, 0
        elif e == 2:
            unit, slot = 2 + i % 2, i // 2
        else:
            unit, slot = 4 + (i + 3) % 4, 1
        return unit // 2, 0, half, unit % 2, slot, 4 * half + (i + e) % 4
    upper, lower = i + half * (e - i), e + half * (i - e)
    return upper, 1, (i + e) % 2, lower // 2, half, 4 * (1 - half) + e


def blocks_of(z, lo, hi, core):
    if z < 2:
        near = (core, core + 2)
    elif z == 2:
        near = (core, core + 1)
    else:
        near = (2 + core, (3 + core) % 4)
    far = (z, 4 + 2 * core + (hi + z) % 2)
    return tuple(4 * hi * (1 - lo) + n + lo * (f - n) for n, f in zip(near, far))


class Place:
    def __init__(self):
        self.tm = lax.axis_index("tm")
        self.mode = lax.axis_index("mode")
        self.x, self.z, self.lo = self.tm // 8, (self.tm // 2) % 4, self.tm % 2
        self.hi, self.core = self.mode // 2, self.mode % 2
        self.right = ((self.tm + 8) % 32, self.mode)
        self.left = ((self.tm + 24) % 32, self.mode)

    def at(self, z, lo, hi, core):
        return (8 * self.x + 2 * z + lo, 2 * hi + core)

    def is_here(self, device):
        return jnp.logical_and(device[0] == self.tm, device[1] == self.mode)


def greet(place):
    barrier = pltpu.get_barrier_semaphore()

    def signal(device):
        pl.semaphore_signal(barrier, inc=1, device_id=device, device_id_type=MESH)

    for n in range(32):
        device = (8 * place.x + n // 4, n % 4)

        @pl.when(jnp.logical_not(place.is_here(device)))
        def _():
            signal(device)

    signal(place.right)
    signal(place.left)
    pl.semaphore_wait(barrier, 33)


def remote(src, dst, send, recv, device):
    return pltpu.make_async_remote_copy(
        src_ref=src, dst_ref=dst, send_sem=send, recv_sem=recv,
        device_id=device, device_id_type=MESH,
    )


def send_or_keep(place, src, dst, send, recv, device):
    here = place.is_here(device)

    @pl.when(jnp.logical_not(here))
    def _():
        remote(src, dst, send, recv, device).start()

    @pl.when(here)
    def _():
        pltpu.make_async_copy(src, dst, recv).start()


def sent(place, src, dst, send, recv, device):
    @pl.when(jnp.logical_not(place.is_here(device)))
    def _():
        remote(src, dst, send, recv, device).wait_send()


def landed(ref, sem):
    pltpu.make_async_copy(ref, ref, sem).wait()


def pair_sums(one, two):
    real = one[0] * two[0] - one[1] * two[1]
    imag = one[0] * two[1] + one[1] * two[0]
    return [jnp.sum(value, axis=0, keepdims=True) for value in (real, imag)]


def contract(
    mom, seps, codes, scales, all_left, all_right, all_ids, out,
    left, right, ids,
    fields, whole, homes, field_tail, mid_y, mid_z, products, mid, s_homes, s_tail, r_homes,
    mid_left, mid_right, mid_ids, hits_left, hits_right, hits_ids,
    left_t, source, partial, weights, box_sums, cross_sums, noise_sums, tiles, gather,
    code_sem, asm_send, asm_recv, fwd_send, fwd_recv,
    left_send, left_z_send, left_z_recv, left_y_send, left_recv,
    id_send, id_z_send, id_z_recv, id_y_send, id_recv,
    right_z_send, right_z_recv, right_y_send, right_recv,
    ring_send, ring_recv, relay_send, relay_recv,
    near_send, cross_z_send, cross_z_recv, cross_y_send,
    whole_z_send, whole_y_send, whole_y_recv, whole_pass_send, home_recv,
    send1, recv1, send2, recv2,
    field_send, field_recv, halo_send, halo_recv, keep, sum_send, sum_recv,
):
    f32, bf16 = jnp.float32, jnp.bfloat16
    me = Place()
    loads = [pltpu.make_async_copy(codes.at[:, s], fields.at[:, s], code_sem.at[s])
             for s in range(2)]
    for copy in loads:
        copy.start()
    tiles[...] = jnp.zeros_like(tiles)
    greet(me)
    flip = me.tm + 1 - 2 * me.lo
    when = 2 * (1 - me.lo) + me.hi
    sends = []

    def start(*copy, only=None):
        sends.append((copy, only))
        if only is None:
            send_or_keep(me, *copy)
        else:

            @pl.when(me.lo == only)
            def _():
                send_or_keep(me, *copy)

    def all_sent():
        for copy, only in sends:
            if only is None:
                sent(me, *copy)
            else:

                @pl.when(me.lo == only)
                def _():
                    sent(me, *copy)

        sends.clear()

    def landed_if(only, ref, sem):
        @pl.when(me.lo == only)
        def _():
            landed(ref, sem)

    def tile(n):
        return pl.ds(n * BLK if isinstance(n, int) else pl.multiple_of(n * BLK, BLK), BLK)

    def rows_of(block, m):
        return whole.at[m, :, pl.ds(pl.multiple_of(block * 256, 256), 256), :]

    assembly = []
    for s in range(2):
        loads[s].wait()
        for m in range(2):
            column = jnp.broadcast_to(scales[m, s:s + 1, :], (BLK, 256)).T

            @pl.loop(0, 8)
            def _(n):
                for c in range(2):
                    value = fields[m, s, c, :, tile(n)].astype(f32) * column
                    fields[m, s, c, :, tile(n)] = value.astype(bf16)

            assembly.append(remote(fields.at[m, s], rows_of(me.mode, m), asm_send.at[s, m],
                                   asm_recv.at[me.hi, m], (flip, 2 * s + me.core)))
            assembly[-1].start()

    for ref, into, count in ((all_left, left, 8), (all_right, right, 2)):
        for c in range(2):
            value = ref[:, c, :]
            for n in range(count):
                into[n, c] = value[:, n * BLK:(n + 1) * BLK]
    row = all_ids[...].astype(f32)
    ids[...] = jnp.broadcast_to(jnp.concatenate([row, row], axis=1), (16, BLK)).astype(bf16)

    for z in range(4):
        for slot in range(2):
            hi = me.hi + slot * (1 - 2 * me.hi)
            far = blocks_of(z, 1 - me.lo, hi, me.core)[slot]
            start(left.at[far], mid_left.at[slot, me.z], left_z_send.at[z, slot],
                  left_z_recv.at[slot, me.z], me.at(z, me.lo, me.hi, me.core))
        start(ids, mid_ids.at[me.z], id_z_send.at[z], id_z_recv.at[me.z],
              me.at(z, me.lo, me.hi, me.core))
    for a in range(2):
        for same in (False, True):
            for e in range(4):
                z, lo, hi, core, slot, col = home(2 * me.core + a, me.hi, e, same)
                group = slot if same else 2 + hi
                start(right.at[a], mid_right.at[group, me.z], right_z_send.at[a, int(same), e],
                      right_z_recv.at[group, me.z], me.at(z, me.lo, me.hi, core))

    for a in range(2):
        row = 2 * me.core + a
        for e in range(4):
            z, _, hi, core, slot, col = home(row, me.hi, e, True)
            far = home(row, me.hi, e, False)

            def pick(one, two):
                return one + me.lo * (two - one)

            s, group = pick(1 - far[2], 1 - me.hi), pick(far[2], slot)
            start(fields.at[:, s, :, tile(a), tile(pick(far[5], col))], mid_y.at[group, me.z],
                  cross_z_send.at[a, e], cross_z_recv.at[group, me.z],
                  me.at(pick(far[0], z), me.lo, me.hi, pick(far[3], core)))
        for s in range(2):
            for e in range(4):
                z, _, hi, core, slot, col = home(row, me.hi, e, True)
                start(fields.at[:, s, :, tile(a), tile(col)], homes.at[slot, 4 * me.z + s],
                      near_send.at[s, a, e], home_recv.at[slot, 4 * me.z + s],
                      me.at(z, 0, me.hi, core), only=0)
            for b in range(2):
                other = 2 * b + (me.hi + a) % 2
                z, _, hi, core, slot, col = home(row, me.hi, other, False)
                start(fields.at[:, s, :, tile(a), tile(col)], homes.at[slot, 4 * me.z + 2 + s],
                      near_send.at[s, a, 4 + b], home_recv.at[slot, 4 * me.z + 2 + s],
                      me.at(z, 1, me.hi, core), only=1)

    for z in range(4):
        for slot in range(2):
            hi = me.hi + slot * (1 - 2 * me.hi)
            landed(mid_left.at[slot, z], left_z_recv.at[slot, z])
            start(mid_left.at[slot, z], hits_left.at[slot, me.x, z, me.lo],
                  left_y_send.at[slot, z], left_recv.at[slot, z, me.lo],
                  me.at(me.z, 1 - me.lo, hi, me.core))
        landed(mid_ids.at[z], id_z_recv.at[z])
        start(mid_ids.at[z], hits_ids.at[me.x, z, me.lo], id_y_send.at[z],
              id_recv.at[z, me.lo], me.at(me.z, 1 - me.lo, me.hi, me.core))
        for group in range(4):
            if group < 2:
                slot, device = group, me.at(me.z, 0, me.hi, me.core)
            else:
                slot, device = me.hi, me.at(me.z, 1, group - 2, me.core)
            landed(mid_right.at[group, z], right_z_recv.at[group, z])
            start(mid_right.at[group, z], hits_right.at[slot, me.x, z, me.lo],
                  right_y_send.at[group, z], right_recv.at[slot, z, me.lo], device)
        for slot in range(2):
            near = blocks_of(z, me.lo, me.hi, me.core)[slot]
            start(left.at[near], hits_left.at[slot, me.x, me.z, me.lo], left_send.at[z, slot],
                  left_recv.at[slot, me.z, me.lo], me.at(z, me.lo, me.hi, me.core))
        start(ids, hits_ids.at[me.x, me.z, me.lo], id_send.at[z], id_recv.at[me.z, me.lo],
              me.at(z, me.lo, me.hi, me.core))

    ring = []

    def start_ring():
        for z in range(4):
            for lo in range(2):
                for slot in range(2):
                    landed(hits_left.at[slot, me.x, z, lo], left_recv.at[slot, z, lo])
                    landed(hits_right.at[slot, me.x, z, lo], right_recv.at[slot, z, lo])
                landed(hits_ids.at[me.x, z, lo], id_recv.at[z, lo])
        own = [hits_left.at[:, me.x], hits_right.at[:, me.x], hits_ids.at[me.x]]
        for n, ref in enumerate(own):
            ring.append(remote(ref, ref, ring_send.at[0, n], ring_recv.at[0, n], me.right))
        for n, ref in enumerate(own):
            ring.append(remote(ref, ref, ring_send.at[1, n], ring_recv.at[1, n], me.left))
        for copy in ring:
            copy.start()

    before, after, opposite = (me.x + 3) % 4, (me.x + 1) % 4, (me.x + 2) % 4
    relays = []

    def relay():
        held = [hits_left.at[:, before], hits_right.at[:, before], hits_ids.at[before]]
        for n, ref in enumerate(held):
            landed(ref, ring_recv.at[0, n])
            relays.append(remote(ref, ref, relay_send.at[n], relay_recv.at[n], me.right))
            relays[-1].start()

    def serve(only, slot, t):
        landed_if(only, homes.at[slot, t], home_recv.at[slot, t])
        start(homes.at[slot, t], field_tail.at[slot, 6 + t], field_send.at[slot, t],
              field_recv.at[slot, t], me.left, only=only)

    for t in (0, 1, 4, 5):
        for slot in range(2):
            serve(0, slot, t)
    for t in (2, 3):
        serve(1, me.hi, t)

    forwards = []
    for m in range(2):
        for h in range(2):
            block = rows_of(2 * h + me.core, m)
            landed(block, asm_recv.at[h, m])
            forwards.append(remote(block, block, fwd_send.at[h, m], fwd_recv.at[h, m],
                                   (me.tm, me.mode + 1 - 2 * me.core)))
            forwards[-1].start()

    for z in range(4):
        for group in range(2):
            landed(mid_y.at[group, z], cross_z_recv.at[group, z])
            lo, hi = 1 - me.lo, group + me.lo * (me.hi - group)
            slot = me.hi + me.lo * (group - me.hi)
            t = 4 * z + 2 * me.lo + (1 - group) + me.lo * (group - me.hi)
            start(mid_y.at[group, z], homes.at[slot, t], cross_y_send.at[group, z],
                  home_recv.at[slot, t], me.at(me.z, lo, hi, me.core))

    start_ring()

    for m in range(2):
        for h in range(2):
            landed(rows_of(2 * h + 1 - me.core, m), fwd_recv.at[h, m])
    for hi in range(2):
        for z in range(4):
            pair = blocks_of(z, 1, hi, me.core)
            row, col = pair[1 - hi], pair[hi]
            start(whole.at[:, :, tile(row), tile(col)], mid_z.at[me.hi, z],
                  whole_y_send.at[hi, z], whole_y_recv.at[me.hi, z],
                  me.at(me.z, 1, hi, me.core), only=0)
    for z in range(4):
        pair = blocks_of(z, me.lo, me.hi, me.core)
        for slot in range(2):
            row, col = pair[slot], pair[1 - slot]
            if z == 0:
                col = col + (1 - me.lo) * (row - col)
            start(whole.at[:, :, tile(row), tile(col)], homes.at[slot, 4 * me.z + when],
                  whole_z_send.at[z, slot], home_recv.at[slot, 4 * me.z + when],
                  me.at(z, me.lo, me.hi, me.core))

    base = pl.multiple_of(me.core * 512, 512)
    m1, m2, m3, m4 = (mom[i] for i in range(4))

    def cdot(ar, ai, br, bi):
        def dot(a, b):
            return jnp.dot(a, b, preferred_element_type=f32)

        return dot(ar, br) - dot(ai, bi), dot(ar, bi) + dot(ai, br)

    def product_s():
        @pl.loop(0, 4)
        def _(pair):
            cols = pl.ds(pl.multiple_of(pair * 256, 256), 256)
            rows = pl.ds(base, 512)
            parts = cdot(whole[m2, 0, rows, :], whole[m2, 1, rows, :],
                         whole[m3, 0, :, cols], whole[m3, 1, :, cols])
            for c in range(2):
                for a in range(4):
                    for b in range(2):
                        piece = parts[c][a * BLK:(a + 1) * BLK, b * BLK:(b + 1) * BLK]
                        products[0, a, 2 * pair + b, c] = piece.astype(bf16)

    def product_r():
        @pl.loop(0, 4)
        def _(step):
            pair, half = step // 2, step % 2
            cols = pl.ds(pl.multiple_of(base + pair * 256, 256), 256)
            rows = pl.ds(pl.multiple_of(half * 512, 512), 512)
            parts = cdot(whole[m4, 0, rows, :], whole[m4, 1, rows, :],
                         whole[m1, 0, :, cols], whole[m1, 1, :, cols])
            for c in range(2):
                for a in range(2):
                    for b in range(4):
                        piece = parts[c][b * BLK:(b + 1) * BLK, a * BLK:(a + 1) * BLK]
                        products[1, 2 * pair + a, 4 * half + b, c] = piece.T.astype(bf16)

    def send_products(p):
        for i in range(4):
            for same in (False, True):
                for e in range(4):
                    z, lo, hi, core, slot, col = home(i, me.core, e, same)

                    def either(one, two):
                        return one + slot * (two - one)

                    device = me.at(either(me.z, z), either(lo, me.lo), either(hi, me.hi), core)
                    at = (p, slot, either(z, 2 * lo + hi), either(when, me.z))
                    start(products.at[p, i, col], mid.at[at], send1.at[p, i, int(same), e],
                          recv1.at[at], device)

    def pass_on(p):
        ref = (s_homes, r_homes)[p]
        for j in range(4):
            for k in range(4):
                landed(mid.at[p, 0, k, j], recv1.at[p, 0, k, j])
                start(mid.at[p, 0, k, j], ref.at[0, 4 * me.z + j],
                      send2.at[p, 0, k, j], recv2.at[p, 0, 4 * me.z + j],
                      me.at(k, me.lo, me.hi, me.core))
                landed(mid.at[p, 1, k, j], recv1.at[p, 1, k, j])
                start(mid.at[p, 1, k, j], ref.at[1, 4 * j + when],
                      send2.at[p, 1, k, j], recv2.at[p, 1, 4 * j + when],
                      me.at(me.z, k // 2, k % 2, me.core))

    def pass_fields():
        for hi in range(2):
            for z in range(4):
                landed_if(1, mid_z.at[hi, z], whole_y_recv.at[hi, z])
                start(mid_z.at[hi, z], homes.at[1 - me.hi, 4 * me.z + 2 + hi],
                      whole_pass_send.at[hi, z], home_recv.at[1 - me.hi, 4 * me.z + 2 + hi],
                      me.at(z, 1, me.hi, me.core), only=1)

    def serve_rest():
        for t in (2, 3):
            for slot in range(2):
                serve(0, slot, t)
        for t in (0, 1, 4, 5):
            serve(1, me.hi, t)
        for t in range(6):
            serve(1, 1 - me.hi, t)

    kept = []

    def fields_here():
        for slot in range(2):
            for t in range(6, 16):
                landed(homes.at[slot, t], home_recv.at[slot, t])
            kept.append(pltpu.make_async_copy(
                homes.at[slot, pl.ds(10, 6)], field_tail.at[slot, pl.ds(0, 6)], keep.at[0, slot]))
            kept[-1].start()

    def serve_products():
        for slot in range(2):
            for t in range(6):
                landed(s_homes.at[slot, t], recv2.at[0, slot, t])
                start(s_homes.at[slot, t], s_tail.at[slot, 6 + t], halo_send.at[slot, t],
                      halo_recv.at[slot, t], me.left)

    def products_here():
        for slot in range(2):
            for t in range(6, 16):
                landed(s_homes.at[slot, t], recv2.at[0, slot, t])
            kept.append(pltpu.make_async_copy(
                s_homes.at[slot, pl.ds(10, 6)], s_tail.at[slot, pl.ds(0, 6)], keep.at[1, slot]))
            kept[-1].start()

    lanes = lax.broadcasted_iota(jnp.int32, (16, BLK), 1)
    order = (me.x, before, after, opposite)

    def left_vectors(planes):
        for n in planes:
            for role in range(2):
                for c in range(2):

                    @pl.loop(0, 4)
                    def _(part):
                        block = hits_left[role, order[n], part, :, c].reshape(BLK, BLK)
                        left_t[role, pl.ds(c * BLK, BLK), tile(4 * n + part)] = block.T

            @pl.loop(0, 4)
            def _(part):
                one, two = (hits_ids[order[n], part, lo].astype(f32) for lo in range(2))
                source[:, tile(4 * n + part)] = jnp.where(lanes < 64, one, two)

    diagonal = jnp.logical_and(me.lo == 0, me.z == 0)

    def add_weights(planes, first):
        span = slice(512 * planes[0], 512 * (planes[-1] + 1))

        @pl.loop(0, SPAN)
        def _(t):
            stamp = (me.x * SPAN + t).astype(f32)
            chosen = (source[:1, span] == stamp).astype(f32).astype(bf16)
            for slot in range(2):
                mate = jnp.where(diagonal, slot, 1 - slot)
                vectors = jnp.concatenate([
                    jnp.concatenate([hits_right[mate, order[n], :, :, c].reshape(512, BLK)
                                     for n in planes], axis=0)
                    for c in range(2)
                ], axis=1)
                pieces = jnp.dot(left_t[slot, :, span] * chosen, vectors,
                                 preferred_element_type=f32)
                values = (pieces[:BLK, :BLK] - pieces[BLK:, BLK:],
                          pieces[:BLK, BLK:] + pieces[BLK:, :BLK])
                for c in range(2):
                    if first:
                        partial[slot, t, c] = values[c]
                    else:
                        weights[slot, t, c] = (partial[slot, t, c] + values[c]).astype(bf16)

    def box(begin, end, later, shift):
        @pl.loop(begin, end)
        def _(t):
            totals = [[jnp.zeros((1, BLK), f32) for _ in range(4)] for _ in range(3)]
            for slot in range(2):
                mate = jnp.where(diagonal, slot, 1 - slot)
                p1 = [homes[slot, t, m1, c].astype(f32).T for c in range(2)]
                p4 = [homes[slot, t, m4, c].astype(f32).T for c in range(2)]
                for k in range(3):
                    u = t + seps[k] - shift
                    p2 = [later[mate, u, m2, c].astype(f32) for c in range(2)]
                    p3 = [later[mate, u, m3, c].astype(f32) for c in range(2)]
                    new = pair_sums(p1, p2) + pair_sums(p4, p3)
                    totals[k] = [a + b for a, b in zip(totals[k], new)]
            for k in range(3):
                box_sums[3 * t + k] = jnp.concatenate(totals[k], axis=0)

    def product_sums(begin, end, later, shift, first, sums):
        @pl.loop(begin, end)
        def _(t):
            totals = [[jnp.zeros((1, BLK), f32) for _ in range(2)] for _ in range(3)]
            for slot in range(2):
                one = [first[slot, t, c].astype(f32) for c in range(2)]
                for k in range(3):
                    u = t + seps[k] - shift
                    two = [later[slot, u, c].astype(f32) for c in range(2)]
                    totals[k] = [a + b for a, b in zip(totals[k], pair_sums(one, two))]
            for k in range(3):
                sums[3 * t + k] = jnp.concatenate(totals[k], axis=0)

    def to_tiles(begin, end, sums):
        reduced = jnp.sum(sums[...], axis=-1)
        for q in range(8):
            tiles[q, 0:6, begin:end] = reduced[6 * q:6 * q + 6]

    product_s()
    send_products(0)
    product_r()
    pass_fields()
    relay()
    serve_rest()
    pass_on(0)
    send_products(1)
    fields_here()
    box(0, 10, homes, 0)
    ring_refs = [hits_left.at[:, after], hits_right.at[:, after], hits_ids.at[after]]
    relay_refs = [hits_left.at[:, opposite], hits_right.at[:, opposite], hits_ids.at[opposite]]
    for n in range(3):
        landed(ring_refs[n], ring_recv.at[1, n])
    left_vectors((0, 1, 2))
    add_weights((0, 1, 2), True)
    serve_products()
    pass_on(1)
    for n in range(3):
        landed(relay_refs[n], relay_recv.at[n])
    left_vectors((3,))
    add_weights((3,), False)
    for copy in kept:
        copy.wait()
    for slot in range(2):
        for t in range(6):
            landed(field_tail.at[slot, 6 + t], field_recv.at[slot, t])
    box(10, 16, field_tail, 10)
    to_tiles(0, 4, box_sums)
    products_here()
    product_sums(0, 10, s_homes, 0, weights, noise_sums)
    for copy in kept[2:]:
        copy.wait()
    for slot in range(2):
        for t in range(6):
            landed(s_tail.at[slot, 6 + t], halo_recv.at[slot, t])
    product_sums(10, 16, s_tail, 10, weights, noise_sums)
    to_tiles(6, 8, noise_sums)
    for copy in assembly + forwards + ring + relays:
        copy.wait_send()
    all_sent()
    for slot in range(2):
        for t in range(16):
            landed(r_homes.at[slot, t], recv2.at[1, slot, t])
    product_sums(0, 10, s_homes, 0, r_homes, cross_sums)
    product_sums(10, 16, s_tail, 10, r_homes, cross_sums)
    to_tiles(4, 6, cross_sums)

    mine = 4 * (me.tm % 8) + me.mode
    for n in range(32):
        start(tiles.at[n // 4], gather.at[mine], sum_send.at[n], sum_recv.at[mine],
              (8 * me.x + n // 4, n % 4))
    for n in range(32):
        landed(gather.at[n], sum_recv.at[n])
    out[...] = jnp.sum(gather[...], axis=0)

    all_sent()


def params(ident):
    return pltpu.CompilerParams(
        vmem_limit_bytes=VMEM_LIMIT, collective_id=ident, has_side_effects=True
    )


def on_device(field_codes, scales, mom_index, separations, source_slice, noise_left, noise_right):
    bf16, f32 = jnp.bfloat16, jnp.float32
    dma = pltpu.SemaphoreType.DMA
    any_spec = pl.BlockSpec(memory_space=ANY)
    smem = pl.BlockSpec(memory_space=pltpu.SMEM)
    vmem = pl.BlockSpec(memory_space=pltpu.VMEM)
    dims = lambda *shape: pltpu.VMEM(shape, bf16)
    total = pl.pallas_call(
        contract,
        out_shape=jax.ShapeDtypeStruct((8, BLK), f32),
        in_specs=[smem, smem, any_spec, vmem, vmem, vmem, vmem],
        out_specs=vmem,
        scratch_shapes=[
            dims(8, 2, 64, BLK),
            dims(2, 2, 64, BLK),
            dims(16, BLK),
            dims(2, 2, 2, 256, 1024),
            dims(2, 2, 1024, 1024),
            dims(2, 16, 2, 2, BLK, BLK),
            dims(2, 12, 2, 2, BLK, BLK),
            dims(2, 4, 2, 2, BLK, BLK),
            dims(2, 4, 2, 2, BLK, BLK),
            dims(2, 4, 8, 2, BLK, BLK),
            dims(2, 2, 4, 4, 2, BLK, BLK),
            dims(2, 16, 2, BLK, BLK),
            dims(2, 12, 2, BLK, BLK),
            dims(2, 16, 2, BLK, BLK),
            dims(2, 4, 2, 64, BLK),
            dims(4, 4, 2, 64, BLK),
            dims(4, 16, BLK),
            dims(2, 4, 4, 2, 2, 64, BLK),
            dims(2, 4, 4, 2, 2, 64, BLK),
            dims(4, 4, 2, 16, BLK),
            dims(2, 2 * BLK, 2048),
            pltpu.VMEM((16, 2048), f32),
            pltpu.VMEM((2, SPAN, 2, BLK, BLK), f32),
            dims(2, SPAN, 2, BLK, BLK),
            pltpu.VMEM((3 * SPAN, 4, BLK), f32),
            pltpu.VMEM((3 * SPAN, 2, BLK), f32),
            pltpu.VMEM((3 * SPAN, 2, BLK), f32),
            pltpu.VMEM((8, 8, BLK), f32),
            pltpu.VMEM((32, 8, BLK), f32),
            dma((2,)), dma((2, 2)), dma((2, 2)), dma((2, 2)), dma((2, 2)),
            dma((4, 2)), dma((4, 2)), dma((2, 4)), dma((2, 4)), dma((2, 4, 2)),
            dma((4,)), dma((4,)), dma((4,)), dma((4,)), dma((4, 2)),
            dma((2, 2, 4)), dma((4, 4)), dma((4, 4)), dma((2, 4, 2)),
            dma((2, 3)), dma((2, 3)), dma((3,)), dma((3,)),
            dma((2, 2, 6)), dma((2, 4)), dma((2, 4)), dma((2, 4)),
            dma((4, 2)), dma((2, 4)), dma((2, 4)), dma((2, 4)), dma((2, 16)),
            dma((2, 4, 2, 4)), dma((2, 2, 4, 4)), dma((2, 2, 4, 4)), dma((2, 2, 16)),
            dma((2, 6)), dma((2, 6)), dma((2, 6)), dma((2, 6)), dma((2, 2)),
            dma((32,)), dma((32,)),
        ],
        compiler_params=params(0),
        name="contract",
    )(
        mom_index, separations, field_codes, scales, noise_left, noise_right,
        source_slice.reshape(1, 64),
    )
    mine = total[:6, :8].reshape(2, 3, 8)
    box = jnp.stack(
        [
            mine[..., 0] * mine[..., 2] - mine[..., 1] * mine[..., 3],
            mine[..., 0] * mine[..., 3] + mine[..., 1] * mine[..., 2],
        ],
        axis=-1,
    )
    return box, mine[..., 4:6], mine[..., 6:8]


def solution(mesh):
    in_specs = (
        P(None, "tm", None, "mode", None),
        P(None, "tm", "mode"),
        P(),
        P(),
        P("tm"),
        P("tm", None, None),
        P("tm", None, "mode"),
    )
    out_specs = (P("tm", None, None), P("tm", None, None), P("tm", None, None))
    return jax.shard_map(
        on_device, mesh=mesh, in_specs=in_specs, out_specs=out_specs, check_vma=False
    )
```
